512 devices in a mesh: dom: 32 (over x_lo, z, core), slab: 16 (over y, x_hi).
Axes of the slice: x: 4 (x_hi: 2, x_lo: 2; x = x_hi * 2 + x_lo), y: 8, z: 8, core: 2. Of those that a mesh axis runs over, the one named last changes fastest.
Arguments:
- volume: bfloat16 [16384, 2, 256], P('slab'), may hold values from -6 to 6
- images: bfloat16 [2048, 256, 2, 256], P(('dom', 'slab')), may hold values from -6 to 6
- defocus: float32 [2048], P(('dom', 'slab')), may hold values from 8 to 40
- soft_weights: float32 [2048, 4, 32, 32], P(('dom', 'slab')), may hold values from 0 to 1
- slice_lines: int32 [4, 256], replicated, may hold values from 0 to 16383, as said below
- shift_y: int32 [32], replicated, may hold values from -16 to 15
- shift_x: int32 [32], replicated, may hold values from -16 to 15
Outputs:
- scores: float32 [2048, 4, 32, 32], P(('dom', 'slab'))
- line_update: bfloat16 [16384, 2, 256], P('slab')
The draws below stay inside these ranges and needn't reach their ends.
Inputs may be any that keep to these rules, and one draw needn't show every extreme that they name: `slice_lines`: in every orientation, each slab s (the lines s * 1024 to (s+1) * 1024 - 1) holds exactly 16 of the 256 slice rows; a line may be named more than once.
All inputs are finite; a program needn't handle non-finite values.
Results may differ from the reference program's by a relative error of at most 0.0055.
Values may be sent and summed in bfloat16 or wider, within the bound.
A program may use at most 128 MiB of HBM per device.

```python
import math
import jax
import jax.numpy as jnp
from jax import lax

KS = 256
P_DEV = 4
LINES_DEV = 1024
ORIENT = 4
NTY = 32
NTX = 32
OWNED = 16
NLINES = 16384
PARTICLES = 2048


def draw_slice_lines(key, part):
    key = jax.random.fold_in(key, 7)
    orient_keys = jax.random.split(jax.random.fold_in(key, 1), ORIENT)
    slot_order = jax.vmap(lambda single_key: jax.random.permutation(single_key, KS))(orient_keys).astype(jnp.int32)
    row_owner = slot_order // OWNED
    local_line = jax.random.randint(jax.random.fold_in(key, 2), (ORIENT, KS), 0, LINES_DEV).astype(jnp.int32)
    first_orient = jnp.arange(ORIENT, dtype=jnp.int32)[:, None] == 0
    local_line = jnp.where(first_orient & (slot_order == KS - 1), LINES_DEV - 1, local_line)
    local_line = jnp.where(first_orient & (slot_order == 0), 0, local_line)
    return (row_owner * LINES_DEV + local_line).astype(jnp.int32)


def place_ends(array, stream_key, least, high):
    index_at = [jax.random.randint(jax.random.fold_in(stream_key, axis), (), 0, length) for axis, length in enumerate(array.shape)]
    main_axis = array.shape.index(max(array.shape))
    neighbour = index_at[:main_axis] + [(index_at[main_axis] + 1) % array.shape[main_axis]] + index_at[main_axis + 1:]
    return array.at[tuple(index_at)].set(least).at[tuple(neighbour)].set(high)


def level_of(rng, extent, cuts, low, top_value):
    loudness = 1.0
    for position, blocks in cuts:
        heights = jax.random.uniform(jax.random.fold_in(jax.random.fold_in(rng, 6), position), (blocks,), jnp.float32, low / len(cuts), top_value / len(cuts))
        loudness = loudness * jnp.repeat(jnp.exp(heights), extent[position] // blocks).reshape((-1,) + (1,) * (len(extent) - 1 - position))
    return loudness


def scatter_about(rng, extent, deviation, limit, shards=(), kind=jnp.bfloat16):
    level = level_of(rng, extent, shards, -0.22, 0.18) if shards else 1.0
    entries = jax.random.normal(rng, extent, jnp.float32) * deviation * level
    return jnp.minimum(jnp.maximum(entries, -limit), limit).astype(kind)


def setup_inputs(seed: int = 0) -> dict:
    key_of = jax.random.split(jax.random.key(seed), 8)
    volume = scatter_about(key_of[0], (NLINES, 2, KS), 1.0, 6.0, ((0, 16),))
    images = scatter_about(key_of[1], (PARTICLES, KS, 2, KS), 1.0, 6.0, ((0, 512),))
    defocus = jnp.clip(8.0 + 32.0 * jax.random.uniform(key_of[2], (PARTICLES,), jnp.float32) ** level_of(key_of[2], (PARTICLES,), ((0, 512),), -0.2, 0.2), 8.0, 40.0)
    soft_weights = jnp.clip(1.0 * jax.random.uniform(key_of[3], (PARTICLES, ORIENT, NTY, NTX), jnp.float32) ** level_of(key_of[3], (PARTICLES, ORIENT, NTY, NTX), ((0, 512),), -0.2, 0.2), 0.0, 1.0)
    slice_lines = draw_slice_lines(jax.random.fold_in(key_of[7], 71), 0)
    shift_y = place_ends(jax.random.randint(key_of[5], (NTY,), 0 - KS // 16, KS // 16), jax.random.fold_in(key_of[5], 1), 0 - KS // 16, (KS // 16) - 1).astype(jnp.int32)
    shift_x = place_ends(jax.random.randint(key_of[6], (NTX,), 0 - KS // 16, KS // 16), jax.random.fold_in(key_of[6], 1), 0 - KS // 16, (KS // 16) - 1).astype(jnp.int32)
    return dict(volume=volume, images=images, defocus=defocus, soft_weights=soft_weights, slice_lines=slice_lines, shift_y=shift_y, shift_x=shift_x)


def phase_angles(frequency, shifts, image_side):
    turns = jnp.mod(frequency[..., None] * shifts, image_side)
    return turns.astype(jnp.float32) * (2.0 * math.pi / image_side)

def contrast(defocus, frequency, image_side):
    half_side = image_side // 2
    radius = (frequency[:, None] ** 2 + frequency[None, :] ** 2).astype(jnp.float32) / float(half_side * half_side)
    aberration = defocus[:, None, None] * radius
    return -(0.995 * jnp.sin(aberration) + 0.1 * jnp.cos(aberration))

def rounded(value):
    return lax.optimization_barrier(value.astype(jnp.bfloat16)).astype(jnp.float32)

def reference(volume, images, defocus, soft_weights, slice_lines, shift_y, shift_x):
    highest = lax.Precision.HIGHEST
    frequency = jnp.arange(KS, dtype=jnp.int32) - KS // 2
    angle_x = phase_angles(frequency, shift_x, KS)
    angle_y = phase_angles(frequency, shift_y, KS)
    fx_re = jnp.cos(angle_x).astype(jnp.bfloat16)
    fx_im = (-jnp.sin(angle_x)).astype(jnp.bfloat16)
    fx_table = jnp.concatenate([jnp.concatenate([fx_re, fx_im], 1), jnp.concatenate([-fx_im, fx_re], 1)], 0).astype(jnp.float32)
    fy_re = jnp.cos(angle_y)
    fy_im = -jnp.sin(angle_y)
    back_re = jnp.cos(angle_x)
    back_im = jnp.sin(angle_x)
    ey_re = rounded(jnp.cos(angle_y))
    ey_im = rounded(jnp.sin(angle_y))
    slices = volume[slice_lines].astype(jnp.float32)
    slice_re = slices[:, :, 0][None]
    slice_im = slices[:, :, 1][None]

    def visit_block(running, block_index):
        first_row = block_index * P_DEV
        xblock = lax.dynamic_slice_in_dim(images, first_row, P_DEV, 0).astype(jnp.float32)
        dblock = lax.dynamic_slice_in_dim(defocus, first_row, P_DEV, 0)
        wblock = lax.dynamic_slice_in_dim(soft_weights, first_row, P_DEV, 0)
        contrast_map = contrast(dblock, frequency, KS)
        x_re = xblock[:, :, 0]
        x_im = xblock[:, :, 1]
        c_map = contrast_map[:, None]
        q_re = c_map * (slice_re * x_re[:, None] + slice_im * x_im[:, None])
        q_im = c_map * (slice_re * x_im[:, None] - slice_im * x_re[:, None])
        q_cat = rounded(jnp.concatenate([q_re, q_im], -1))
        correlated = jnp.einsum('bokj,jx->bokx', q_cat, fx_table, precision=highest)
        z_re = correlated[..., :NTX]
        z_im = correlated[..., NTX:]
        block_scores = (jnp.einsum('kt,bokx->botx', fy_re, z_re, precision=highest) - jnp.einsum('kt,bokx->botx', fy_im, z_im, precision=highest)) / KS
        h_re = rounded(jnp.einsum('botx,kx->botk', wblock, back_re, precision=highest))
        h_im = rounded(jnp.einsum('botx,kx->botk', wblock, back_im, precision=highest))
        g_re = jnp.einsum('kt,botj->bokj', ey_re, h_re, precision=highest) - jnp.einsum('kt,botj->bokj', ey_im, h_im, precision=highest)
        g_im = jnp.einsum('kt,botj->bokj', ey_im, h_re, precision=highest) + jnp.einsum('kt,botj->bokj', ey_re, h_im, precision=highest)
        c_re = (contrast_map * x_re)[:, None]
        c_im = (contrast_map * x_im)[:, None]
        t_re = lax.optimization_barrier(jnp.sum(c_re * g_re - c_im * g_im, axis=0))
        t_im = lax.optimization_barrier(jnp.sum(c_re * g_im + c_im * g_re, axis=0))
        return ((running[0] + t_re, running[1] + t_im), block_scores)
    zero_term = jnp.zeros((ORIENT, KS, KS), jnp.float32)
    summed, scores = lax.scan(visit_block, (zero_term, zero_term), jnp.arange(PARTICLES // P_DEV, dtype=jnp.int32))
    scores = scores.reshape(PARTICLES, ORIENT, NTY, NTX)
    inserted = jnp.stack([summed[0], summed[1]], 2).reshape(ORIENT * KS, 2, KS)
    line_update = jnp.zeros((NLINES, 2, KS), jnp.float32).at[slice_lines.reshape(-1)].add(inserted)
    scale_factor = 1.0 / math.sqrt(NTY * NTX * PARTICLES)
    return (scores, (line_update * scale_factor).astype(jnp.bfloat16))
```

```python
import math

import jax
import jax.numpy as jnp
from jax import lax
from jax.experimental import pallas as pl
from jax.experimental.pallas import tpu as pltpu
from jax.sharding import PartitionSpec as P

KS = 256
HALF = KS // 2
P_DEV = 4
LINES = 1024
ORIENT = 4
NT = 32
OWNED = 16
PARTICLES = 2048
SLABS = 16
ZS = 8
XLO = 2
SCALE = 1.0 / math.sqrt(NT * NT * PARTICLES)
F32 = jnp.float32
BF16 = jnp.bfloat16
MESH = pl.DeviceIdType.MESH


def dot(a, b):
    return jnp.dot(a, b, preferred_element_type=F32)


def dot_t(a, b):
    return lax.dot_general(a, b, (((0,), (0,)), ((), ())), preferred_element_type=F32)


def poly_sin_cos(r):
    s = r * r
    sin = r * (1.0 + s * (-1 / 6 + s * (1 / 120 + s * (-1 / 5040 + s * (1 / 362880)))))
    cos = 1.0 + s * (-0.5 + s * (1 / 24 + s * (-1 / 720 + s * (1 / 40320))))
    return sin, cos


def rotate(quadrant, sin, cos):
    q = quadrant & 3
    odd = (q & 1) == 1
    s = jnp.where(odd, cos, sin)
    c = jnp.where(odd, sin, cos)
    s = jnp.where(q >= 2, -s, s)
    c = jnp.where((q == 1) | (q == 2), -c, c)
    return s, c


def turns_sin_cos(turns):
    t = turns & (KS - 1)
    q = (t + KS // 8) >> 6
    r = (t - (q << 6)).astype(F32) * (2.0 * math.pi / KS)
    return rotate(q, *poly_sin_cos(r))


def angle_sin_cos(x):
    n = jnp.floor(x * (2.0 / math.pi) + 0.5)
    r = x - n * 1.5703125
    r = r - n * 4.837512969970703e-4
    r = r - n * 7.549789948768648e-8
    return rotate(n.astype(jnp.int32), *poly_sin_cos(r))


def iota(shape, dim):
    return lax.broadcasted_iota(jnp.int32, shape, dim)


def kernel(
    lines_ref, weights_ref, defocus_ref, sy_ref, sx_ref, volume_hbm, images_hbm,
    scores_ref, update_hbm,
    vbuf, ibuf, split, own, arrived, gather, insert, place_s, place_t,
    fx, ephase, fy, hs, cx, term, sent, landed, zsend, zrecv, tile_f32, tsend, trecv,
    agsend, agrecv, rows, zacc, su,
    in_sem, out_sem, s_send, s_recv, x_send, x_recv, z_send, z_recv, t_send, t_recv, a_send, a_recv,
):
    dom = lax.axis_index("dom")
    slab = lax.axis_index("slab")
    x_lo = dom // 16
    z = (dom // 2) % 8
    c = dom % 2
    zc = z * 2 + c
    partner = (dom + 1 - 2 * c, slab)

    loads = []
    for j in range(2):
        cols = pl.ds(j * 128, 128)
        loads.append(pltpu.make_async_copy(volume_hbm.at[:, :, cols], vbuf.at[j], in_sem.at[j]))
    for j in range(2):
        cols = pl.ds(j * 128, 128)
        loads.append(
            pltpu.make_async_copy(images_hbm.at[:, :, :, cols], ibuf.at[j], in_sem.at[2 + j])
        )
    for load in loads:
        load.start()

    barrier = pltpu.get_barrier_semaphore()

    def tile_peer(k):
        place = lax.rem(x_lo * SLABS + slab + k, XLO * SLABS)
        return (place // SLABS) * 16 + zc, lax.rem(place, SLABS)

    def dom_peer(k):
        return x_lo * 16 + lax.rem(zc + k, 16), slab

    def greet_tile(k, carry):
        pl.semaphore_signal(barrier, inc=1, device_id=tile_peer(k), device_id_type=MESH)
        return carry

    def greet_dom(k, carry):
        pl.semaphore_signal(barrier, inc=1, device_id=dom_peer(k), device_id_type=MESH)
        return carry

    lax.fori_loop(1, XLO * SLABS, greet_tile, 0)
    lax.fori_loop(1, 16, greet_dom, 0)

    lines = lines_ref[...]
    owner = lines >> 10
    local = (lines & (LINES - 1)).astype(F32)
    slab_rows = iota((SLABS, KS), 0)
    marks = jnp.concatenate(
        [(owner[o : o + 1] == slab_rows).astype(F32) for o in range(ORIENT)], 0
    )
    before = (iota((KS, KS), 0) < iota((KS, KS), 1)).astype(F32).astype(BF16)
    earlier = dot(marks.astype(BF16), before) * marks
    ranks = [
        jnp.sum(earlier[o * SLABS : (o + 1) * SLABS], axis=0, keepdims=True).astype(jnp.int32)
        for o in range(ORIENT)
    ]
    own_line = []
    for o in range(ORIENT):
        mine = (owner[o : o + 1] == slab) & (ranks[o] == slab_rows)
        own_line.append(
            jnp.sum(jnp.where(mine, local[o : o + 1], 0.0), axis=1, keepdims=True)
        )
    own_line = jnp.concatenate(own_line, 0).astype(jnp.int32)
    column = iota((ORIENT * OWNED, 2 * LINES), 1)
    gather[0 : ORIENT * OWNED] = (column == 2 * own_line).astype(F32).astype(BF16)
    gather[ORIENT * OWNED :] = (column == 2 * own_line + 1).astype(F32).astype(BF16)

    for j in range(2):
        loads[j].wait()
        picked = dot(gather[...], vbuf.at[j].reshape(2 * LINES, 128)[...]).astype(BF16)
        for part in range(2):
            at = slice(part * KS + j * 128, part * KS + j * 128 + 128)
            for h in range(2):
                first = part * 64 + h * 32
                own[h, :, at] = picked[first : first + 32]

    pl.semaphore_wait(barrier, XLO * SLABS - 1 + 15)

    def slab_copy(k):
        to = lax.rem(slab + k, SLABS)
        return pltpu.make_async_remote_copy(
            src_ref=own.at[c],
            dst_ref=arrived.at[c, slab],
            send_sem=s_send.at[0],
            recv_sem=s_recv.at[0],
            device_id=(dom, to),
            device_id_type=MESH,
        )

    def send_slab(k, carry):
        slab_copy(k).start()
        return carry

    lax.fori_loop(1, SLABS, send_slab, 0)
    arrived[c, slab] = own[c]

    lane = iota((8, 128), 1) % NT
    row_x = jnp.zeros((8, 128), jnp.int32)
    row_y = jnp.zeros((8, 128), jnp.int32)
    for t in range(NT):
        row_x = jnp.where(lane == t, sx_ref[t], row_x)
        row_y = jnp.where(lane == t, sy_ref[t], row_y)
    freq = iota((KS, 128), 0) - HALF
    sin_x, cos_x = turns_sin_cos(freq * row_x[0:1])
    sin_y, cos_y = turns_sin_cos(freq * row_y[0:1])
    wide_lane = iota((KS, 128), 1)
    ephase[0:KS] = jnp.where(wide_lane < NT, cos_y, -sin_y)[:, : 2 * NT].astype(BF16)
    ephase[KS:] = jnp.where(wide_lane < NT, sin_y, cos_y)[:, : 2 * NT].astype(BF16)
    t_cos = cos_x.T[0:NT]
    t_sin = sin_x.T[0:NT]
    table = jnp.concatenate([t_cos, t_sin], 1)
    table_hi = table.astype(BF16)
    table_lo = (table - table_hi.astype(F32)).astype(BF16)
    weights = weights_ref[...]
    weights_hi = weights.astype(BF16)
    weights_lo = (weights - weights_hi.astype(F32)).astype(BF16)
    h = dot(weights_hi, table_hi) + dot(weights_lo, table_hi) + dot(weights_hi, table_lo)
    h = h.astype(BF16).reshape(P_DEV * ORIENT, NT, 2 * KS)
    hs[:, 0:NT] = h[:, :, 0:KS]
    hs[:, NT:] = h[:, :, KS:]
    for o in range(ORIENT):
        rank = ranks[o]
        row = owner[o : o + 1]
        at_t = (rank & 7) * 32 + (rank >> 3) * SLABS + row
        place_t[o] = (iota((KS, KS), 0) == at_t).astype(F32).astype(BF16)

    freq_row = (iota((8, KS), 1) - HALF).astype(F32)
    which = iota((8, KS), 0)
    focus = jnp.zeros((8, KS), F32)
    for p in range(P_DEV):
        focus = jnp.where(which == p, defocus_ref[p], focus)
    sin_d, cos_d = angle_sin_cos(focus * (freq_row * freq_row * (1.0 / (HALF * HALF))))
    sin_col = sin_d.T
    cos_col = cos_d.T
    u_row = 0.1 * sin_d - 0.995 * cos_d
    v_row = -0.995 * sin_d - 0.1 * cos_d
    loads[2].wait()
    loads[3].wait()
    for p in range(P_DEV):
        for j in range(2):
            at = slice(j * 128, j * 128 + 128)
            split[...] = ibuf.at[j, p].reshape(2 * KS, 128)[...].astype(F32)
            ctf = (
                sin_col[:, p : p + 1] * u_row[p : p + 1, at]
                + cos_col[:, p : p + 1] * v_row[p : p + 1, at]
            )
            cx[p, 0, :, at] = ctf * split[pl.ds(0, KS, stride=2), :]
            cx[p, 1, :, at] = ctf * split[pl.ds(1, KS, stride=2), :]

    def placed_term(o):
        for block in range(2):
            at = slice(block * 128, block * 128 + 128)
            low = slice(KS + block * 128, KS + block * 128 + 128)
            t_re = None
            for p in range(P_DEV):
                table_h = hs[p * ORIENT + o]
                g_re = dot(ephase[at], table_h)
                g_im = dot(ephase[low], table_h)
                c_re = cx[p, 0, at]
                c_im = cx[p, 1, at]
                if t_re is None:
                    t_re = c_re * g_re - c_im * g_im
                    t_im = c_re * g_im + c_im * g_re
                else:
                    t_re += c_re * g_re - c_im * g_im
                    t_im += c_re * g_im + c_im * g_re
            term[at, 0:KS] = t_re.astype(BF16)
            term[at, KS:] = t_im.astype(BF16)
        return dot(place_t[o], term[...])

    def pair_copy(j):
        return pltpu.make_async_remote_copy(
            src_ref=sent.at[j],
            dst_ref=landed.at[j],
            send_sem=x_send.at[j],
            recv_sem=x_recv.at[j],
            device_id=partner,
            device_id_type=MESH,
        )

    def z_copy(j, k):
        to = lax.rem(z + k, ZS)
        return pltpu.make_async_remote_copy(
            src_ref=zsend.at[to, j],
            dst_ref=zrecv.at[z, j],
            send_sem=z_send.at[0],
            recv_sem=z_recv.at[0],
            device_id=(x_lo * 16 + to * 2 + c, slab),
            device_id_type=MESH,
        )

    def give(j, carry):
        sent[j] = placed_term(2 * (1 - c) + j).astype(BF16)
        pair_copy(j).start()
        return carry

    lax.fori_loop(0, 2, give, 0)

    def keep(j, carry):
        mine = placed_term(2 * c + j)
        pair_copy(j).wait_recv()
        both = (mine + landed[j].astype(F32)).astype(BF16)
        zsend[:, j] = both.reshape(ZS, NT, 2 * KS)

        def send_z(k, inner):
            z_copy(j, k).start()
            return inner

        lax.fori_loop(1, ZS, send_z, 0)
        zrecv[z, j] = zsend[z, j]
        return carry

    lax.fori_loop(0, 2, keep, 0)

    pltpu.make_async_copy(
        arrived.at[0, pl.ds(0, SLABS - 1)], arrived.at[0, pl.ds(0, SLABS - 1)], s_recv.at[0]
    ).wait()
    forward = pltpu.make_async_remote_copy(
        src_ref=arrived.at[c],
        dst_ref=arrived.at[c],
        send_sem=s_send.at[1],
        recv_sem=s_recv.at[1],
        device_id=partner,
        device_id_type=MESH,
    )
    forward.start()
    for o in range(ORIENT):
        at_s = owner[o : o + 1] * OWNED + ranks[o]
        place_s[o] = (iota((KS, KS), 0) == at_s).astype(F32).astype(BF16)
    group = wide_lane // NT
    for o in range(ORIENT):
        cos_o = jnp.where(group == o, cos_x, 0.0).astype(BF16)
        sin_o = jnp.where(group == o, sin_x, 0.0).astype(BF16)
        fx[o, 0:KS, 0:128] = cos_o
        fx[o, 0:KS, 128:] = -sin_o
        fx[o, KS:, 0:128] = sin_o
        fx[o, KS:, 128:] = cos_o
    table_y = jnp.concatenate([cos_y.T[0:NT], sin_y.T[0:NT]], 1) * (1.0 / KS)
    fy_hi = table_y.astype(BF16)
    fy[0:NT] = fy_hi
    fy[NT:] = (table_y - fy_hi.astype(F32)).astype(BF16)
    insert[...] = gather[...].astype(F32).T.astype(BF16)

    def correlate(half, first):
        for j in range(2):
            o = 2 * half + j
            rows_s = arrived[half, :, j * OWNED : (j + 1) * OWNED, :].reshape(KS, 2 * KS)
            su[...] = dot_t(place_s[o], rows_s)
            for block in range(2):
                at = slice(block * 128, block * 128 + 128)
                for p in range(P_DEV):
                    s_re = su[at, 0:KS]
                    s_im = su[at, KS:]
                    c_re = cx[p, 0, at]
                    c_im = cx[p, 1, at]
                    q_re = (s_re * c_re + s_im * c_im).astype(BF16)
                    q_im = (s_re * c_im - s_im * c_re).astype(BF16)
                    part = dot(q_re, fx[o, 0:KS]) + dot(q_im, fx[o, KS:])
                    if first and j == 0:
                        zacc[p, at] = part
                    else:
                        zacc[p, at] += part

    correlate(c, True)
    forward.wait_recv()
    correlate(1 - c, False)
    for p in range(P_DEV):
        full = jnp.concatenate([zacc[p, :, 0:128], zacc[p, :, 128:]], 0)
        full_hi = full.astype(BF16)
        full_lo = (full - full_hi.astype(F32)).astype(BF16)
        both = dot(fy[...], full_hi)
        scores_ref[p] = both[0:NT] + both[NT:] + dot(fy[0:NT], full_lo)

    pltpu.make_async_copy(zrecv.at[pl.ds(0, ZS - 1)], zrecv.at[pl.ds(0, ZS - 1)], z_recv.at[0]).wait()
    for j in range(2):
        for r in range(2):
            at = slice(r * SLABS, (r + 1) * SLABS)
            total = zrecv[0, j, at].astype(F32)
            for other in range(1, ZS):
                total += zrecv[other, j, at].astype(F32)
            for b in range(4):
                tile_f32[pl.ds(j * 8 + r * 4 + b, SLABS, stride=16), :] = total[
                    :, b * 128 : (b + 1) * 128
                ]
    tsend[...] = tile_f32[...].astype(BF16).reshape(SLABS, 16, 128)

    here = x_lo * SLABS + slab

    def tile_copy(k):
        to = tile_peer(k)
        return pltpu.make_async_remote_copy(
            src_ref=tsend.at[to[1]],
            dst_ref=trecv.at[here],
            send_sem=t_send.at[0],
            recv_sem=t_recv.at[0],
            device_id=to,
            device_id_type=MESH,
        )

    def send_tile(k, carry):
        tile_copy(k).start()
        return carry

    lax.fori_loop(1, XLO * SLABS, send_tile, 0)
    trecv[here] = tsend[slab]
    pltpu.make_async_copy(
        trecv.at[pl.ds(0, XLO * SLABS - 1)], trecv.at[pl.ds(0, XLO * SLABS - 1)], t_recv.at[0]
    ).wait()
    total = trecv[0].astype(F32)
    for other in range(1, XLO * SLABS):
        total += trecv[other].astype(F32)
    agsend[...] = (total * SCALE).astype(BF16)

    def dom_copy(k):
        return pltpu.make_async_remote_copy(
            src_ref=agsend,
            dst_ref=agrecv.at[zc],
            send_sem=a_send.at[0],
            recv_sem=a_recv.at[0],
            device_id=dom_peer(k),
            device_id_type=MESH,
        )

    def send_dom(k, carry):
        dom_copy(k).start()
        return carry

    lax.fori_loop(1, 16, send_dom, 0)
    agrecv[zc] = agsend[...]
    pltpu.make_async_copy(agrecv.at[pl.ds(0, 15)], agrecv.at[pl.ds(0, 15)], a_recv.at[0]).wait()

    tile_f32[...] = agrecv[...].astype(F32).reshape(256, 128)
    for o in range(ORIENT):
        for r in range(2):
            for b in range(4):
                got = tile_f32[
                    pl.ds((o // 2) * 16 + (o % 2) * 8 + r * 4 + b, ZS, stride=32), :
                ]
                first = (b // 2) * 64 + o * OWNED + r * 8
                rows[first : first + 8, (b % 2) * 128 : (b % 2) * 128 + 128] = got
    rows_bf16 = rows[...].astype(BF16)
    placed = dot(insert[...], rows_bf16).astype(BF16)
    outs = []
    for j in range(2):
        vbuf.at[j].reshape(2 * LINES, 128)[...] = placed[:, j * 128 : j * 128 + 128]
        outs.append(
            pltpu.make_async_copy(
                vbuf.at[j], update_hbm.at[:, :, pl.ds(j * 128, 128)], out_sem.at[j]
            )
        )
        outs[j].start()

    pltpu.make_async_copy(
        arrived.at[0, pl.ds(0, SLABS - 1)], arrived.at[0, pl.ds(0, SLABS - 1)], s_send.at[0]
    ).wait()
    forward.wait_send()
    for j in range(2):
        pair_copy(j).wait_send()
    pltpu.make_async_copy(zrecv.at[pl.ds(0, ZS - 1)], zrecv.at[pl.ds(0, ZS - 1)], z_send.at[0]).wait()
    pltpu.make_async_copy(
        trecv.at[pl.ds(0, XLO * SLABS - 1)], trecv.at[pl.ds(0, XLO * SLABS - 1)], t_send.at[0]
    ).wait()
    pltpu.make_async_copy(agrecv.at[pl.ds(0, 15)], agrecv.at[pl.ds(0, 15)], a_send.at[0]).wait()
    for out in outs:
        out.wait()


def body(volume, images, defocus, soft_weights, slice_lines, shift_y, shift_x):
    vmem = pl.BlockSpec(memory_space=pltpu.VMEM)
    smem = pl.BlockSpec(memory_space=pltpu.SMEM)
    hbm = pl.BlockSpec(memory_space=pl.ANY)
    dma = pltpu.SemaphoreType.DMA
    scores, line_update = pl.pallas_call(
        kernel,
        out_shape=(
            jax.ShapeDtypeStruct((P_DEV, NT, ORIENT * NT), F32),
            jax.ShapeDtypeStruct((LINES, 2, KS), BF16),
        ),
        in_specs=[vmem, vmem, smem, smem, smem, hbm, hbm],
        out_specs=(vmem, hbm),
        scratch_shapes=[
            pltpu.VMEM((2, LINES, 2, 128), BF16),
            pltpu.VMEM((2, P_DEV, KS, 2, 128), BF16),
            pltpu.VMEM((2 * KS, 128), F32),
            pltpu.VMEM((2, 2 * OWNED, 2 * KS), BF16),
            pltpu.VMEM((2, SLABS, 2 * OWNED, 2 * KS), BF16),
            pltpu.VMEM((2 * ORIENT * OWNED, 2 * LINES), BF16),
            pltpu.VMEM((2 * LINES, 2 * ORIENT * OWNED), BF16),
            pltpu.VMEM((ORIENT, KS, KS), BF16),
            pltpu.VMEM((ORIENT, KS, KS), BF16),
            pltpu.VMEM((ORIENT, 2 * KS, 256), BF16),
            pltpu.VMEM((2 * KS, 2 * NT), BF16),
            pltpu.VMEM((2 * NT, 2 * KS), BF16),
            pltpu.VMEM((P_DEV * ORIENT, 2 * NT, KS), BF16),
            pltpu.VMEM((P_DEV, 2, KS, KS), F32),
            pltpu.VMEM((KS, 2 * KS), BF16),
            pltpu.VMEM((2, KS, 2 * KS), BF16),
            pltpu.VMEM((2, KS, 2 * KS), BF16),
            pltpu.VMEM((ZS, 2, NT, 2 * KS), BF16),
            pltpu.VMEM((ZS, 2, NT, 2 * KS), BF16),
            pltpu.VMEM((256, 128), F32),
            pltpu.VMEM((SLABS, 16, 128), BF16),
            pltpu.VMEM((XLO * SLABS, 16, 128), BF16),
            pltpu.VMEM((16, 128), BF16),
            pltpu.VMEM((16, 16, 128), BF16),
            pltpu.VMEM((2 * ORIENT * OWNED, KS), F32),
            pltpu.VMEM((P_DEV, KS, 256), F32),
            pltpu.VMEM((KS, 2 * KS), F32),
            dma((4,)),
            dma((2,)),
            dma((2,)),
            dma((2,)),
            dma((2,)),
            dma((2,)),
            dma((1,)),
            dma((1,)),
            dma((1,)),
            dma((1,)),
            dma((1,)),
            dma((1,)),
        ],
        compiler_params=pltpu.CompilerParams(
            collective_id=0, has_side_effects=True, vmem_limit_bytes=48 * 1024 * 1024
        ),
        name="cryo",
    )(
        slice_lines,
        soft_weights.reshape(P_DEV * ORIENT * NT, NT),
        defocus,
        shift_y,
        shift_x,
        volume,
        images,
    )
    scores = scores.reshape(P_DEV, NT, ORIENT, NT).transpose(0, 2, 1, 3)
    return scores, line_update


def solution(mesh):
    placed = (
        P("slab", None, None),
        P(("dom", "slab"), None, None, None),
        P(("dom", "slab")),
        P(("dom", "slab"), None, None, None),
        P(),
        P(),
        P(),
    )
    return jax.shard_map(
        body,
        mesh=mesh,
        in_specs=placed,
        out_specs=(P(("dom", "slab"), None, None, None), P("slab", None, None)),
        check_vma=False,
    )
```

```python
import math

import jax
import jax.numpy as jnp
from jax import lax
from jax.experimental import pallas as pl
from jax.experimental.pallas import tpu as pltpu
from jax.sharding import PartitionSpec as P

KS = 256
HALF = KS // 2
P_DEV = 4
LINES = 1024
ORIENT = 4
NT = 32
OWNED = 16
PARTICLES = 2048
SLABS = 16
ZS = 8
YS = 8
XLO = 2
SCALE = 1.0 / math.sqrt(NT * NT * PARTICLES)
F32 = jnp.float32
BF16 = jnp.bfloat16
MESH = pl.DeviceIdType.MESH


def dot(a, b):
    return jnp.dot(a, b, preferred_element_type=F32)


def dot_t(a, b):
    return lax.dot_general(a, b, (((0,), (0,)), ((), ())), preferred_element_type=F32)


def poly_sin_cos(r):
    s = r * r
    sin = r * (1.0 + s * (-1 / 6 + s * (1 / 120 + s * (-1 / 5040 + s * (1 / 362880)))))
    cos = 1.0 + s * (-0.5 + s * (1 / 24 + s * (-1 / 720 + s * (1 / 40320))))
    return sin, cos


def rotate(quadrant, sin, cos):
    q = quadrant & 3
    odd = (q & 1) == 1
    s = jnp.where(odd, cos, sin)
    c = jnp.where(odd, sin, cos)
    s = jnp.where(q >= 2, -s, s)
    c = jnp.where((q == 1) | (q == 2), -c, c)
    return s, c


def turns_sin_cos(turns):
    t = turns & (KS - 1)
    q = (t + KS // 8) >> 6
    r = (t - (q << 6)).astype(F32) * (2.0 * math.pi / KS)
    return rotate(q, *poly_sin_cos(r))


def angle_sin_cos(x):
    n = jnp.floor(x * (2.0 / math.pi) + 0.5)
    r = x - n * 1.5703125
    r = r - n * 4.837512969970703e-4
    r = r - n * 7.549789948768648e-8
    return rotate(n.astype(jnp.int32), *poly_sin_cos(r))


def iota(shape, dim):
    return lax.broadcasted_iota(jnp.int32, shape, dim)


def kernel(
    lines_hbm, weights_hbm, defocus_hbm, sy_hbm, sx_hbm, volume_hbm, images_hbm,
    scores_ref, update_hbm,
    lines_ref, weights_ref, defocus_ref, sy_ref, sx_ref,
    vbuf, ibuf, split, own, arrived, gather, insert, place_s, place_t,
    fx, ephase, fy, hs, cx, term, sent, landed, xsend, xrecv, zsend, zrecv, ysend, yrecv,
    agsend, agrecv, tile_z, tile_f32, rows, zacc, su,
    small_sem, in_sem, out_sem, s_send, s_recv, p_send, p_recv, x_send, x_recv, z_send, z_recv,
    y_send, y_recv, a_send, a_recv,
):
    dom = lax.axis_index("dom")
    slab = lax.axis_index("slab")
    x_lo = dom // 16
    z = (dom // 2) % 8
    c = dom % 2
    zc = z * 2 + c
    partner = (dom + 1 - 2 * c, slab)
    y = slab // 2
    x_hi = slab % 2
    x = x_hi * 2 + x_lo

    small = [
        pltpu.make_async_copy(src, dst, small_sem.at[i])
        for i, (src, dst) in enumerate(
            (
                (lines_hbm, lines_ref),
                (sx_hbm, sx_ref),
                (sy_hbm, sy_ref),
                (defocus_hbm, defocus_ref),
                (weights_hbm, weights_ref),
            )
        )
    ]
    for load in small:
        load.start()
    loads = []
    for j in range(2):
        cols = pl.ds(j * 128, 128)
        loads.append(pltpu.make_async_copy(volume_hbm.at[:, :, cols], vbuf.at[j], in_sem.at[j]))
    for j in range(2):
        cols = pl.ds(j * 128, 128)
        loads.append(
            pltpu.make_async_copy(images_hbm.at[:, :, :, cols], ibuf.at[j], in_sem.at[2 + j])
        )
    for load in loads:
        load.start()

    barrier = pltpu.get_barrier_semaphore()

    def slab_peer(k):
        return dom, lax.rem(slab + k, SLABS)

    def x_peer(k):
        to = lax.rem(x + k, 4)
        return (to % 2) * 16 + zc, y * 2 + to // 2

    def y_peer(k):
        to = lax.rem(x_lo * YS + y + k, XLO * YS)
        return (to // YS) * 16 + zc, (to % YS) * 2 + x_hi

    def dom_peer(k):
        return x_lo * 16 + lax.rem(zc + k, 16), slab

    def greet(peer):
        pl.semaphore_signal(barrier, inc=1, device_id=peer, device_id_type=MESH)

    def greet_both(k, carry):
        greet(slab_peer(k))
        greet(dom_peer(k))
        return carry

    def greet_other(k, carry):
        greet(((1 - x_lo) * 16 + zc, k * 2 + x_hi))
        return carry

    lax.fori_loop(1, SLABS, greet_both, 0)
    lax.fori_loop(0, YS, greet_other, 0)
    greet(((1 - x_lo) * 16 + zc, y * 2 + 1 - x_hi))

    small[0].wait()
    lines = lines_ref[...]
    owner = lines >> 10
    local = (lines & (LINES - 1)).astype(F32)
    slab_rows = iota((SLABS, KS), 0)
    marks = jnp.concatenate(
        [(owner[o : o + 1] == slab_rows).astype(F32) for o in range(ORIENT)], 0
    )
    before = (iota((KS, KS), 0) < iota((KS, KS), 1)).astype(F32).astype(BF16)
    earlier = dot(marks.astype(BF16), before) * marks
    ranks = [
        jnp.sum(earlier[o * SLABS : (o + 1) * SLABS], axis=0, keepdims=True).astype(jnp.int32)
        for o in range(ORIENT)
    ]
    own_line = []
    for o in range(ORIENT):
        mine = (owner[o : o + 1] == slab) & (ranks[o] == slab_rows)
        own_line.append(
            jnp.sum(jnp.where(mine, local[o : o + 1], 0.0), axis=1, keepdims=True)
        )
    own_line = jnp.concatenate(own_line, 0).astype(jnp.int32)
    half_line = jnp.where(c == 0, own_line[0 : 2 * OWNED], own_line[2 * OWNED :])
    column = iota((2 * OWNED, 2 * LINES), 1)
    gather[0 : 2 * OWNED] = (column == 2 * half_line).astype(F32).astype(BF16)
    gather[2 * OWNED :] = (column == 2 * half_line + 1).astype(F32).astype(BF16)

    for j in range(2):
        loads[j].wait()
        picked = dot(gather[...], vbuf.at[j].reshape(2 * LINES, 128)[...]).astype(BF16)
        for part in range(2):
            at = slice(part * KS + j * 128, part * KS + j * 128 + 128)
            own[:, at] = picked[part * 32 : part * 32 + 32]

    pl.semaphore_wait(barrier, 2 * (SLABS - 1) + YS + 1)

    def slab_copy(k):
        return pltpu.make_async_remote_copy(
            src_ref=own,
            dst_ref=arrived.at[c, slab],
            send_sem=s_send.at[0],
            recv_sem=s_recv.at[0],
            device_id=slab_peer(k),
            device_id_type=MESH,
        )

    def send_slab(k, carry):
        slab_copy(k).start()
        return carry

    lax.fori_loop(1, SLABS, send_slab, 0)
    arrived[c, slab] = own[...]

    small[1].wait()
    small[2].wait()
    lane = iota((8, 128), 1) % NT
    row_x = jnp.zeros((8, 128), jnp.int32)
    row_y = jnp.zeros((8, 128), jnp.int32)
    for t in range(NT):
        row_x = jnp.where(lane == t, sx_ref[t], row_x)
        row_y = jnp.where(lane == t, sy_ref[t], row_y)
    freq = iota((KS, 128), 0) - HALF
    sin_x, cos_x = turns_sin_cos(freq * row_x[0:1])
    sin_y, cos_y = turns_sin_cos(freq * row_y[0:1])
    wide_lane = iota((KS, 128), 1)
    ephase[0:KS] = jnp.where(wide_lane < NT, cos_y, -sin_y)[:, : 2 * NT].astype(BF16)
    ephase[KS:] = jnp.where(wide_lane < NT, sin_y, cos_y)[:, : 2 * NT].astype(BF16)
    t_cos = cos_x.T[0:NT]
    t_sin = sin_x.T[0:NT]
    table = jnp.concatenate([t_cos, t_sin], 1)
    table_hi = table.astype(BF16)
    table_lo = (table - table_hi.astype(F32)).astype(BF16)
    small[4].wait()
    weights = weights_ref[...]
    weights_hi = weights.astype(BF16)
    weights_lo = (weights - weights_hi.astype(F32)).astype(BF16)
    h = dot(weights_hi, table_hi) + dot(weights_lo, table_hi) + dot(weights_hi, table_lo)
    h = h.astype(BF16).reshape(P_DEV * ORIENT, NT, 2 * KS)
    hs[:, 0:NT] = h[:, :, 0:KS]
    hs[:, NT:] = h[:, :, KS:]
    for o in range(ORIENT):
        rank = ranks[o]
        row = owner[o : o + 1]
        at_t = (row & 1) * 128 + (rank >> 3) * 64 + (rank & 7) * YS + (row >> 1)
        place_t[o] = (iota((KS, KS), 0) == at_t).astype(F32).astype(BF16)

    freq_row = (iota((8, KS), 1) - HALF).astype(F32)
    which = iota((8, KS), 0)
    focus = jnp.zeros((8, KS), F32)
    small[3].wait()
    for p in range(P_DEV):
        focus = jnp.where(which == p, defocus_ref[p], focus)
    sin_d, cos_d = angle_sin_cos(focus * (freq_row * freq_row * (1.0 / (HALF * HALF))))
    sin_col = sin_d.T
    cos_col = cos_d.T
    u_row = 0.1 * sin_d - 0.995 * cos_d
    v_row = -0.995 * sin_d - 0.1 * cos_d
    loads[2].wait()
    loads[3].wait()
    for p in range(P_DEV):
        for j in range(2):
            at = slice(j * 128, j * 128 + 128)
            split[...] = ibuf.at[j, p].reshape(2 * KS, 128)[...].astype(F32)
            ctf = (
                sin_col[:, p : p + 1] * u_row[p : p + 1, at]
                + cos_col[:, p : p + 1] * v_row[p : p + 1, at]
            )
            cx[p, 0, :, at] = ctf * split[pl.ds(0, KS, stride=2), :]
            cx[p, 1, :, at] = ctf * split[pl.ds(1, KS, stride=2), :]

    def placed_term(o):
        for block in range(2):
            at = slice(block * 128, block * 128 + 128)
            low = slice(KS + block * 128, KS + block * 128 + 128)
            t_re = None
            for p in range(P_DEV):
                table_h = hs[p * ORIENT + o]
                g_re = dot(ephase[at], table_h)
                g_im = dot(ephase[low], table_h)
                c_re = cx[p, 0, at]
                c_im = cx[p, 1, at]
                if t_re is None:
                    t_re = c_re * g_re - c_im * g_im
                    t_im = c_re * g_im + c_im * g_re
                else:
                    t_re += c_re * g_re - c_im * g_im
                    t_im += c_re * g_im + c_im * g_re
            term[at, 0:KS] = t_re.astype(BF16)
            term[at, KS:] = t_im.astype(BF16)
        return dot(place_t[o], term[...])

    def pair_copy(j):
        return pltpu.make_async_remote_copy(
            src_ref=sent.at[j],
            dst_ref=landed.at[j],
            send_sem=p_send.at[j],
            recv_sem=p_recv.at[j],
            device_id=partner,
            device_id_type=MESH,
        )

    def x_copy(j, k):
        return pltpu.make_async_remote_copy(
            src_ref=xsend.at[j, lax.rem(x + k, 4)],
            dst_ref=xrecv.at[j, x],
            send_sem=x_send.at[j],
            recv_sem=x_recv.at[j],
            device_id=x_peer(k),
            device_id_type=MESH,
        )

    def z_copy(j, k):
        to = lax.rem(z + k, ZS)
        return pltpu.make_async_remote_copy(
            src_ref=zsend.at[j, to],
            dst_ref=zrecv.at[j, z],
            send_sem=z_send.at[0],
            recv_sem=z_recv.at[0],
            device_id=(x_lo * 16 + to * 2 + c, slab),
            device_id_type=MESH,
        )

    def give(j, carry):
        sent[j] = placed_term(2 * (1 - c) + j).astype(BF16)
        pair_copy(j).start()
        return carry

    lax.fori_loop(0, 2, give, 0)

    def keep(j, carry):
        mine = placed_term(2 * c + j)
        pair_copy(j).wait_recv()
        both = (mine + landed[j].astype(F32)).astype(BF16)
        xsend[j] = both.reshape(4, 64, 2 * KS)

        def send_x(k, inner):
            x_copy(j, k).start()
            return inner

        lax.fori_loop(1, 4, send_x, 0)
        xrecv[j, x] = xsend[j, x]
        return carry

    lax.fori_loop(0, 2, keep, 0)

    pltpu.make_async_copy(
        arrived.at[0, pl.ds(0, SLABS - 1)], arrived.at[0, pl.ds(0, SLABS - 1)], s_recv.at[0]
    ).wait()
    forward = pltpu.make_async_remote_copy(
        src_ref=arrived.at[c],
        dst_ref=arrived.at[c],
        send_sem=s_send.at[1],
        recv_sem=s_recv.at[1],
        device_id=partner,
        device_id_type=MESH,
    )
    forward.start()
    for o in range(ORIENT):
        at_s = owner[o : o + 1] * OWNED + ranks[o]
        place_s[o] = (iota((KS, KS), 0) == at_s).astype(F32).astype(BF16)
    group = wide_lane // NT
    for o in range(ORIENT):
        cos_o = jnp.where(group == o, cos_x, 0.0).astype(BF16)
        sin_o = jnp.where(group == o, sin_x, 0.0).astype(BF16)
        fx[o, 0:KS, 0:128] = cos_o
        fx[o, 0:KS, 128:] = -sin_o
        fx[o, KS:, 0:128] = sin_o
        fx[o, KS:, 128:] = cos_o
    table_y = jnp.concatenate([cos_y.T[0:NT], sin_y.T[0:NT]], 1) * (1.0 / KS)
    fy_hi = table_y.astype(BF16)
    fy[0:NT] = fy_hi
    fy[NT:] = (table_y - fy_hi.astype(F32)).astype(BF16)

    def correlate(half, first):
        for j in range(2):
            o = 2 * half + j
            rows_s = arrived[half, :, j * OWNED : (j + 1) * OWNED, :].reshape(KS, 2 * KS)
            su[...] = dot_t(place_s[o], rows_s)
            for block in range(2):
                at = slice(block * 128, block * 128 + 128)
                for p in range(P_DEV):
                    s_re = su[at, 0:KS]
                    s_im = su[at, KS:]
                    c_re = cx[p, 0, at]
                    c_im = cx[p, 1, at]
                    q_re = (s_re * c_re + s_im * c_im).astype(BF16)
                    q_im = (s_re * c_im - s_im * c_re).astype(BF16)
                    part = dot(q_re, fx[o, 0:KS]) + dot(q_im, fx[o, KS:])
                    if first and j == 0:
                        zacc[p, at] = part
                    else:
                        zacc[p, at] += part

    correlate(c, True)

    def pass_on(j, carry):
        pltpu.make_async_copy(
            xrecv.at[j, pl.ds(0, 3)], xrecv.at[j, pl.ds(0, 3)], x_recv.at[j]
        ).wait()
        for part in range(2):
            at = slice(part * KS, part * KS + KS)
            total = xrecv[j, 0, :, at].astype(F32)
            for other in range(1, 4):
                total += xrecv[j, other, :, at].astype(F32)
            tile_z[:, part * YS : part * YS + YS] = total.reshape(ZS, YS, KS)
        zsend[j] = tile_z[...].astype(BF16)

        def send_z(k, inner):
            z_copy(j, k).start()
            return inner

        lax.fori_loop(1, ZS, send_z, 0)
        zrecv[j, z] = zsend[j, z]
        return carry

    lax.fori_loop(0, 2, pass_on, 0)
    forward.wait_recv()
    correlate(1 - c, False)
    pltpu.make_async_copy(
        zrecv.at[:, pl.ds(0, ZS - 1)], zrecv.at[:, pl.ds(0, ZS - 1)], z_recv.at[0]
    ).wait()
    for j in range(2):
        total = zrecv[j, 0].astype(F32)
        for other in range(1, ZS):
            total += zrecv[j, other].astype(F32)
        for part in range(2):
            for b in range(2):
                tile_f32[pl.ds(j * 4 + part * 2 + b, YS, stride=8), :] = total[
                    part * YS : part * YS + YS, b * 128 : b * 128 + 128
                ]
    ysend[...] = tile_f32[0 : YS * 8].reshape(YS, 8, 128)

    def y_copy(k):
        to = lax.rem(x_lo * YS + y + k, XLO * YS)
        return pltpu.make_async_remote_copy(
            src_ref=ysend.at[to % YS],
            dst_ref=yrecv.at[x_lo * YS + y],
            send_sem=y_send.at[0],
            recv_sem=y_recv.at[0],
            device_id=y_peer(k),
            device_id_type=MESH,
        )

    def send_y(k, carry):
        y_copy(k).start()
        return carry

    lax.fori_loop(1, XLO * YS, send_y, 0)
    yrecv[x_lo * YS + y] = ysend[y]
    for p in range(P_DEV):
        full = jnp.concatenate([zacc[p, :, 0:128], zacc[p, :, 128:]], 0)
        full_hi = full.astype(BF16)
        full_lo = (full - full_hi.astype(F32)).astype(BF16)
        both = dot(fy[...], full_hi)
        scores_ref[p] = both[0:NT] + both[NT:] + dot(fy[0:NT], full_lo)

    line_row = jnp.concatenate([2 * own_line, 2 * own_line + 1], 0).astype(F32)
    line_row = jnp.broadcast_to(line_row, (128, 128)).T[0:1].astype(jnp.int32)
    insert[...] = (iota((2 * LINES, 128), 0) == line_row).astype(F32).astype(BF16)
    pltpu.make_async_copy(
        yrecv.at[pl.ds(0, XLO * YS - 1)], yrecv.at[pl.ds(0, XLO * YS - 1)], y_recv.at[0]
    ).wait()
    sums = []
    for half in range(XLO):
        total = yrecv[half * YS]
        for other in range(1, YS):
            total += yrecv[half * YS + other]
        sums.append(total * SCALE)
    agsend[...] = jnp.concatenate(sums, 0).astype(BF16)

    def dom_copy(k):
        return pltpu.make_async_remote_copy(
            src_ref=agsend,
            dst_ref=agrecv.at[zc],
            send_sem=a_send.at[0],
            recv_sem=a_recv.at[0],
            device_id=dom_peer(k),
            device_id_type=MESH,
        )

    def send_dom(k, carry):
        dom_copy(k).start()
        return carry

    lax.fori_loop(1, 16, send_dom, 0)
    agrecv[zc] = agsend[...]
    pltpu.make_async_copy(agrecv.at[pl.ds(0, 15)], agrecv.at[pl.ds(0, 15)], a_recv.at[0]).wait()

    tile_f32[...] = agrecv[...].astype(F32).reshape(256, 128)
    for o in range(ORIENT):
        for r in range(2):
            for b in range(4):
                got = tile_f32[
                    pl.ds((o // 2) * 16 + r * 8 + (o % 2) * 4 + b, ZS, stride=32), :
                ]
                first = (b // 2) * 64 + o * OWNED + r * 8
                rows[first : first + 8, (b % 2) * 128 : (b % 2) * 128 + 128] = got
    rows_bf16 = rows[...].astype(BF16)
    placed = dot(insert[...], rows_bf16).astype(BF16)
    outs = []
    for j in range(2):
        vbuf.at[j].reshape(2 * LINES, 128)[...] = placed[:, j * 128 : j * 128 + 128]
        outs.append(
            pltpu.make_async_copy(
                vbuf.at[j], update_hbm.at[:, :, pl.ds(j * 128, 128)], out_sem.at[j]
            )
        )
        outs[j].start()

    pltpu.make_async_copy(
        arrived.at[0, pl.ds(0, SLABS - 1)], arrived.at[0, pl.ds(0, SLABS - 1)], s_send.at[0]
    ).wait()
    forward.wait_send()
    for j in range(2):
        pair_copy(j).wait_send()
    for j in range(2):
        pltpu.make_async_copy(
            xrecv.at[j, pl.ds(0, 3)], xrecv.at[j, pl.ds(0, 3)], x_send.at[j]
        ).wait()
    pltpu.make_async_copy(
        zrecv.at[:, pl.ds(0, ZS - 1)], zrecv.at[:, pl.ds(0, ZS - 1)], z_send.at[0]
    ).wait()
    pltpu.make_async_copy(
        yrecv.at[pl.ds(0, XLO * YS - 1)], yrecv.at[pl.ds(0, XLO * YS - 1)], y_send.at[0]
    ).wait()
    pltpu.make_async_copy(agrecv.at[pl.ds(0, 15)], agrecv.at[pl.ds(0, 15)], a_send.at[0]).wait()
    for out in outs:
        out.wait()


def body(volume, images, defocus, soft_weights, slice_lines, shift_y, shift_x):
    vmem = pl.BlockSpec(memory_space=pltpu.VMEM)
    hbm = pl.BlockSpec(memory_space=pl.ANY)
    dma = pltpu.SemaphoreType.DMA
    scores, line_update = pl.pallas_call(
        kernel,
        out_shape=(
            jax.ShapeDtypeStruct((P_DEV, NT, ORIENT * NT), F32),
            jax.ShapeDtypeStruct((LINES, 2, KS), BF16),
        ),
        in_specs=[hbm] * 7,
        out_specs=(vmem, hbm),
        scratch_shapes=[
            pltpu.VMEM((ORIENT, KS), jnp.int32),
            pltpu.VMEM((P_DEV * ORIENT * NT, NT), F32),
            pltpu.SMEM((P_DEV,), F32),
            pltpu.SMEM((NT,), jnp.int32),
            pltpu.SMEM((NT,), jnp.int32),
            pltpu.VMEM((2, LINES, 2, 128), BF16),
            pltpu.VMEM((2, P_DEV, KS, 2, 128), BF16),
            pltpu.VMEM((2 * KS, 128), F32),
            pltpu.VMEM((2 * OWNED, 2 * KS), BF16),
            pltpu.VMEM((2, SLABS, 2 * OWNED, 2 * KS), BF16),
            pltpu.VMEM((4 * OWNED, 2 * LINES), BF16),
            pltpu.VMEM((2 * LINES, 2 * ORIENT * OWNED), BF16),
            pltpu.VMEM((ORIENT, KS, KS), BF16),
            pltpu.VMEM((ORIENT, KS, KS), BF16),
            pltpu.VMEM((ORIENT, 2 * KS, 256), BF16),
            pltpu.VMEM((2 * KS, 2 * NT), BF16),
            pltpu.VMEM((2 * NT, 2 * KS), BF16),
            pltpu.VMEM((P_DEV * ORIENT, 2 * NT, KS), BF16),
            pltpu.VMEM((P_DEV, 2, KS, KS), F32),
            pltpu.VMEM((KS, 2 * KS), BF16),
            pltpu.VMEM((2, KS, 2 * KS), BF16),
            pltpu.VMEM((2, KS, 2 * KS), BF16),
            pltpu.VMEM((2, 4, 64, 2 * KS), BF16),
            pltpu.VMEM((2, 4, 64, 2 * KS), BF16),
            pltpu.VMEM((2, ZS, 16, KS), BF16),
            pltpu.VMEM((2, ZS, 16, KS), BF16),
            pltpu.VMEM((YS, 8, 128), F32),
            pltpu.VMEM((XLO * YS, 8, 128), F32),
            pltpu.VMEM((16, 128), BF16),
            pltpu.VMEM((16, 16, 128), BF16),
            pltpu.VMEM((ZS, 16, KS), F32),
            pltpu.VMEM((256, 128), F32),
            pltpu.VMEM((2 * ORIENT * OWNED, KS), F32),
            pltpu.VMEM((P_DEV, KS, 256), F32),
            pltpu.VMEM((KS, 2 * KS), F32),
            dma((5,)),
            dma((4,)),
            dma((2,)),
            dma((2,)),
            dma((2,)),
            dma((2,)),
            dma((2,)),
            dma((2,)),
            dma((2,)),
            dma((1,)),
            dma((1,)),
            dma((1,)),
            dma((1,)),
            dma((1,)),
            dma((1,)),
        ],
        compiler_params=pltpu.CompilerParams(
            collective_id=0, has_side_effects=True, vmem_limit_bytes=48 * 1024 * 1024
        ),
        name="cryo",
    )(
        slice_lines,
        soft_weights.reshape(P_DEV * ORIENT * NT, NT),
        defocus,
        shift_y,
        shift_x,
        volume,
        images,
    )
    scores = scores.reshape(P_DEV, NT, ORIENT, NT).transpose(0, 2, 1, 3)
    return scores, line_update


def solution(mesh):
    placed = (
        P("slab", None, None),
        P(("dom", "slab"), None, None, None),
        P(("dom", "slab")),
        P(("dom", "slab"), None, None, None),
        P(),
        P(),
        P(),
    )
    return jax.shard_map(
        body,
        mesh=mesh,
        in_specs=placed,
        out_specs=(P(("dom", "slab"), None, None, None), P("slab", None, None)),
        check_vma=False,
    )
```

```python
import math

import jax
import jax.numpy as jnp
from jax import lax
from jax.experimental import pallas as pl
from jax.experimental.pallas import tpu as pltpu
from jax.sharding import PartitionSpec as P

KS = 256
HALF = KS // 2
P_DEV = 4
LINES = 1024
ORIENT = 4
NT = 32
OWNED = 16
PARTICLES = 2048
SLABS = 16
ZS = 8
YS = 8
XLO = 2
SCALE = 1.0 / math.sqrt(NT * NT * PARTICLES)
F32 = jnp.float32
BF16 = jnp.bfloat16
MESH = pl.DeviceIdType.MESH


def dot(a, b):
    return jnp.dot(a, b, preferred_element_type=F32)


def dot_t(a, b):
    return lax.dot_general(a, b, (((0,), (0,)), ((), ())), preferred_element_type=F32)


def poly_sin_cos(r):
    s = r * r
    sin = r * (1.0 + s * (-1 / 6 + s * (1 / 120 + s * (-1 / 5040 + s * (1 / 362880)))))
    cos = 1.0 + s * (-0.5 + s * (1 / 24 + s * (-1 / 720 + s * (1 / 40320))))
    return sin, cos


def rotate(quadrant, sin, cos):
    q = quadrant & 3
    odd = (q & 1) == 1
    s = jnp.where(odd, cos, sin)
    c = jnp.where(odd, sin, cos)
    s = jnp.where(q >= 2, -s, s)
    c = jnp.where((q == 1) | (q == 2), -c, c)
    return s, c


def turns_sin_cos(turns):
    t = turns & (KS - 1)
    q = (t + KS // 8) >> 6
    r = (t - (q << 6)).astype(F32) * (2.0 * math.pi / KS)
    return rotate(q, *poly_sin_cos(r))


def angle_sin_cos(x):
    n = jnp.floor(x * (2.0 / math.pi) + 0.5)
    r = x - n * 1.5703125
    r = r - n * 4.837512969970703e-4
    r = r - n * 7.549789948768648e-8
    return rotate(n.astype(jnp.int32), *poly_sin_cos(r))


def iota(shape, dim):
    return lax.broadcasted_iota(jnp.int32, shape, dim)


def kernel(
    lines_hbm, weights_hbm, defocus_hbm, sy_hbm, sx_hbm, volume_hbm, images_hbm,
    scores_ref, update_hbm,
    lines_ref, weights_ref, defocus_ref, sy_ref, sx_ref,
    vbuf, ibuf, split, own, arrived, gather, insert, place_s, place_t,
    fx, ephase, fy, hs, cx, term, sent, landed, xsend, xrecv, ysend, yrecv, zsend, zrecv,
    fin, tile_y, rows, zacc, su,
    small_sem, in_sem, out_sem, s_send, s_recv, p_send, p_recv, x_send, x_recv, z_send, z_recv,
    y_send, y_recv, f_send, f_recv,
):
    dom = lax.axis_index("dom")
    slab = lax.axis_index("slab")
    x_lo = dom // 16
    z = (dom // 2) % 8
    c = dom % 2
    zc = z * 2 + c
    partner = (dom + 1 - 2 * c, slab)
    y = slab // 2
    x_hi = slab % 2
    x = x_hi * 2 + x_lo

    small = [
        pltpu.make_async_copy(src, dst, small_sem.at[i])
        for i, (src, dst) in enumerate(
            (
                (lines_hbm, lines_ref),
                (sx_hbm, sx_ref),
                (sy_hbm, sy_ref),
                (defocus_hbm, defocus_ref),
                (weights_hbm, weights_ref),
            )
        )
    ]
    for load in small:
        load.start()
    loads = []
    for j in range(2):
        cols = pl.ds(j * 128, 128)
        loads.append(pltpu.make_async_copy(volume_hbm.at[:, :, cols], vbuf.at[j], in_sem.at[j]))
    for j in range(2):
        cols = pl.ds(j * 128, 128)
        loads.append(
            pltpu.make_async_copy(images_hbm.at[:, :, :, cols], ibuf.at[j], in_sem.at[2 + j])
        )
    for load in loads:
        load.start()

    barrier = pltpu.get_barrier_semaphore()

    def slab_peer(k):
        return dom, lax.rem(slab + k, SLABS)

    def x_peer(k):
        to = lax.rem(x + k, 4)
        return (to % 2) * 16 + zc, y * 2 + to // 2

    def y_peer(k):
        return dom, lax.rem(y + k, YS) * 2 + x_hi

    def z_peer(k):
        return x_lo * 16 + lax.rem(z + k, ZS) * 2 + c, slab

    def group_peer(k):
        to = lax.rem(x_lo * 2 + c + k, 4)
        return (to // 2) * 16 + z * 2 + to % 2, slab

    def greet(peer):
        pl.semaphore_signal(barrier, inc=1, device_id=peer, device_id_type=MESH)

    def greet_slab(k, carry):
        greet(slab_peer(k))
        return carry

    def greet_z(k, carry):
        greet(z_peer(k))
        return carry

    lax.fori_loop(1, SLABS, greet_slab, 0)
    lax.fori_loop(1, ZS, greet_z, 0)
    for k in range(1, 4):
        greet(group_peer(k))
    greet(((1 - x_lo) * 16 + zc, y * 2 + 1 - x_hi))

    small[0].wait()
    lines = lines_ref[...]
    owner = lines >> 10
    local = (lines & (LINES - 1)).astype(F32)
    slab_rows = iota((SLABS, KS), 0)
    marks = jnp.concatenate(
        [(owner[o : o + 1] == slab_rows).astype(F32) for o in range(ORIENT)], 0
    )
    before = (iota((KS, KS), 0) < iota((KS, KS), 1)).astype(F32).astype(BF16)
    earlier = dot(marks.astype(BF16), before) * marks
    ranks = [
        jnp.sum(earlier[o * SLABS : (o + 1) * SLABS], axis=0, keepdims=True).astype(jnp.int32)
        for o in range(ORIENT)
    ]
    own_line = []
    for o in range(ORIENT):
        mine = (owner[o : o + 1] == slab) & (ranks[o] == slab_rows)
        own_line.append(
            jnp.sum(jnp.where(mine, local[o : o + 1], 0.0), axis=1, keepdims=True)
        )
    own_line = jnp.concatenate(own_line, 0).astype(jnp.int32)
    half_line = jnp.where(c == 0, own_line[0 : 2 * OWNED], own_line[2 * OWNED :])
    column = iota((2 * OWNED, 2 * LINES), 1)
    gather[0 : 2 * OWNED] = (column == 2 * half_line).astype(F32).astype(BF16)
    gather[2 * OWNED :] = (column == 2 * half_line + 1).astype(F32).astype(BF16)

    for j in range(2):
        loads[j].wait()
        picked = dot(gather[...], vbuf.at[j].reshape(2 * LINES, 128)[...]).astype(BF16)
        for part in range(2):
            at = slice(part * KS + j * 128, part * KS + j * 128 + 128)
            own[:, at] = picked[part * 32 : part * 32 + 32]

    pl.semaphore_wait(barrier, SLABS - 1 + ZS - 1 + 3 + 1)

    def slab_copy(k):
        return pltpu.make_async_remote_copy(
            src_ref=own,
            dst_ref=arrived.at[c, slab],
            send_sem=s_send.at[0],
            recv_sem=s_recv.at[0],
            device_id=slab_peer(k),
            device_id_type=MESH,
        )

    def send_slab(k, carry):
        slab_copy(k).start()
        return carry

    lax.fori_loop(1, SLABS, send_slab, 0)
    arrived[c, slab] = own[...]

    small[1].wait()
    small[2].wait()
    lane = iota((8, 128), 1) % NT
    row_x = jnp.zeros((8, 128), jnp.int32)
    row_y = jnp.zeros((8, 128), jnp.int32)
    for t in range(NT):
        row_x = jnp.where(lane == t, sx_ref[t], row_x)
        row_y = jnp.where(lane == t, sy_ref[t], row_y)
    freq = iota((KS, 128), 0) - HALF
    sin_x, cos_x = turns_sin_cos(freq * row_x[0:1])
    sin_y, cos_y = turns_sin_cos(freq * row_y[0:1])
    wide_lane = iota((KS, 128), 1)
    ephase[0:KS] = jnp.where(wide_lane < NT, cos_y, -sin_y)[:, : 2 * NT].astype(BF16)
    ephase[KS:] = jnp.where(wide_lane < NT, sin_y, cos_y)[:, : 2 * NT].astype(BF16)
    t_cos = cos_x.T[0:NT]
    t_sin = sin_x.T[0:NT]
    table = jnp.concatenate([t_cos, t_sin], 1)
    table_hi = table.astype(BF16)
    table_lo = (table - table_hi.astype(F32)).astype(BF16)
    small[4].wait()
    weights = weights_ref[...]
    weights_hi = weights.astype(BF16)
    weights_lo = (weights - weights_hi.astype(F32)).astype(BF16)
    h = dot(weights_hi, table_hi) + dot(weights_lo, table_hi) + dot(weights_hi, table_lo)
    h = h.astype(BF16).reshape(P_DEV * ORIENT, NT, 2 * KS)
    hs[:, 0:NT] = h[:, :, 0:KS]
    hs[:, NT:] = h[:, :, KS:]
    for o in range(ORIENT):
        rank = ranks[o]
        row = owner[o : o + 1]
        at_t = (row & 1) * 128 + (rank >> 3) * 64 + (row >> 1) * 8 + (rank & 7)
        place_t[o] = (iota((KS, KS), 0) == at_t).astype(F32).astype(BF16)

    freq_row = (iota((8, KS), 1) - HALF).astype(F32)
    which = iota((8, KS), 0)
    focus = jnp.zeros((8, KS), F32)
    small[3].wait()
    for p in range(P_DEV):
        focus = jnp.where(which == p, defocus_ref[p], focus)
    sin_d, cos_d = angle_sin_cos(focus * (freq_row * freq_row * (1.0 / (HALF * HALF))))
    sin_col = sin_d.T
    cos_col = cos_d.T
    u_row = 0.1 * sin_d - 0.995 * cos_d
    v_row = -0.995 * sin_d - 0.1 * cos_d
    loads[2].wait()
    loads[3].wait()
    for p in range(P_DEV):
        for j in range(2):
            at = slice(j * 128, j * 128 + 128)
            split[...] = ibuf.at[j, p].reshape(2 * KS, 128)[...].astype(F32)
            ctf = (
                sin_col[:, p : p + 1] * u_row[p : p + 1, at]
                + cos_col[:, p : p + 1] * v_row[p : p + 1, at]
            )
            cx[p, 0, :, at] = ctf * split[pl.ds(0, KS, stride=2), :]
            cx[p, 1, :, at] = ctf * split[pl.ds(1, KS, stride=2), :]

    def placed_term(o):
        for block in range(2):
            at = slice(block * 128, block * 128 + 128)
            low = slice(KS + block * 128, KS + block * 128 + 128)
            t_re = None
            for p in range(P_DEV):
                table_h = hs[p * ORIENT + o]
                g_re = dot(ephase[at], table_h)
                g_im = dot(ephase[low], table_h)
                c_re = cx[p, 0, at]
                c_im = cx[p, 1, at]
                if t_re is None:
                    t_re = c_re * g_re - c_im * g_im
                    t_im = c_re * g_im + c_im * g_re
                else:
                    t_re += c_re * g_re - c_im * g_im
                    t_im += c_re * g_im + c_im * g_re
            term[at, 0:KS] = t_re.astype(BF16)
            term[at, KS:] = t_im.astype(BF16)
        return dot(place_t[o], term[...])

    def pair_copy(j):
        return pltpu.make_async_remote_copy(
            src_ref=sent.at[j],
            dst_ref=landed.at[j],
            send_sem=p_send.at[j],
            recv_sem=p_recv.at[j],
            device_id=partner,
            device_id_type=MESH,
        )

    def x_copy(j, k):
        return pltpu.make_async_remote_copy(
            src_ref=xsend.at[j, lax.rem(x + k, 4)],
            dst_ref=xrecv.at[j, x],
            send_sem=x_send.at[j],
            recv_sem=x_recv.at[j],
            device_id=x_peer(k),
            device_id_type=MESH,
        )

    def y_copy(j, k):
        return pltpu.make_async_remote_copy(
            src_ref=ysend.at[j, lax.rem(y + k, YS)],
            dst_ref=yrecv.at[j, y],
            send_sem=y_send.at[0],
            recv_sem=y_recv.at[0],
            device_id=y_peer(k),
            device_id_type=MESH,
        )

    def z_copy(k):
        return pltpu.make_async_remote_copy(
            src_ref=zsend,
            dst_ref=zrecv.at[z],
            send_sem=z_send.at[0],
            recv_sem=z_recv.at[0],
            device_id=z_peer(k),
            device_id_type=MESH,
        )

    def give(j, carry):
        sent[j] = placed_term(2 * (1 - c) + j).astype(BF16)
        pair_copy(j).start()
        return carry

    lax.fori_loop(0, 2, give, 0)

    def keep(j, carry):
        mine = placed_term(2 * c + j)
        pair_copy(j).wait_recv()
        both = (mine + landed[j].astype(F32)).astype(BF16)
        xsend[j] = both.reshape(4, 64, 2 * KS)

        def send_x(k, inner):
            x_copy(j, k).start()
            return inner

        lax.fori_loop(1, 4, send_x, 0)
        xrecv[j, x] = xsend[j, x]
        return carry

    lax.fori_loop(0, 2, keep, 0)

    for o in range(ORIENT):
        at_s = owner[o : o + 1] * OWNED + ranks[o]
        place_s[o] = (iota((KS, KS), 0) == at_s).astype(F32).astype(BF16)
    group = wide_lane // NT
    for o in range(ORIENT):
        cos_o = jnp.where(group == o, cos_x, 0.0).astype(BF16)
        sin_o = jnp.where(group == o, sin_x, 0.0).astype(BF16)
        fx[o, 0:KS, 0:128] = cos_o
        fx[o, 0:KS, 128:] = -sin_o
        fx[o, KS:, 0:128] = sin_o
        fx[o, KS:, 128:] = cos_o
    table_y = jnp.concatenate([cos_y.T[0:NT], sin_y.T[0:NT]], 1) * (1.0 / KS)
    fy_hi = table_y.astype(BF16)
    fy[0:NT] = fy_hi
    fy[NT:] = (table_y - fy_hi.astype(F32)).astype(BF16)

    def correlate(half, first):
        for j in range(2):
            o = 2 * half + j
            rows_s = arrived[half, :, j * OWNED : (j + 1) * OWNED, :].reshape(KS, 2 * KS)
            su[...] = dot_t(place_s[o], rows_s)
            for block in range(2):
                at = slice(block * 128, block * 128 + 128)
                for p in range(P_DEV):
                    s_re = su[at, 0:KS]
                    s_im = su[at, KS:]
                    c_re = cx[p, 0, at]
                    c_im = cx[p, 1, at]
                    q_re = (s_re * c_re + s_im * c_im).astype(BF16)
                    q_im = (s_re * c_im - s_im * c_re).astype(BF16)
                    part = dot(q_re, fx[o, 0:KS]) + dot(q_im, fx[o, KS:])
                    if first and j == 0:
                        zacc[p, at] = part
                    else:
                        zacc[p, at] += part

    line_row = jnp.concatenate([2 * own_line, 2 * own_line + 1], 0).astype(F32)
    line_row = jnp.broadcast_to(line_row, (128, 128)).T[0:1].astype(jnp.int32)
    insert[...] = (iota((2 * LINES, 128), 0) == line_row).astype(F32).astype(BF16)
    def pass_on(j, carry):
        pltpu.make_async_copy(
            xrecv.at[j, pl.ds(0, 3)], xrecv.at[j, pl.ds(0, 3)], x_recv.at[j]
        ).wait()
        for part in range(2):
            at = slice(part * KS, part * KS + KS)
            total = xrecv[j, 0, :, at].astype(F32)
            for other in range(1, 4):
                total += xrecv[j, other, :, at].astype(F32)
            tile_y[:, part * 8 : part * 8 + 8] = total.reshape(YS, 8, KS)
        ysend[j] = tile_y[...].astype(BF16)

        def send_y(k, inner):
            y_copy(j, k).start()
            return inner

        lax.fori_loop(1, YS, send_y, 0)
        yrecv[j, y] = ysend[j, y]
        return carry

    lax.fori_loop(0, 2, pass_on, 0)
    pltpu.make_async_copy(
        arrived.at[0, pl.ds(0, SLABS - 1)], arrived.at[0, pl.ds(0, SLABS - 1)], s_recv.at[0]
    ).wait()
    forward = pltpu.make_async_remote_copy(
        src_ref=arrived.at[c],
        dst_ref=arrived.at[c],
        send_sem=s_send.at[1],
        recv_sem=s_recv.at[1],
        device_id=partner,
        device_id_type=MESH,
    )
    forward.start()
    correlate(c, True)

    pltpu.make_async_copy(
        yrecv.at[:, pl.ds(0, YS - 1)], yrecv.at[:, pl.ds(0, YS - 1)], y_recv.at[0]
    ).wait()
    for j in range(2):
        total = yrecv[j, 0].astype(F32)
        for other in range(1, YS):
            total += yrecv[j, other].astype(F32)
        zsend[j] = total.astype(BF16)

    def send_z(k, carry):
        z_copy(k).start()
        return carry

    lax.fori_loop(1, ZS, send_z, 0)
    zrecv[z] = zsend[...]
    forward.wait_recv()
    correlate(1 - c, False)

    pltpu.make_async_copy(zrecv.at[pl.ds(0, ZS - 1)], zrecv.at[pl.ds(0, ZS - 1)], z_recv.at[0]).wait()
    total = zrecv[0].astype(F32)
    for other in range(1, ZS):
        total += zrecv[other].astype(F32)
    place = x_lo * 2 + c
    fin[place] = (total * SCALE).astype(BF16)

    def group_copy(k):
        return pltpu.make_async_remote_copy(
            src_ref=fin.at[place],
            dst_ref=fin.at[place],
            send_sem=f_send.at[0],
            recv_sem=f_recv.at[0],
            device_id=group_peer(k),
            device_id_type=MESH,
        )

    for k in range(1, 4):
        group_copy(k).start()
    for p in range(P_DEV):
        full = jnp.concatenate([zacc[p, :, 0:128], zacc[p, :, 128:]], 0)
        full_hi = full.astype(BF16)
        full_lo = (full - full_hi.astype(F32)).astype(BF16)
        both = dot(fy[...], full_hi)
        scores_ref[p] = both[0:NT] + both[NT:] + dot(fy[0:NT], full_lo)

    pltpu.make_async_copy(fin.at[pl.ds(0, 3)], fin.at[pl.ds(0, 3)], f_recv.at[0]).wait()

    for o in range(ORIENT):
        for r in range(2):
            got = fin[r * 2 + o // 2, o % 2].astype(F32)
            for part in range(2):
                first = part * 64 + o * OWNED + r * 8
                rows[first : first + 8] = got[part * 8 : part * 8 + 8]
    rows_bf16 = rows[...].astype(BF16)
    placed = dot(insert[...], rows_bf16).astype(BF16)
    outs = []
    for j in range(2):
        vbuf.at[j].reshape(2 * LINES, 128)[...] = placed[:, j * 128 : j * 128 + 128]
        outs.append(
            pltpu.make_async_copy(
                vbuf.at[j], update_hbm.at[:, :, pl.ds(j * 128, 128)], out_sem.at[j]
            )
        )
        outs[j].start()

    pltpu.make_async_copy(
        arrived.at[0, pl.ds(0, SLABS - 1)], arrived.at[0, pl.ds(0, SLABS - 1)], s_send.at[0]
    ).wait()
    forward.wait_send()
    for j in range(2):
        pair_copy(j).wait_send()
    for j in range(2):
        pltpu.make_async_copy(
            xrecv.at[j, pl.ds(0, 3)], xrecv.at[j, pl.ds(0, 3)], x_send.at[j]
        ).wait()
    pltpu.make_async_copy(
        yrecv.at[:, pl.ds(0, YS - 1)], yrecv.at[:, pl.ds(0, YS - 1)], y_send.at[0]
    ).wait()
    pltpu.make_async_copy(zrecv.at[pl.ds(0, ZS - 1)], zrecv.at[pl.ds(0, ZS - 1)], z_send.at[0]).wait()
    pltpu.make_async_copy(fin.at[pl.ds(0, 3)], fin.at[pl.ds(0, 3)], f_send.at[0]).wait()
    for out in outs:
        out.wait()


def body(volume, images, defocus, soft_weights, slice_lines, shift_y, shift_x):
    vmem = pl.BlockSpec(memory_space=pltpu.VMEM)
    hbm = pl.BlockSpec(memory_space=pltpu.HBM)
    dma = pltpu.SemaphoreType.DMA
    scores, line_update = pl.pallas_call(
        kernel,
        out_shape=(
            jax.ShapeDtypeStruct((P_DEV, NT, ORIENT * NT), F32),
            jax.ShapeDtypeStruct((LINES, 2, KS), BF16),
        ),
        in_specs=[hbm] * 7,
        out_specs=(vmem, hbm),
        scratch_shapes=[
            pltpu.VMEM((ORIENT, KS), jnp.int32),
            pltpu.VMEM((P_DEV * ORIENT * NT, NT), F32),
            pltpu.SMEM((P_DEV,), F32),
            pltpu.SMEM((NT,), jnp.int32),
            pltpu.SMEM((NT,), jnp.int32),
            pltpu.VMEM((2, LINES, 2, 128), BF16),
            pltpu.VMEM((2, P_DEV, KS, 2, 128), BF16),
            pltpu.VMEM((2 * KS, 128), F32),
            pltpu.VMEM((2 * OWNED, 2 * KS), BF16),
            pltpu.VMEM((2, SLABS, 2 * OWNED, 2 * KS), BF16),
            pltpu.VMEM((4 * OWNED, 2 * LINES), BF16),
            pltpu.VMEM((2 * LINES, 2 * ORIENT * OWNED), BF16),
            pltpu.VMEM((ORIENT, KS, KS), BF16),
            pltpu.VMEM((ORIENT, KS, KS), BF16),
            pltpu.VMEM((ORIENT, 2 * KS, 256), BF16),
            pltpu.VMEM((2 * KS, 2 * NT), BF16),
            pltpu.VMEM((2 * NT, 2 * KS), BF16),
            pltpu.VMEM((P_DEV * ORIENT, 2 * NT, KS), BF16),
            pltpu.VMEM((P_DEV, 2, KS, KS), F32),
            pltpu.VMEM((KS, 2 * KS), BF16),
            pltpu.VMEM((2, KS, 2 * KS), BF16),
            pltpu.VMEM((2, KS, 2 * KS), BF16),
            pltpu.VMEM((2, 4, 64, 2 * KS), BF16),
            pltpu.VMEM((2, 4, 64, 2 * KS), BF16),
            pltpu.VMEM((2, YS, 16, KS), BF16),
            pltpu.VMEM((2, YS, 16, KS), BF16),
            pltpu.VMEM((2, 16, KS), BF16),
            pltpu.VMEM((ZS, 2, 16, KS), BF16),
            pltpu.VMEM((4, 2, 16, KS), BF16),
            pltpu.VMEM((YS, 16, KS), F32),
            pltpu.VMEM((2 * ORIENT * OWNED, KS), F32),
            pltpu.VMEM((P_DEV, KS, 256), F32),
            pltpu.VMEM((KS, 2 * KS), F32),
            dma((5,)),
            dma((4,)),
            dma((2,)),
            dma((2,)),
            dma((2,)),
            dma((2,)),
            dma((2,)),
            dma((2,)),
            dma((2,)),
            dma((1,)),
            dma((1,)),
            dma((1,)),
            dma((1,)),
            dma((1,)),
            dma((1,)),
        ],
        compiler_params=pltpu.CompilerParams(
            collective_id=0, has_side_effects=True, vmem_limit_bytes=48 * 1024 * 1024
        ),
        name="cryo",
    )(
        slice_lines,
        soft_weights.reshape(P_DEV * ORIENT * NT, NT),
        defocus,
        shift_y,
        shift_x,
        volume,
        images,
    )
    scores = scores.reshape(P_DEV, NT, ORIENT, NT).transpose(0, 2, 1, 3)
    return scores, line_update


def solution(mesh):
    placed = (
        P("slab", None, None),
        P(("dom", "slab"), None, None, None),
        P(("dom", "slab")),
        P(("dom", "slab"), None, None, None),
        P(),
        P(),
        P(),
    )
    return jax.shard_map(
        body,
        mesh=mesh,
        in_specs=placed,
        out_specs=(P(("dom", "slab"), None, None, None), P("slab", None, None)),
        check_vma=False,
    )
```

```python
import math

import jax
import jax.numpy as jnp
from jax import lax
from jax.experimental import pallas as pl
from jax.experimental.pallas import tpu as pltpu
from jax.sharding import PartitionSpec as P

KS = 256
HALF = KS // 2
P_DEV = 4
LINES = 1024
ORIENT = 4
NT = 32
OWNED = 16
PARTICLES = 2048
SLABS = 16
ZS = 8
YS = 8
XLO = 2
SCALE = 1.0 / math.sqrt(NT * NT * PARTICLES)
F32 = jnp.float32
BF16 = jnp.bfloat16
MESH = pl.DeviceIdType.MESH


def dot(a, b):
    return jnp.dot(a, b, preferred_element_type=F32)


def dot_t(a, b):
    return lax.dot_general(a, b, (((0,), (0,)), ((), ())), preferred_element_type=F32)


def poly_sin_cos(r):
    s = r * r
    sin = r * (1.0 + s * (-1 / 6 + s * (1 / 120 + s * (-1 / 5040 + s * (1 / 362880)))))
    cos = 1.0 + s * (-0.5 + s * (1 / 24 + s * (-1 / 720 + s * (1 / 40320))))
    return sin, cos


def rotate(quadrant, sin, cos):
    q = quadrant & 3
    odd = (q & 1) == 1
    s = jnp.where(odd, cos, sin)
    c = jnp.where(odd, sin, cos)
    s = jnp.where(q >= 2, -s, s)
    c = jnp.where((q == 1) | (q == 2), -c, c)
    return s, c


def turns_sin_cos(turns):
    t = turns & (KS - 1)
    q = (t + KS // 8) >> 6
    r = (t - (q << 6)).astype(F32) * (2.0 * math.pi / KS)
    return rotate(q, *poly_sin_cos(r))


def angle_sin_cos(x):
    n = jnp.floor(x * (2.0 / math.pi) + 0.5)
    r = x - n * 1.5703125
    r = r - n * 4.837512969970703e-4
    r = r - n * 7.549789948768648e-8
    return rotate(n.astype(jnp.int32), *poly_sin_cos(r))


def iota(shape, dim):
    return lax.broadcasted_iota(jnp.int32, shape, dim)


def kernel(
    lines_hbm, weights_hbm, defocus_hbm, sy_hbm, sx_hbm, volume_hbm, images_hbm,
    scores_ref, update_hbm,
    lines_ref, weights_ref, defocus_ref, sy_ref, sx_ref,
    vbuf, ibuf, split, own, arrived, gather, insert, place_s, place_t,
    fx, ephase, fy, hs, cx, term, sent, landed, xsend, xrecv, ysend, yrecv, zsend, zrecv,
    fin, tile_y, rows, zacc, su,
    small_sem, in_sem, out_sem, s_send, s_recv, p_send, p_recv, x_send, x_recv, z_send, z_recv,
    y_send, y_recv, f_send, f_recv,
):
    dom = lax.axis_index("dom")
    slab = lax.axis_index("slab")
    x_lo = dom // 16
    z = (dom // 2) % 8
    c = dom % 2
    zc = z * 2 + c
    partner = (dom + 1 - 2 * c, slab)
    y = slab // 2
    x_hi = slab % 2
    x = x_hi * 2 + x_lo

    small = [
        pltpu.make_async_copy(src, dst, small_sem.at[i])
        for i, (src, dst) in enumerate(
            (
                (lines_hbm, lines_ref),
                (sx_hbm, sx_ref),
                (sy_hbm, sy_ref),
                (defocus_hbm, defocus_ref),
                (weights_hbm, weights_ref),
            )
        )
    ]
    for load in small:
        load.start()
    loads = []
    for j in range(2):
        cols = pl.ds(j * 128, 128)
        loads.append(pltpu.make_async_copy(volume_hbm.at[:, :, cols], vbuf.at[j], in_sem.at[j]))
    for j in range(2):
        cols = pl.ds(j * 128, 128)
        loads.append(
            pltpu.make_async_copy(images_hbm.at[:, :, :, cols], ibuf.at[j], in_sem.at[2 + j])
        )
    for load in loads:
        load.start()

    barrier = pltpu.get_barrier_semaphore()

    def slab_peer(k):
        to = lax.rem(slab + k, SLABS)
        flip = (to % 2 + x_hi) % 2
        return ((x_lo + flip) % 2) * 16 + zc, to

    def x_peer(k):
        to = lax.rem(x + k, 4)
        return (to % 2) * 16 + zc, y * 2 + to // 2

    def y_peer(k):
        return dom, lax.rem(y + k, YS) * 2 + x_hi

    def z_peer(k):
        return x_lo * 16 + lax.rem(z + k, ZS) * 2 + c, slab

    def group_peer(k):
        to = lax.rem(x_lo * 2 + c + k, 4)
        return (to // 2) * 16 + z * 2 + to % 2, slab

    def greet(peer):
        pl.semaphore_signal(barrier, inc=1, device_id=peer, device_id_type=MESH)

    def greet_slab(k, carry):
        greet(slab_peer(k))
        return carry

    def greet_z(k, carry):
        greet(z_peer(k))
        return carry

    lax.fori_loop(1, SLABS, greet_slab, 0)
    lax.fori_loop(1, ZS, greet_z, 0)
    for k in range(1, 4):
        greet(group_peer(k))
    greet((dom, y * 2 + 1 - x_hi))

    small[0].wait()
    lines = lines_ref[...]
    owner = lines >> 10
    local = (lines & (LINES - 1)).astype(F32)
    slab_rows = iota((SLABS, KS), 0)
    marks = jnp.concatenate(
        [(owner[o : o + 1] == slab_rows).astype(F32) for o in range(ORIENT)], 0
    )
    before = (iota((KS, KS), 0) < iota((KS, KS), 1)).astype(F32).astype(BF16)
    earlier = dot(marks.astype(BF16), before) * marks
    ranks = [
        jnp.sum(earlier[o * SLABS : (o + 1) * SLABS], axis=0, keepdims=True).astype(jnp.int32)
        for o in range(ORIENT)
    ]
    own_line = []
    for o in range(ORIENT):
        mine = (owner[o : o + 1] == slab) & (ranks[o] == slab_rows)
        own_line.append(
            jnp.sum(jnp.where(mine, local[o : o + 1], 0.0), axis=1, keepdims=True)
        )
    own_line = jnp.concatenate(own_line, 0).astype(jnp.int32)
    half_line = jnp.where(c == 0, own_line[0 : 2 * OWNED], own_line[2 * OWNED :])
    column = iota((2 * OWNED, 2 * LINES), 1)
    gather[0 : 2 * OWNED] = (column == 2 * half_line).astype(F32).astype(BF16)
    gather[2 * OWNED :] = (column == 2 * half_line + 1).astype(F32).astype(BF16)

    for j in range(2):
        loads[j].wait()
        picked = dot(gather[...], vbuf.at[j].reshape(2 * LINES, 128)[...]).astype(BF16)
        for part in range(2):
            at = slice(part * KS + j * 128, part * KS + j * 128 + 128)
            own[:, at] = picked[part * 32 : part * 32 + 32]

    pl.semaphore_wait(barrier, SLABS - 1 + ZS - 1 + 3 + 1)

    def slab_copy(k):
        return pltpu.make_async_remote_copy(
            src_ref=own,
            dst_ref=arrived.at[c, slab],
            send_sem=s_send.at[0],
            recv_sem=s_recv.at[0],
            device_id=slab_peer(k),
            device_id_type=MESH,
        )

    def send_slab(k, carry):
        slab_copy(k).start()
        return carry

    lax.fori_loop(1, SLABS, send_slab, 0)
    arrived[c, slab] = own[...]

    small[1].wait()
    small[2].wait()
    lane = iota((8, 128), 1) % NT
    row_x = jnp.zeros((8, 128), jnp.int32)
    row_y = jnp.zeros((8, 128), jnp.int32)
    for t in range(NT):
        row_x = jnp.where(lane == t, sx_ref[t], row_x)
        row_y = jnp.where(lane == t, sy_ref[t], row_y)
    freq = iota((KS, 128), 0) - HALF
    sin_x, cos_x = turns_sin_cos(freq * row_x[0:1])
    sin_y, cos_y = turns_sin_cos(freq * row_y[0:1])
    wide_lane = iota((KS, 128), 1)
    ephase[0:KS] = jnp.where(wide_lane < NT, cos_y, -sin_y)[:, : 2 * NT].astype(BF16)
    ephase[KS:] = jnp.where(wide_lane < NT, sin_y, cos_y)[:, : 2 * NT].astype(BF16)
    t_cos = cos_x.T[0:NT]
    t_sin = sin_x.T[0:NT]
    table = jnp.concatenate([t_cos, t_sin], 1)
    table_hi = table.astype(BF16)
    table_lo = (table - table_hi.astype(F32)).astype(BF16)
    small[4].wait()
    weights = weights_ref[...]
    weights_hi = weights.astype(BF16)
    weights_lo = (weights - weights_hi.astype(F32)).astype(BF16)
    h = dot(weights_hi, table_hi) + dot(weights_lo, table_hi) + dot(weights_hi, table_lo)
    h = h.astype(BF16).reshape(P_DEV * ORIENT, NT, 2 * KS)
    hs[:, 0:NT] = h[:, :, 0:KS]
    hs[:, NT:] = h[:, :, KS:]
    for o in range(ORIENT):
        rank = ranks[o]
        row = owner[o : o + 1]
        at_t = (row & 1) * 128 + (rank >> 3) * 64 + (row >> 1) * 8 + (rank & 7)
        place_t[o] = (iota((KS, KS), 0) == at_t).astype(F32).astype(BF16)

    freq_row = (iota((8, KS), 1) - HALF).astype(F32)
    which = iota((8, KS), 0)
    focus = jnp.zeros((8, KS), F32)
    small[3].wait()
    for p in range(P_DEV):
        focus = jnp.where(which == p, defocus_ref[p], focus)
    sin_d, cos_d = angle_sin_cos(focus * (freq_row * freq_row * (1.0 / (HALF * HALF))))
    sin_col = sin_d.T
    cos_col = cos_d.T
    u_row = 0.1 * sin_d - 0.995 * cos_d
    v_row = -0.995 * sin_d - 0.1 * cos_d
    loads[2].wait()
    loads[3].wait()
    for p in range(P_DEV):
        for j in range(2):
            at = slice(j * 128, j * 128 + 128)
            split[...] = ibuf.at[j, p].reshape(2 * KS, 128)[...].astype(F32)
            ctf = (
                sin_col[:, p : p + 1] * u_row[p : p + 1, at]
                + cos_col[:, p : p + 1] * v_row[p : p + 1, at]
            )
            cx[p, 0, :, at] = ctf * split[pl.ds(0, KS, stride=2), :]
            cx[p, 1, :, at] = ctf * split[pl.ds(1, KS, stride=2), :]

    def placed_term(o):
        for block in range(2):
            at = slice(block * 128, block * 128 + 128)
            low = slice(KS + block * 128, KS + block * 128 + 128)
            t_re = None
            for p in range(P_DEV):
                table_h = hs[p * ORIENT + o]
                g_re = dot(ephase[at], table_h)
                g_im = dot(ephase[low], table_h)
                c_re = cx[p, 0, at]
                c_im = cx[p, 1, at]
                if t_re is None:
                    t_re = c_re * g_re - c_im * g_im
                    t_im = c_re * g_im + c_im * g_re
                else:
                    t_re += c_re * g_re - c_im * g_im
                    t_im += c_re * g_im + c_im * g_re
            term[at, 0:KS] = t_re.astype(BF16)
            term[at, KS:] = t_im.astype(BF16)
        return dot(place_t[o], term[...])

    def pair_copy(j):
        return pltpu.make_async_remote_copy(
            src_ref=sent.at[j],
            dst_ref=landed.at[j],
            send_sem=p_send.at[j],
            recv_sem=p_recv.at[j],
            device_id=partner,
            device_id_type=MESH,
        )

    def x_copy(j, k):
        return pltpu.make_async_remote_copy(
            src_ref=xsend.at[j, lax.rem(x + k, 4)],
            dst_ref=xrecv.at[j, x],
            send_sem=x_send.at[j],
            recv_sem=x_recv.at[j],
            device_id=x_peer(k),
            device_id_type=MESH,
        )

    def y_copy(j, k):
        return pltpu.make_async_remote_copy(
            src_ref=ysend.at[j, lax.rem(y + k, YS)],
            dst_ref=yrecv.at[j, y],
            send_sem=y_send.at[0],
            recv_sem=y_recv.at[0],
            device_id=y_peer(k),
            device_id_type=MESH,
        )

    def z_copy(k):
        return pltpu.make_async_remote_copy(
            src_ref=zsend,
            dst_ref=zrecv.at[z],
            send_sem=z_send.at[0],
            recv_sem=z_recv.at[0],
            device_id=z_peer(k),
            device_id_type=MESH,
        )

    def give(j, carry):
        sent[j] = placed_term(2 * (1 - c) + j).astype(BF16)
        pair_copy(j).start()
        return carry

    lax.fori_loop(0, 2, give, 0)

    def keep(j, carry):
        mine = placed_term(2 * c + j)
        pair_copy(j).wait_recv()
        both = (mine + landed[j].astype(F32)).astype(BF16)
        xsend[j] = both.reshape(4, 64, 2 * KS)

        def send_x(k, inner):
            x_copy(j, k).start()
            return inner

        lax.fori_loop(1, 4, send_x, 0)
        xrecv[j, x] = xsend[j, x]
        return carry

    lax.fori_loop(0, 2, keep, 0)

    for o in range(ORIENT):
        at_s = owner[o : o + 1] * OWNED + ranks[o]
        place_s[o] = (iota((KS, KS), 0) == at_s).astype(F32).astype(BF16)
    group = wide_lane // NT
    for o in range(ORIENT):
        cos_o = jnp.where(group == o, cos_x, 0.0).astype(BF16)
        sin_o = jnp.where(group == o, sin_x, 0.0).astype(BF16)
        at = (o % 2) * 2 * KS
        fx[o // 2, at : at + KS, 0:128] = cos_o
        fx[o // 2, at : at + KS, 128:] = -sin_o
        fx[o // 2, at + KS : at + 2 * KS, 0:128] = sin_o
        fx[o // 2, at + KS : at + 2 * KS, 128:] = cos_o
    table_y = jnp.concatenate([cos_y.T[0:NT], sin_y.T[0:NT]], 1) * (1.0 / KS)
    fy_hi = table_y.astype(BF16)
    fy[0:NT] = fy_hi
    fy[NT:] = (table_y - fy_hi.astype(F32)).astype(BF16)

    def correlate(half, first):
        for j in range(2):
            rows_s = arrived[half, :, j * OWNED : (j + 1) * OWNED, :].reshape(KS, 2 * KS)
            su[j] = dot_t(place_s[2 * half + j], rows_s)
        for block in range(2):
            at = slice(block * 128, block * 128 + 128)
            for p in range(P_DEV):
                c_re = cx[p, 0, at]
                c_im = cx[p, 1, at]
                q = []
                for j in range(2):
                    s_re = su[j, at, 0:KS]
                    s_im = su[j, at, KS:]
                    q.append((s_re * c_re + s_im * c_im).astype(BF16))
                    q.append((s_re * c_im - s_im * c_re).astype(BF16))
                part = dot(jnp.concatenate(q, 1), fx[half])
                if first:
                    zacc[p, at] = part
                else:
                    zacc[p, at] += part

    line_row = jnp.concatenate([2 * own_line, 2 * own_line + 1], 0).astype(F32)
    line_row = jnp.broadcast_to(line_row, (128, 128)).T[0:1].astype(jnp.int32)
    insert[...] = (iota((2 * LINES, 128), 0) == line_row).astype(F32).astype(BF16)
    def pass_on(j, carry):
        pltpu.make_async_copy(
            xrecv.at[j, pl.ds(0, 3)], xrecv.at[j, pl.ds(0, 3)], x_recv.at[j]
        ).wait()
        for part in range(2):
            at = slice(part * KS, part * KS + KS)
            total = xrecv[j, 0, :, at].astype(F32)
            for other in range(1, 4):
                total += xrecv[j, other, :, at].astype(F32)
            tile_y[:, part * 8 : part * 8 + 8] = total.reshape(YS, 8, KS)
        ysend[j] = tile_y[...].astype(BF16)

        def send_y(k, inner):
            y_copy(j, k).start()
            return inner

        lax.fori_loop(1, YS, send_y, 0)
        yrecv[j, y] = ysend[j, y]
        return carry

    lax.fori_loop(0, 2, pass_on, 0)
    pltpu.make_async_copy(
        arrived.at[0, pl.ds(0, SLABS - 1)], arrived.at[0, pl.ds(0, SLABS - 1)], s_recv.at[0]
    ).wait()
    forward = pltpu.make_async_remote_copy(
        src_ref=arrived.at[c],
        dst_ref=arrived.at[c],
        send_sem=s_send.at[1],
        recv_sem=s_recv.at[1],
        device_id=partner,
        device_id_type=MESH,
    )
    forward.start()
    correlate(c, True)

    pltpu.make_async_copy(
        yrecv.at[:, pl.ds(0, YS - 1)], yrecv.at[:, pl.ds(0, YS - 1)], y_recv.at[0]
    ).wait()
    for j in range(2):
        total = yrecv[j, 0].astype(F32)
        for other in range(1, YS):
            total += yrecv[j, other].astype(F32)
        zsend[j] = total.astype(BF16)

    def send_z(k, carry):
        z_copy(k).start()
        return carry

    lax.fori_loop(1, ZS, send_z, 0)
    zrecv[z] = zsend[...]
    forward.wait_recv()
    correlate(1 - c, False)

    pltpu.make_async_copy(zrecv.at[pl.ds(0, ZS - 1)], zrecv.at[pl.ds(0, ZS - 1)], z_recv.at[0]).wait()
    total = zrecv[0].astype(F32)
    for other in range(1, ZS):
        total += zrecv[other].astype(F32)
    place = x_lo * 2 + c
    fin[place] = (total * SCALE).astype(BF16)

    def group_copy(k):
        return pltpu.make_async_remote_copy(
            src_ref=fin.at[place],
            dst_ref=fin.at[place],
            send_sem=f_send.at[0],
            recv_sem=f_recv.at[0],
            device_id=group_peer(k),
            device_id_type=MESH,
        )

    for k in range(1, 4):
        group_copy(k).start()
    for p in range(P_DEV):
        full = jnp.concatenate([zacc[p, :, 0:128], zacc[p, :, 128:]], 0)
        full_hi = full.astype(BF16)
        full_lo = (full - full_hi.astype(F32)).astype(BF16)
        both = dot(fy[...], full_hi)
        scores_ref[p] = both[0:NT] + both[NT:] + dot(fy[0:NT], full_lo)

    pltpu.make_async_copy(fin.at[pl.ds(0, 3)], fin.at[pl.ds(0, 3)], f_recv.at[0]).wait()

    for o in range(ORIENT):
        for r in range(2):
            got = fin[r * 2 + o // 2, o % 2].astype(F32)
            for part in range(2):
                first = part * 64 + o * OWNED + r * 8
                rows[first : first + 8] = got[part * 8 : part * 8 + 8]
    rows_bf16 = rows[...].astype(BF16)
    outs = []
    for piece in range(4):
        at = slice(piece * 512, piece * 512 + 512)
        of = pl.ds(piece * 256, 256)
        placed = dot(insert[at], rows_bf16).astype(BF16)
        for j in range(2):
            vbuf.at[j, of].reshape(512, 128)[...] = placed[:, j * 128 : j * 128 + 128]
            outs.append(
                pltpu.make_async_copy(
                    vbuf.at[j, of],
                    update_hbm.at[of, :, pl.ds(j * 128, 128)],
                    out_sem.at[piece * 2 + j],
                )
            )
            outs[-1].start()

    pltpu.make_async_copy(
        arrived.at[0, pl.ds(0, SLABS - 1)], arrived.at[0, pl.ds(0, SLABS - 1)], s_send.at[0]
    ).wait()
    forward.wait_send()
    for j in range(2):
        pair_copy(j).wait_send()
    for j in range(2):
        pltpu.make_async_copy(
            xrecv.at[j, pl.ds(0, 3)], xrecv.at[j, pl.ds(0, 3)], x_send.at[j]
        ).wait()
    pltpu.make_async_copy(
        yrecv.at[:, pl.ds(0, YS - 1)], yrecv.at[:, pl.ds(0, YS - 1)], y_send.at[0]
    ).wait()
    pltpu.make_async_copy(zrecv.at[pl.ds(0, ZS - 1)], zrecv.at[pl.ds(0, ZS - 1)], z_send.at[0]).wait()
    pltpu.make_async_copy(fin.at[pl.ds(0, 3)], fin.at[pl.ds(0, 3)], f_send.at[0]).wait()
    for out in outs:
        out.wait()


def body(volume, images, defocus, soft_weights, slice_lines, shift_y, shift_x):
    vmem = pl.BlockSpec(memory_space=pltpu.VMEM)
    hbm = pl.BlockSpec(memory_space=pltpu.HBM)
    dma = pltpu.SemaphoreType.DMA
    scores, line_update = pl.pallas_call(
        kernel,
        out_shape=(
            jax.ShapeDtypeStruct((P_DEV, NT, ORIENT * NT), F32),
            jax.ShapeDtypeStruct((LINES, 2, KS), BF16),
        ),
        in_specs=[hbm] * 7,
        out_specs=(vmem, hbm),
        scratch_shapes=[
            pltpu.VMEM((ORIENT, KS), jnp.int32),
            pltpu.VMEM((P_DEV * ORIENT * NT, NT), F32),
            pltpu.SMEM((P_DEV,), F32),
            pltpu.SMEM((NT,), jnp.int32),
            pltpu.SMEM((NT,), jnp.int32),
            pltpu.VMEM((2, LINES, 2, 128), BF16),
            pltpu.VMEM((2, P_DEV, KS, 2, 128), BF16),
            pltpu.VMEM((2 * KS, 128), F32),
            pltpu.VMEM((2 * OWNED, 2 * KS), BF16),
            pltpu.VMEM((2, SLABS, 2 * OWNED, 2 * KS), BF16),
            pltpu.VMEM((4 * OWNED, 2 * LINES), BF16),
            pltpu.VMEM((2 * LINES, 2 * ORIENT * OWNED), BF16),
            pltpu.VMEM((ORIENT, KS, KS), BF16),
            pltpu.VMEM((ORIENT, KS, KS), BF16),
            pltpu.VMEM((2, 4 * KS, 256), BF16),
            pltpu.VMEM((2 * KS, 2 * NT), BF16),
            pltpu.VMEM((2 * NT, 2 * KS), BF16),
            pltpu.VMEM((P_DEV * ORIENT, 2 * NT, KS), BF16),
            pltpu.VMEM((P_DEV, 2, KS, KS), F32),
            pltpu.VMEM((KS, 2 * KS), BF16),
            pltpu.VMEM((2, KS, 2 * KS), BF16),
            pltpu.VMEM((2, KS, 2 * KS), BF16),
            pltpu.VMEM((2, 4, 64, 2 * KS), BF16),
            pltpu.VMEM((2, 4, 64, 2 * KS), BF16),
            pltpu.VMEM((2, YS, 16, KS), BF16),
            pltpu.VMEM((2, YS, 16, KS), BF16),
            pltpu.VMEM((2, 16, KS), BF16),
            pltpu.VMEM((ZS, 2, 16, KS), BF16),
            pltpu.VMEM((4, 2, 16, KS), BF16),
            pltpu.VMEM((YS, 16, KS), F32),
            pltpu.VMEM((2 * ORIENT * OWNED, KS), F32),
            pltpu.VMEM((P_DEV, KS, 256), F32),
            pltpu.VMEM((2, KS, 2 * KS), F32),
            dma((5,)),
            dma((4,)),
            dma((8,)),
            dma((2,)),
            dma((2,)),
            dma((2,)),
            dma((2,)),
            dma((2,)),
            dma((2,)),
            dma((1,)),
            dma((1,)),
            dma((1,)),
            dma((1,)),
            dma((1,)),
            dma((1,)),
        ],
        compiler_params=pltpu.CompilerParams(
            collective_id=0, has_side_effects=True, vmem_limit_bytes=60 * 1024 * 1024
        ),
        name="cryo",
    )(
        slice_lines,
        soft_weights.reshape(P_DEV * ORIENT * NT, NT),
        defocus,
        shift_y,
        shift_x,
        volume,
        images,
    )
    scores = scores.reshape(P_DEV, NT, ORIENT, NT).transpose(0, 2, 1, 3)
    return scores, line_update


def solution(mesh):
    placed = (
        P("slab", None, None),
        P(("dom", "slab"), None, None, None),
        P(("dom", "slab")),
        P(("dom", "slab"), None, None, None),
        P(),
        P(),
        P(),
    )
    return jax.shard_map(
        body,
        mesh=mesh,
        in_specs=placed,
        out_specs=(P(("dom", "slab"), None, None, None), P("slab", None, None)),
        check_vma=False,
    )
```

```python
import math

import jax
import jax.numpy as jnp
from jax import lax
from jax.experimental import pallas as pl
from jax.experimental.pallas import tpu as pltpu
from jax.sharding import PartitionSpec as P

KS = 256
HALF = KS // 2
P_DEV = 4
LINES = 1024
ORIENT = 4
NT = 32
OWNED = 16
PARTICLES = 2048
SLABS = 16
ZS = 8
YS = 8
XLO = 2
SCALE = 1.0 / math.sqrt(NT * NT * PARTICLES)
F32 = jnp.float32
BF16 = jnp.bfloat16
MESH = pl.DeviceIdType.MESH


def dot(a, b):
    return jnp.dot(a, b, preferred_element_type=F32)


def dot_t(a, b):
    return lax.dot_general(a, b, (((0,), (0,)), ((), ())), preferred_element_type=F32)


def poly_sin_cos(r):
    s = r * r
    sin = r * (1.0 + s * (-1 / 6 + s * (1 / 120 + s * (-1 / 5040 + s * (1 / 362880)))))
    cos = 1.0 + s * (-0.5 + s * (1 / 24 + s * (-1 / 720 + s * (1 / 40320))))
    return sin, cos


def rotate(quadrant, sin, cos):
    q = quadrant & 3
    odd = (q & 1) == 1
    s = jnp.where(odd, cos, sin)
    c = jnp.where(odd, sin, cos)
    s = jnp.where(q >= 2, -s, s)
    c = jnp.where((q == 1) | (q == 2), -c, c)
    return s, c


def turns_sin_cos(turns):
    t = turns & (KS - 1)
    q = (t + KS // 8) >> 6
    r = (t - (q << 6)).astype(F32) * (2.0 * math.pi / KS)
    return rotate(q, *poly_sin_cos(r))


def angle_sin_cos(x):
    n = jnp.floor(x * (2.0 / math.pi) + 0.5)
    r = x - n * 1.5703125
    r = r - n * 4.837512969970703e-4
    r = r - n * 7.549789948768648e-8
    return rotate(n.astype(jnp.int32), *poly_sin_cos(r))


def iota(shape, dim):
    return lax.broadcasted_iota(jnp.int32, shape, dim)


def kernel(
    lines_hbm, weights_hbm, defocus_hbm, sy_hbm, sx_hbm, volume_hbm, images_hbm,
    scores_hbm, rows_hbm, line_hbm,
    scores_ref, line_ref, lines_ref, weights_ref, defocus_ref, sy_ref, sx_ref,
    vbuf, ibuf, split, own, arrived, gather, place_s, place_t,
    fx, ephase, fy, hs, cx, term, sent, landed, xsend, xrecv, ysend, yrecv, zsend, zrecv,
    fin, tile_y, zacc, su,
    small_sem, in_sem, out_sem, s_send, s_recv, p_send, p_recv, x_send, x_recv, z_send, z_recv,
    y_send, y_recv, f_send, f_recv,
):
    dom = lax.axis_index("dom")
    slab = lax.axis_index("slab")
    x_lo = dom // 16
    z = (dom // 2) % 8
    c = dom % 2
    zc = z * 2 + c
    partner = (dom + 1 - 2 * c, slab)
    y = slab // 2
    x_hi = slab % 2
    x = x_hi * 2 + x_lo

    small = [
        pltpu.make_async_copy(src, dst, small_sem.at[i])
        for i, (src, dst) in enumerate(
            (
                (lines_hbm, lines_ref),
                (sx_hbm, sx_ref),
                (sy_hbm, sy_ref),
                (defocus_hbm, defocus_ref),
                (weights_hbm, weights_ref),
            )
        )
    ]
    for load in small:
        load.start()
    loads = []
    for j in range(2):
        cols = pl.ds(j * 128, 128)
        loads.append(pltpu.make_async_copy(volume_hbm.at[:, :, cols], vbuf.at[j], in_sem.at[j]))
    for j in range(2):
        cols = pl.ds(j * 128, 128)
        loads.append(
            pltpu.make_async_copy(images_hbm.at[:, :, :, cols], ibuf.at[j], in_sem.at[2 + j])
        )
    for load in loads:
        load.start()

    barrier = pltpu.get_barrier_semaphore()

    def slab_peer(k):
        to = lax.rem(slab + k, SLABS)
        flip = (to % 2 + x_hi) % 2
        return ((x_lo + flip) % 2) * 16 + zc, to

    def x_peer(k):
        to = lax.rem(x + k, 4)
        return (to % 2) * 16 + zc, y * 2 + to // 2

    def y_peer(k):
        return dom, lax.rem(y + k, YS) * 2 + x_hi

    def z_peer(k):
        return x_lo * 16 + lax.rem(z + k, ZS) * 2 + c, slab

    def group_peer(k):
        to = lax.rem(x_lo * 2 + c + k, 4)
        return (to // 2) * 16 + z * 2 + to % 2, slab

    def greet(peer):
        pl.semaphore_signal(barrier, inc=1, device_id=peer, device_id_type=MESH)

    def greet_slab(k, carry):
        greet(slab_peer(k))
        return carry

    def greet_z(k, carry):
        greet(z_peer(k))
        return carry

    lax.fori_loop(1, SLABS, greet_slab, 0)
    lax.fori_loop(1, ZS, greet_z, 0)
    for k in range(1, 4):
        greet(group_peer(k))
    greet((dom, y * 2 + 1 - x_hi))

    small[0].wait()
    lines = lines_ref[...]
    owner = lines >> 10
    local = (lines & (LINES - 1)).astype(F32)
    slab_rows = iota((SLABS, KS), 0)
    marks = jnp.concatenate(
        [(owner[o : o + 1] == slab_rows).astype(F32) for o in range(ORIENT)], 0
    )
    before = (iota((KS, KS), 0) < iota((KS, KS), 1)).astype(F32).astype(BF16)
    earlier = dot(marks.astype(BF16), before) * marks
    ranks = [
        jnp.sum(earlier[o * SLABS : (o + 1) * SLABS], axis=0, keepdims=True).astype(jnp.int32)
        for o in range(ORIENT)
    ]
    own_line = []
    for o in range(ORIENT):
        mine = (owner[o : o + 1] == slab) & (ranks[o] == slab_rows)
        own_line.append(
            jnp.sum(jnp.where(mine, local[o : o + 1], 0.0), axis=1, keepdims=True)
        )
    own_line = jnp.concatenate(own_line, 0).astype(jnp.int32)
    half_line = jnp.where(c == 0, own_line[0 : 2 * OWNED], own_line[2 * OWNED :])
    column = iota((2 * OWNED, 2 * LINES), 1)
    gather[0 : 2 * OWNED] = (column == 2 * half_line).astype(F32).astype(BF16)
    gather[2 * OWNED :] = (column == 2 * half_line + 1).astype(F32).astype(BF16)

    for j in range(2):
        loads[j].wait()
        picked = dot(gather[...], vbuf.at[j].reshape(2 * LINES, 128)[...]).astype(BF16)
        for part in range(2):
            at = slice(part * KS + j * 128, part * KS + j * 128 + 128)
            own[:, at] = picked[part * 32 : part * 32 + 32]

    pl.semaphore_wait(barrier, SLABS - 1 + ZS - 1 + 3 + 1)

    def slab_copy(k):
        return pltpu.make_async_remote_copy(
            src_ref=own,
            dst_ref=arrived.at[c, slab],
            send_sem=s_send.at[0],
            recv_sem=s_recv.at[0],
            device_id=slab_peer(k),
            device_id_type=MESH,
        )

    def send_slab(k, carry):
        slab_copy(k).start()
        return carry

    lax.fori_loop(1, SLABS, send_slab, 0)
    arrived[c, slab] = own[...]

    small[1].wait()
    small[2].wait()
    lane = iota((8, 128), 1) % NT
    row_x = jnp.zeros((8, 128), jnp.int32)
    row_y = jnp.zeros((8, 128), jnp.int32)
    for t in range(NT):
        row_x = jnp.where(lane == t, sx_ref[t], row_x)
        row_y = jnp.where(lane == t, sy_ref[t], row_y)
    freq = iota((KS, 128), 0) - HALF
    sin_x, cos_x = turns_sin_cos(freq * row_x[0:1])
    sin_y, cos_y = turns_sin_cos(freq * row_y[0:1])
    wide_lane = iota((KS, 128), 1)
    ephase[0:KS] = jnp.where(wide_lane < NT, cos_y, -sin_y)[:, : 2 * NT].astype(BF16)
    ephase[KS:] = jnp.where(wide_lane < NT, sin_y, cos_y)[:, : 2 * NT].astype(BF16)
    t_cos = cos_x.T[0:NT]
    t_sin = sin_x.T[0:NT]
    table = jnp.concatenate([t_cos, t_sin], 1)
    table_hi = table.astype(BF16)
    table_lo = (table - table_hi.astype(F32)).astype(BF16)
    small[4].wait()
    weights = weights_ref[...]
    weights_hi = weights.astype(BF16)
    weights_lo = (weights - weights_hi.astype(F32)).astype(BF16)
    h = dot(weights_hi, table_hi) + dot(weights_lo, table_hi) + dot(weights_hi, table_lo)
    h = h.astype(BF16).reshape(P_DEV * ORIENT, NT, 2 * KS)
    hs[:, 0:NT] = h[:, :, 0:KS]
    hs[:, NT:] = h[:, :, KS:]
    for o in range(ORIENT):
        rank = ranks[o]
        row = owner[o : o + 1]
        at_t = (row & 1) * 128 + (rank >> 3) * 64 + (row >> 1) * 8 + (rank & 7)
        place_t[o] = (iota((KS, KS), 0) == at_t).astype(F32).astype(BF16)

    freq_row = (iota((8, KS), 1) - HALF).astype(F32)
    which = iota((8, KS), 0)
    focus = jnp.zeros((8, KS), F32)
    small[3].wait()
    for p in range(P_DEV):
        focus = jnp.where(which == p, defocus_ref[p], focus)
    sin_d, cos_d = angle_sin_cos(focus * (freq_row * freq_row * (1.0 / (HALF * HALF))))
    sin_col = sin_d.T
    cos_col = cos_d.T
    u_row = 0.1 * sin_d - 0.995 * cos_d
    v_row = -0.995 * sin_d - 0.1 * cos_d
    loads[2].wait()
    loads[3].wait()
    for p in range(P_DEV):
        for j in range(2):
            at = slice(j * 128, j * 128 + 128)
            split[...] = ibuf.at[j, p].reshape(2 * KS, 128)[...].astype(F32)
            ctf = (
                sin_col[:, p : p + 1] * u_row[p : p + 1, at]
                + cos_col[:, p : p + 1] * v_row[p : p + 1, at]
            )
            cx[p, 0, :, at] = ctf * split[pl.ds(0, KS, stride=2), :]
            cx[p, 1, :, at] = ctf * split[pl.ds(1, KS, stride=2), :]

    def placed_term(o):
        for block in range(2):
            at = slice(block * 128, block * 128 + 128)
            low = slice(KS + block * 128, KS + block * 128 + 128)
            t_re = None
            for p in range(P_DEV):
                table_h = hs[p * ORIENT + o]
                g_re = dot(ephase[at], table_h)
                g_im = dot(ephase[low], table_h)
                c_re = cx[p, 0, at]
                c_im = cx[p, 1, at]
                if t_re is None:
                    t_re = c_re * g_re - c_im * g_im
                    t_im = c_re * g_im + c_im * g_re
                else:
                    t_re += c_re * g_re - c_im * g_im
                    t_im += c_re * g_im + c_im * g_re
            term[at, 0:KS] = t_re.astype(BF16)
            term[at, KS:] = t_im.astype(BF16)
        return dot(place_t[o], term[...])

    def pair_copy(j):
        return pltpu.make_async_remote_copy(
            src_ref=sent.at[j],
            dst_ref=landed.at[j],
            send_sem=p_send.at[j],
            recv_sem=p_recv.at[j],
            device_id=partner,
            device_id_type=MESH,
        )

    def x_copy(j, k):
        return pltpu.make_async_remote_copy(
            src_ref=xsend.at[j, lax.rem(x + k, 4)],
            dst_ref=xrecv.at[j, x],
            send_sem=x_send.at[j],
            recv_sem=x_recv.at[j],
            device_id=x_peer(k),
            device_id_type=MESH,
        )

    def y_copy(j, k):
        return pltpu.make_async_remote_copy(
            src_ref=ysend.at[j, lax.rem(y + k, YS)],
            dst_ref=yrecv.at[j, y],
            send_sem=y_send.at[j],
            recv_sem=y_recv.at[j],
            device_id=y_peer(k),
            device_id_type=MESH,
        )

    def z_copy(j, k):
        return pltpu.make_async_remote_copy(
            src_ref=zsend.at[j],
            dst_ref=zrecv.at[j, z],
            send_sem=z_send.at[j],
            recv_sem=z_recv.at[j],
            device_id=z_peer(k),
            device_id_type=MESH,
        )

    def give(j, carry):
        sent[j] = placed_term(2 * (1 - c) + j).astype(BF16)
        pair_copy(j).start()
        return carry

    lax.fori_loop(0, 2, give, 0)

    def keep(j, carry):
        mine = placed_term(2 * c + j)
        pair_copy(j).wait_recv()
        both = (mine + landed[j].astype(F32)).astype(BF16)
        xsend[j] = both.reshape(4, 64, 2 * KS)

        def send_x(k, inner):
            x_copy(j, k).start()
            return inner

        lax.fori_loop(1, 4, send_x, 0)
        xrecv[j, x] = xsend[j, x]
        return carry

    lax.fori_loop(0, 2, keep, 0)

    for o in range(ORIENT):
        at_s = owner[o : o + 1] * OWNED + ranks[o]
        place_s[o] = (iota((KS, KS), 0) == at_s).astype(F32).astype(BF16)
    group = wide_lane // NT
    for o in range(ORIENT):
        cos_o = jnp.where(group == o, cos_x, 0.0).astype(BF16)
        sin_o = jnp.where(group == o, sin_x, 0.0).astype(BF16)
        at = (o % 2) * 2 * KS
        fx[o // 2, at : at + KS, 0:128] = cos_o
        fx[o // 2, at : at + KS, 128:] = -sin_o
        fx[o // 2, at + KS : at + 2 * KS, 0:128] = sin_o
        fx[o // 2, at + KS : at + 2 * KS, 128:] = cos_o
    table_y = jnp.concatenate([cos_y.T[0:NT], sin_y.T[0:NT]], 1) * (1.0 / KS)
    fy_hi = table_y.astype(BF16)
    fy[0:NT] = fy_hi
    fy[NT:] = (table_y - fy_hi.astype(F32)).astype(BF16)

    def correlate(half, first):
        for j in range(2):
            rows_s = arrived[half, :, j * OWNED : (j + 1) * OWNED, :].reshape(KS, 2 * KS)
            su[j] = dot_t(place_s[2 * half + j], rows_s)
        for block in range(2):
            at = slice(block * 128, block * 128 + 128)
            for p in range(P_DEV):
                c_re = cx[p, 0, at]
                c_im = cx[p, 1, at]
                q = []
                for j in range(2):
                    s_re = su[j, at, 0:KS]
                    s_im = su[j, at, KS:]
                    q.append((s_re * c_re + s_im * c_im).astype(BF16))
                    q.append((s_re * c_im - s_im * c_re).astype(BF16))
                part = dot(jnp.concatenate(q, 1), fx[half])
                if first:
                    zacc[p, at] = part
                else:
                    zacc[p, at] += part

    line_row = jnp.concatenate([2 * own_line, 2 * own_line + 1], 0).astype(F32)
    line_row = jnp.broadcast_to(line_row, (128, 128)).T[0:8].astype(jnp.int32)
    line_ref[...] = line_row
    outs = [pltpu.make_async_copy(line_ref, line_hbm, out_sem.at[0])]
    outs[0].start()
    def pass_on(j, carry):
        pltpu.make_async_copy(
            xrecv.at[j, pl.ds(0, 3)], xrecv.at[j, pl.ds(0, 3)], x_recv.at[j]
        ).wait()
        for part in range(2):
            at = slice(part * KS, part * KS + KS)
            total = xrecv[j, 0, :, at].astype(F32)
            for other in range(1, 4):
                total += xrecv[j, other, :, at].astype(F32)
            tile_y[:, part * 8 : part * 8 + 8] = total.reshape(YS, 8, KS)
        ysend[j] = tile_y[...].astype(BF16)

        def send_y(k, inner):
            y_copy(j, k).start()
            return inner

        lax.fori_loop(1, YS, send_y, 0)
        yrecv[j, y] = ysend[j, y]
        return carry

    lax.fori_loop(0, 2, pass_on, 0)
    pltpu.make_async_copy(
        arrived.at[0, pl.ds(0, SLABS - 1)], arrived.at[0, pl.ds(0, SLABS - 1)], s_recv.at[0]
    ).wait()
    forward = pltpu.make_async_remote_copy(
        src_ref=arrived.at[c],
        dst_ref=arrived.at[c],
        send_sem=s_send.at[1],
        recv_sem=s_recv.at[1],
        device_id=partner,
        device_id_type=MESH,
    )
    forward.start()
    correlate(c, True)

    def spread(j, carry):
        pltpu.make_async_copy(
            yrecv.at[j, pl.ds(0, YS - 1)], yrecv.at[j, pl.ds(0, YS - 1)], y_recv.at[j]
        ).wait()
        total = yrecv[j, 0].astype(F32)
        for other in range(1, YS):
            total += yrecv[j, other].astype(F32)
        zsend[j] = total.astype(BF16)

        def send_z(k, inner):
            z_copy(j, k).start()
            return inner

        lax.fori_loop(1, ZS, send_z, 0)
        zrecv[j, z] = zsend[j]
        return carry

    lax.fori_loop(0, 2, spread, 0)
    forward.wait_recv()
    correlate(1 - c, False)

    place = x_lo * 2 + c
    for j in range(2):
        pltpu.make_async_copy(
            zrecv.at[j, pl.ds(0, ZS - 1)], zrecv.at[j, pl.ds(0, ZS - 1)], z_recv.at[j]
        ).wait()
        total = zrecv[j, 0].astype(F32)
        for other in range(1, ZS):
            total += zrecv[j, other].astype(F32)
        fin[place, j] = (total * SCALE).astype(BF16)

    def group_copy(k):
        return pltpu.make_async_remote_copy(
            src_ref=fin.at[place],
            dst_ref=fin.at[place],
            send_sem=f_send.at[0],
            recv_sem=f_recv.at[0],
            device_id=group_peer(k),
            device_id_type=MESH,
        )

    for k in range(1, 4):
        group_copy(k).start()
    for p in range(P_DEV):
        full = jnp.concatenate([zacc[p, :, 0:128], zacc[p, :, 128:]], 0)
        full_hi = full.astype(BF16)
        full_lo = (full - full_hi.astype(F32)).astype(BF16)
        both = dot(fy[...], full_hi)
        scores_ref[p] = both[0:NT] + both[NT:] + dot(fy[0:NT], full_lo)
    outs.append(pltpu.make_async_copy(scores_ref, scores_hbm, out_sem.at[1]))
    outs[1].start()

    pltpu.make_async_copy(fin.at[pl.ds(0, 3)], fin.at[pl.ds(0, 3)], f_recv.at[0]).wait()
    outs.append(pltpu.make_async_copy(fin, rows_hbm, out_sem.at[2]))
    outs[2].start()

    pltpu.make_async_copy(
        arrived.at[0, pl.ds(0, SLABS - 1)], arrived.at[0, pl.ds(0, SLABS - 1)], s_send.at[0]
    ).wait()
    forward.wait_send()
    for j in range(2):
        pair_copy(j).wait_send()
    for j in range(2):
        pltpu.make_async_copy(
            xrecv.at[j, pl.ds(0, 3)], xrecv.at[j, pl.ds(0, 3)], x_send.at[j]
        ).wait()
    for j in range(2):
        pltpu.make_async_copy(
            yrecv.at[j, pl.ds(0, YS - 1)], yrecv.at[j, pl.ds(0, YS - 1)], y_send.at[j]
        ).wait()
        pltpu.make_async_copy(
            zrecv.at[j, pl.ds(0, ZS - 1)], zrecv.at[j, pl.ds(0, ZS - 1)], z_send.at[j]
        ).wait()
    pltpu.make_async_copy(fin.at[pl.ds(0, 3)], fin.at[pl.ds(0, 3)], f_send.at[0]).wait()
    for out in outs:
        out.wait()


def finish(fin_ref, line_ref, found_ref, scores_ref, update_hbm, rows, buf, out_sem):
    for o in range(ORIENT):
        for r in range(2):
            got = fin_ref[r * 2 + o // 2, o % 2].astype(F32)
            for part in range(2):
                first = part * 64 + o * OWNED + r * 8
                rows[first : first + 8] = got[part * 8 : part * 8 + 8]
    rows_bf16 = rows[...].astype(BF16)
    outs = []
    for piece in range(4):
        of = pl.ds(piece * 256, 256)
        insert = iota((512, 128), 0) + piece * 512 == line_ref[0:1]
        placed = dot(insert.astype(F32).astype(BF16), rows_bf16).astype(BF16)
        for j in range(2):
            buf.at[j, of].reshape(512, 128)[...] = placed[:, j * 128 : j * 128 + 128]
            outs.append(
                pltpu.make_async_copy(
                    buf.at[j, of],
                    update_hbm.at[of, :, pl.ds(j * 128, 128)],
                    out_sem.at[piece * 2 + j],
                )
            )
            outs[-1].start()
    for o in range(ORIENT):
        scores_ref[:, o] = found_ref[:, :, o * NT : (o + 1) * NT]
    for out in outs:
        out.wait()


def body(volume, images, defocus, soft_weights, slice_lines, shift_y, shift_x):
    vmem = pl.BlockSpec(memory_space=pltpu.VMEM)
    hbm = pl.BlockSpec(memory_space=pltpu.HBM)
    dma = pltpu.SemaphoreType.DMA
    found, rows, line = pl.pallas_call(
        kernel,
        out_shape=(
            jax.ShapeDtypeStruct((P_DEV, NT, ORIENT * NT), F32),
            jax.ShapeDtypeStruct((4, 2, 16, KS), BF16),
            jax.ShapeDtypeStruct((8, 128), jnp.int32),
        ),
        in_specs=[hbm] * 7,
        out_specs=(hbm, hbm, hbm),
        scratch_shapes=[
            pltpu.VMEM((P_DEV, NT, ORIENT * NT), F32),
            pltpu.VMEM((8, 128), jnp.int32),
            pltpu.VMEM((ORIENT, KS), jnp.int32),
            pltpu.VMEM((P_DEV * ORIENT * NT, NT), F32),
            pltpu.SMEM((P_DEV,), F32),
            pltpu.SMEM((NT,), jnp.int32),
            pltpu.SMEM((NT,), jnp.int32),
            pltpu.VMEM((2, LINES, 2, 128), BF16),
            pltpu.VMEM((2, P_DEV, KS, 2, 128), BF16),
            pltpu.VMEM((2 * KS, 128), F32),
            pltpu.VMEM((2 * OWNED, 2 * KS), BF16),
            pltpu.VMEM((2, SLABS, 2 * OWNED, 2 * KS), BF16),
            pltpu.VMEM((4 * OWNED, 2 * LINES), BF16),
            pltpu.VMEM((ORIENT, KS, KS), BF16),
            pltpu.VMEM((ORIENT, KS, KS), BF16),
            pltpu.VMEM((2, 4 * KS, 256), BF16),
            pltpu.VMEM((2 * KS, 2 * NT), BF16),
            pltpu.VMEM((2 * NT, 2 * KS), BF16),
            pltpu.VMEM((P_DEV * ORIENT, 2 * NT, KS), BF16),
            pltpu.VMEM((P_DEV, 2, KS, KS), F32),
            pltpu.VMEM((KS, 2 * KS), BF16),
            pltpu.VMEM((2, KS, 2 * KS), BF16),
            pltpu.VMEM((2, KS, 2 * KS), BF16),
            pltpu.VMEM((2, 4, 64, 2 * KS), BF16),
            pltpu.VMEM((2, 4, 64, 2 * KS), BF16),
            pltpu.VMEM((2, YS, 16, KS), BF16),
            pltpu.VMEM((2, YS, 16, KS), BF16),
            pltpu.VMEM((2, 16, KS), BF16),
            pltpu.VMEM((2, ZS, 16, KS), BF16),
            pltpu.VMEM((4, 2, 16, KS), BF16),
            pltpu.VMEM((YS, 16, KS), F32),
            pltpu.VMEM((P_DEV, KS, 256), F32),
            pltpu.VMEM((2, KS, 2 * KS), F32),
            dma((5,)),
            dma((4,)),
            dma((3,)),
            dma((2,)),
            dma((2,)),
            dma((2,)),
            dma((2,)),
            dma((2,)),
            dma((2,)),
            dma((2,)),
            dma((2,)),
            dma((2,)),
            dma((2,)),
            dma((1,)),
            dma((1,)),
        ],
        compiler_params=pltpu.CompilerParams(
            collective_id=0, has_side_effects=True, vmem_limit_bytes=60 * 1024 * 1024
        ),
        name="cryo",
    )(
        slice_lines,
        soft_weights.reshape(P_DEV * ORIENT * NT, NT),
        defocus,
        shift_y,
        shift_x,
        volume,
        images,
    )
    return pl.pallas_call(
        finish,
        out_shape=(
            jax.ShapeDtypeStruct((P_DEV, ORIENT, NT, NT), F32),
            jax.ShapeDtypeStruct((LINES, 2, KS), BF16),
        ),
        in_specs=[vmem] * 3,
        out_specs=(vmem, hbm),
        scratch_shapes=[
            pltpu.VMEM((2 * ORIENT * OWNED, KS), F32),
            pltpu.VMEM((2, LINES, 2, 128), BF16),
            dma((8,)),
        ],
        compiler_params=pltpu.CompilerParams(vmem_limit_bytes=60 * 1024 * 1024),
        name="finish",
    )(rows, line, found)


def solution(mesh):
    placed = (
        P("slab", None, None),
        P(("dom", "slab"), None, None, None),
        P(("dom", "slab")),
        P(("dom", "slab"), None, None, None),
        P(),
        P(),
        P(),
    )
    return jax.shard_map(
        body,
        mesh=mesh,
        in_specs=placed,
        out_specs=(P(("dom", "slab"), None, None, None), P("slab", None, None)),
        check_vma=False,
    )
```

```python
import math

import jax
import jax.numpy as jnp
from jax import lax
from jax.experimental import pallas as pl
from jax.experimental.pallas import tpu as pltpu
from jax.sharding import PartitionSpec as P

KS = 256
HALF = KS // 2
P_DEV = 4
LINES = 1024
ORIENT = 4
NT = 32
OWNED = 16
PARTICLES = 2048
SLABS = 16
ZS = 8
YS = 8
XLO = 2
SCALE = 1.0 / math.sqrt(NT * NT * PARTICLES)
F32 = jnp.float32
BF16 = jnp.bfloat16
MESH = pl.DeviceIdType.MESH


def dot(a, b):
    return jnp.dot(a, b, preferred_element_type=F32)


def dot_t(a, b):
    return lax.dot_general(a, b, (((0,), (0,)), ((), ())), preferred_element_type=F32)


def poly_sin_cos(r):
    s = r * r
    sin = r * (1.0 + s * (-1 / 6 + s * (1 / 120 + s * (-1 / 5040 + s * (1 / 362880)))))
    cos = 1.0 + s * (-0.5 + s * (1 / 24 + s * (-1 / 720 + s * (1 / 40320))))
    return sin, cos


def rotate(quadrant, sin, cos):
    q = quadrant & 3
    odd = (q & 1) == 1
    s = jnp.where(odd, cos, sin)
    c = jnp.where(odd, sin, cos)
    s = jnp.where(q >= 2, -s, s)
    c = jnp.where((q == 1) | (q == 2), -c, c)
    return s, c


def turns_sin_cos(turns):
    t = turns & (KS - 1)
    q = (t + KS // 8) >> 6
    r = (t - (q << 6)).astype(F32) * (2.0 * math.pi / KS)
    return rotate(q, *poly_sin_cos(r))


def angle_sin_cos(x):
    n = jnp.floor(x * (2.0 / math.pi) + 0.5)
    r = x - n * 1.5703125
    r = r - n * 4.837512969970703e-4
    r = r - n * 7.549789948768648e-8
    return rotate(n.astype(jnp.int32), *poly_sin_cos(r))


def iota(shape, dim):
    return lax.broadcasted_iota(jnp.int32, shape, dim)


def kernel(
    lines_hbm, weights_hbm, defocus_hbm, sy_hbm, sx_hbm, volume_hbm, images_hbm,
    scores_hbm, rows_hbm, line_hbm,
    scores_ref, line_ref, lines_ref, weights_ref, defocus_ref, sy_ref, sx_ref,
    vbuf, ibuf, split, own, arrived, gather, place_s, place_t,
    fx, ephase, fy, hs, cx, term, sent, landed, xsend, xrecv, ysend, yrecv, zsend, zrecv,
    fin, tile_y, zacc, su,
    small_sem, in_sem, out_sem, s_send, s_recv, p_send, p_recv, x_send, x_recv, z_send, z_recv,
    y_send, y_recv, f_send, f_recv,
):
    dom = lax.axis_index("dom")
    slab = lax.axis_index("slab")
    x_lo = dom // 16
    z = (dom // 2) % 8
    c = dom % 2
    zc = z * 2 + c
    partner = (dom + 1 - 2 * c, slab)
    y = slab // 2
    x_hi = slab % 2
    x = x_hi * 2 + x_lo

    small = [
        pltpu.make_async_copy(src, dst, small_sem.at[i])
        for i, (src, dst) in enumerate(
            (
                (lines_hbm, lines_ref),
                (sx_hbm, sx_ref),
                (sy_hbm, sy_ref),
                (defocus_hbm, defocus_ref),
                (weights_hbm, weights_ref),
            )
        )
    ]
    for load in small:
        load.start()
    loads = []
    for j in range(2):
        cols = pl.ds(j * 128, 128)
        loads.append(pltpu.make_async_copy(volume_hbm.at[:, :, cols], vbuf.at[j], in_sem.at[j]))
    for j in range(2):
        cols = pl.ds(j * 128, 128)
        loads.append(
            pltpu.make_async_copy(images_hbm.at[:, :, :, cols], ibuf.at[j], in_sem.at[2 + j])
        )
    for load in loads:
        load.start()

    barrier = pltpu.get_barrier_semaphore()

    def slab_peer(k):
        to = lax.rem(slab + k, SLABS)
        flip = (to % 2 + x_hi) % 2
        return ((x_lo + flip) % 2) * 16 + zc, to

    def x_peer(k):
        to = lax.rem(x + k, 4)
        return (to % 2) * 16 + zc, y * 2 + to // 2

    def y_peer(k):
        return dom, lax.rem(y + k, YS) * 2 + x_hi

    def z_peer(k):
        return x_lo * 16 + lax.rem(z + k, ZS) * 2 + c, slab

    def group_peer(k):
        to = lax.rem(x_lo * 2 + c + k, 4)
        return (to // 2) * 16 + z * 2 + to % 2, slab

    def greet(peer):
        pl.semaphore_signal(barrier, inc=1, device_id=peer, device_id_type=MESH)

    def greet_slab(k, carry):
        greet(slab_peer(k))
        return carry

    def greet_z(k, carry):
        greet(z_peer(k))
        return carry

    lax.fori_loop(1, SLABS, greet_slab, 0)
    lax.fori_loop(1, ZS, greet_z, 0)
    for k in range(1, 4):
        greet(group_peer(k))
    greet((dom, y * 2 + 1 - x_hi))

    small[0].wait()
    lines = lines_ref[...]
    owner = lines >> 10
    local = (lines & (LINES - 1)).astype(F32)
    slab_rows = iota((SLABS, KS), 0)
    marks = jnp.concatenate(
        [(owner[o : o + 1] == slab_rows).astype(F32) for o in range(ORIENT)], 0
    )
    before = (iota((KS, KS), 0) < iota((KS, KS), 1)).astype(F32).astype(BF16)
    earlier = dot(marks.astype(BF16), before) * marks
    ranks = [
        jnp.sum(earlier[o * SLABS : (o + 1) * SLABS], axis=0, keepdims=True).astype(jnp.int32)
        for o in range(ORIENT)
    ]
    own_line = []
    for o in range(ORIENT):
        mine = (owner[o : o + 1] == slab) & (ranks[o] == slab_rows)
        own_line.append(
            jnp.sum(jnp.where(mine, local[o : o + 1], 0.0), axis=1, keepdims=True)
        )
    own_line = jnp.concatenate(own_line, 0).astype(jnp.int32)
    o_own = 2 * c + z % 2
    first_line = own_line[0:OWNED]
    for o in range(1, ORIENT):
        first_line = jnp.where(o_own == o, own_line[o * OWNED : (o + 1) * OWNED], first_line)
    column = iota((OWNED, 2 * LINES), 1)
    gather[0:OWNED] = (column == 2 * first_line).astype(F32).astype(BF16)
    gather[OWNED:] = (column == 2 * first_line + 1).astype(F32).astype(BF16)

    for j in range(2):
        loads[j].wait()
        picked = dot(gather[...], vbuf.at[j].reshape(2 * LINES, 128)[...]).astype(BF16)
        for part in range(2):
            at = slice(part * KS + j * 128, part * KS + j * 128 + 128)
            own[:, at] = picked[part * OWNED : part * OWNED + OWNED]

    pl.semaphore_wait(barrier, SLABS - 1 + ZS - 1 + 3 + 1)

    def slab_copy(k):
        return pltpu.make_async_remote_copy(
            src_ref=own,
            dst_ref=arrived.at[o_own, slab],
            send_sem=s_send.at[0],
            recv_sem=s_recv.at[0],
            device_id=slab_peer(k),
            device_id_type=MESH,
        )

    def send_slab(k, carry):
        slab_copy(k).start()
        return carry

    lax.fori_loop(1, SLABS, send_slab, 0)
    arrived[o_own, slab] = own[...]

    small[1].wait()
    small[2].wait()
    lane = iota((8, 128), 1) % NT
    row_x = jnp.zeros((8, 128), jnp.int32)
    row_y = jnp.zeros((8, 128), jnp.int32)
    for t in range(NT):
        row_x = jnp.where(lane == t, sx_ref[t], row_x)
        row_y = jnp.where(lane == t, sy_ref[t], row_y)
    freq = iota((KS, 128), 0) - HALF
    sin_x, cos_x = turns_sin_cos(freq * row_x[0:1])
    sin_y, cos_y = turns_sin_cos(freq * row_y[0:1])
    wide_lane = iota((KS, 128), 1)
    ephase[0:KS] = jnp.where(wide_lane < NT, cos_y, -sin_y)[:, : 2 * NT].astype(BF16)
    ephase[KS:] = jnp.where(wide_lane < NT, sin_y, cos_y)[:, : 2 * NT].astype(BF16)
    t_cos = cos_x.T[0:NT]
    t_sin = sin_x.T[0:NT]
    table = jnp.concatenate([t_cos, t_sin], 1)
    table_hi = table.astype(BF16)
    table_lo = (table - table_hi.astype(F32)).astype(BF16)
    small[4].wait()
    weights = weights_ref[...]
    weights_hi = weights.astype(BF16)
    weights_lo = (weights - weights_hi.astype(F32)).astype(BF16)
    h = dot(weights_hi, table_hi) + dot(weights_lo, table_hi) + dot(weights_hi, table_lo)
    h = h.astype(BF16).reshape(P_DEV * ORIENT, NT, 2 * KS)
    hs[:, 0:NT] = h[:, :, 0:KS]
    hs[:, NT:] = h[:, :, KS:]
    for o in range(ORIENT):
        rank = ranks[o]
        row = owner[o : o + 1]
        at_t = (row & 1) * 128 + (rank >> 3) * 64 + (row >> 1) * 8 + (rank & 7)
        place_t[o] = (iota((KS, KS), 0) == at_t).astype(F32).astype(BF16)

    freq_row = (iota((8, KS), 1) - HALF).astype(F32)
    which = iota((8, KS), 0)
    focus = jnp.zeros((8, KS), F32)
    small[3].wait()
    for p in range(P_DEV):
        focus = jnp.where(which == p, defocus_ref[p], focus)
    sin_d, cos_d = angle_sin_cos(focus * (freq_row * freq_row * (1.0 / (HALF * HALF))))
    sin_col = sin_d.T
    cos_col = cos_d.T
    u_row = 0.1 * sin_d - 0.995 * cos_d
    v_row = -0.995 * sin_d - 0.1 * cos_d
    loads[2].wait()
    loads[3].wait()
    for p in range(P_DEV):
        for j in range(2):
            at = slice(j * 128, j * 128 + 128)
            split[...] = ibuf.at[j, p].reshape(2 * KS, 128)[...].astype(F32)
            ctf = (
                sin_col[:, p : p + 1] * u_row[p : p + 1, at]
                + cos_col[:, p : p + 1] * v_row[p : p + 1, at]
            )
            cx[p, 0, :, at] = ctf * split[pl.ds(0, KS, stride=2), :]
            cx[p, 1, :, at] = ctf * split[pl.ds(1, KS, stride=2), :]

    def placed_term(o):
        for block in range(2):
            at = slice(block * 128, block * 128 + 128)
            low = slice(KS + block * 128, KS + block * 128 + 128)
            t_re = None
            for p in range(P_DEV):
                table_h = hs[p * ORIENT + o]
                g_re = dot(ephase[at], table_h)
                g_im = dot(ephase[low], table_h)
                c_re = cx[p, 0, at]
                c_im = cx[p, 1, at]
                if t_re is None:
                    t_re = c_re * g_re - c_im * g_im
                    t_im = c_re * g_im + c_im * g_re
                else:
                    t_re += c_re * g_re - c_im * g_im
                    t_im += c_re * g_im + c_im * g_re
            term[at, 0:KS] = t_re.astype(BF16)
            term[at, KS:] = t_im.astype(BF16)
        return dot(place_t[o], term[...])

    def pair_copy(j):
        return pltpu.make_async_remote_copy(
            src_ref=sent.at[j],
            dst_ref=landed.at[j],
            send_sem=p_send.at[j],
            recv_sem=p_recv.at[j],
            device_id=partner,
            device_id_type=MESH,
        )

    def x_copy(j, k):
        return pltpu.make_async_remote_copy(
            src_ref=xsend.at[j, lax.rem(x + k, 4)],
            dst_ref=xrecv.at[j, x],
            send_sem=x_send.at[j],
            recv_sem=x_recv.at[j],
            device_id=x_peer(k),
            device_id_type=MESH,
        )

    def y_copy(j, k):
        return pltpu.make_async_remote_copy(
            src_ref=ysend.at[j, lax.rem(y + k, YS)],
            dst_ref=yrecv.at[j, y],
            send_sem=y_send.at[j],
            recv_sem=y_recv.at[j],
            device_id=y_peer(k),
            device_id_type=MESH,
        )

    def z_copy(j, k):
        return pltpu.make_async_remote_copy(
            src_ref=zsend.at[j],
            dst_ref=zrecv.at[j, z],
            send_sem=z_send.at[j],
            recv_sem=z_recv.at[j],
            device_id=z_peer(k),
            device_id_type=MESH,
        )

    def give(j, carry):
        sent[j] = placed_term(2 * (1 - c) + j).astype(BF16)
        pair_copy(j).start()
        return carry

    lax.fori_loop(0, 2, give, 0)

    def keep(j, carry):
        mine = placed_term(2 * c + j)
        pair_copy(j).wait_recv()
        both = (mine + landed[j].astype(F32)).astype(BF16)
        xsend[j] = both.reshape(4, 64, 2 * KS)

        def send_x(k, inner):
            x_copy(j, k).start()
            return inner

        lax.fori_loop(1, 4, send_x, 0)
        xrecv[j, x] = xsend[j, x]
        return carry

    lax.fori_loop(0, 2, keep, 0)

    def wait_rows(n, sem):
        part = arrived.at[0, pl.ds(0, n)]
        pltpu.make_async_copy(part, part, sem).wait()

    def pass_rows(o, sem, first=0, n=SLABS, to=partner):
        part = arrived.at[o, pl.ds(first, n)]
        return pltpu.make_async_remote_copy(
            src_ref=part,
            dst_ref=part,
            send_sem=s_send.at[sem],
            recv_sem=s_recv.at[sem],
            device_id=to,
            device_id_type=MESH,
        )

    wait_rows(SLABS - 1, s_recv.at[0])
    to_up = pass_rows(o_own, 2, 0, 8, z_peer(1))
    to_down = pass_rows(o_own, 3, 8, 8, z_peer(ZS - 1))
    to_partner = pass_rows(o_own, 1)
    to_up.start()
    to_down.start()
    to_partner.start()

    for o in range(ORIENT):
        at_s = owner[o : o + 1] * OWNED + ranks[o]
        place_s[o] = (iota((KS, KS), 0) == at_s).astype(F32).astype(BF16)
    group = wide_lane // NT
    for o in range(ORIENT):
        cos_o = jnp.where(group == o, cos_x, 0.0).astype(BF16)
        sin_o = jnp.where(group == o, sin_x, 0.0).astype(BF16)
        at = (o // 2) * 2 * KS
        fx[o % 2, at : at + KS, 0:128] = cos_o
        fx[o % 2, at : at + KS, 128:] = -sin_o
        fx[o % 2, at + KS : at + 2 * KS, 0:128] = sin_o
        fx[o % 2, at + KS : at + 2 * KS, 128:] = cos_o
    table_y = jnp.concatenate([cos_y.T[0:NT], sin_y.T[0:NT]], 1) * (1.0 / KS)
    fy_hi = table_y.astype(BF16)
    fy[0:NT] = fy_hi
    fy[NT:] = (table_y - fy_hi.astype(F32)).astype(BF16)

    def correlate(parity, first):
        for j in range(2):
            o = 2 * j + parity
            su[j] = dot_t(place_s[o], arrived[o].reshape(KS, 2 * KS))
        for block in range(2):
            at = slice(block * 128, block * 128 + 128)
            for p in range(P_DEV):
                c_re = cx[p, 0, at]
                c_im = cx[p, 1, at]
                q = []
                for j in range(2):
                    s_re = su[j, at, 0:KS]
                    s_im = su[j, at, KS:]
                    q.append((s_re * c_re + s_im * c_im).astype(BF16))
                    q.append((s_re * c_im - s_im * c_re).astype(BF16))
                part = dot(jnp.concatenate(q, 1), fx[parity])
                if first:
                    zacc[p, at] = part
                else:
                    zacc[p, at] += part

    line_row = jnp.concatenate([2 * own_line, 2 * own_line + 1], 0).astype(F32)
    line_row = jnp.broadcast_to(line_row, (128, 128)).T[0:8].astype(jnp.int32)
    line_ref[...] = line_row
    outs = [pltpu.make_async_copy(line_ref, line_hbm, out_sem.at[0])]
    outs[0].start()
    wait_rows(SLABS, s_recv.at[1])
    correlate(z % 2, True)
    def pass_on(j, carry):
        pltpu.make_async_copy(
            xrecv.at[j, pl.ds(0, 3)], xrecv.at[j, pl.ds(0, 3)], x_recv.at[j]
        ).wait()
        for part in range(2):
            at = slice(part * KS, part * KS + KS)
            total = xrecv[j, 0, :, at].astype(F32)
            for other in range(1, 4):
                total += xrecv[j, other, :, at].astype(F32)
            tile_y[:, part * 8 : part * 8 + 8] = total.reshape(YS, 8, KS)
        ysend[j] = tile_y[...].astype(BF16)

        def send_y(k, inner):
            y_copy(j, k).start()
            return inner

        lax.fori_loop(1, YS, send_y, 0)
        yrecv[j, y] = ysend[j, y]
        return carry

    lax.fori_loop(0, 2, pass_on, 0)
    wait_rows(8, s_recv.at[2])
    wait_rows(8, s_recv.at[3])
    to_partner_too = pass_rows(2 * c + 1 - z % 2, 4)
    to_partner_too.start()

    def spread(j, carry):
        pltpu.make_async_copy(
            yrecv.at[j, pl.ds(0, YS - 1)], yrecv.at[j, pl.ds(0, YS - 1)], y_recv.at[j]
        ).wait()
        total = yrecv[j, 0].astype(F32)
        for other in range(1, YS):
            total += yrecv[j, other].astype(F32)
        zsend[j] = total.astype(BF16)

        def send_z(k, inner):
            z_copy(j, k).start()
            return inner

        lax.fori_loop(1, ZS, send_z, 0)
        zrecv[j, z] = zsend[j]
        return carry

    lax.fori_loop(0, 2, spread, 0)
    wait_rows(SLABS, s_recv.at[4])
    correlate(1 - z % 2, False)

    place = x_lo * 2 + c
    for j in range(2):
        pltpu.make_async_copy(
            zrecv.at[j, pl.ds(0, ZS - 1)], zrecv.at[j, pl.ds(0, ZS - 1)], z_recv.at[j]
        ).wait()
        total = zrecv[j, 0].astype(F32)
        for other in range(1, ZS):
            total += zrecv[j, other].astype(F32)
        fin[place, j] = (total * SCALE).astype(BF16)

    def group_copy(k):
        return pltpu.make_async_remote_copy(
            src_ref=fin.at[place],
            dst_ref=fin.at[place],
            send_sem=f_send.at[0],
            recv_sem=f_recv.at[0],
            device_id=group_peer(k),
            device_id_type=MESH,
        )

    for k in range(1, 4):
        group_copy(k).start()
    for p in range(P_DEV):
        full = jnp.concatenate([zacc[p, :, 0:128], zacc[p, :, 128:]], 0)
        full_hi = full.astype(BF16)
        full_lo = (full - full_hi.astype(F32)).astype(BF16)
        both = dot(fy[...], full_hi)
        scores_ref[p] = both[0:NT] + both[NT:] + dot(fy[0:NT], full_lo)
    outs.append(pltpu.make_async_copy(scores_ref, scores_hbm, out_sem.at[1]))
    outs[1].start()

    pltpu.make_async_copy(fin.at[pl.ds(0, 3)], fin.at[pl.ds(0, 3)], f_recv.at[0]).wait()
    outs.append(pltpu.make_async_copy(fin, rows_hbm, out_sem.at[2]))
    outs[2].start()

    wait_rows(SLABS - 1, s_send.at[0])
    for sent_rows in (to_partner, to_up, to_down, to_partner_too):
        sent_rows.wait_send()
    for j in range(2):
        pair_copy(j).wait_send()
    for j in range(2):
        pltpu.make_async_copy(
            xrecv.at[j, pl.ds(0, 3)], xrecv.at[j, pl.ds(0, 3)], x_send.at[j]
        ).wait()
    for j in range(2):
        pltpu.make_async_copy(
            yrecv.at[j, pl.ds(0, YS - 1)], yrecv.at[j, pl.ds(0, YS - 1)], y_send.at[j]
        ).wait()
        pltpu.make_async_copy(
            zrecv.at[j, pl.ds(0, ZS - 1)], zrecv.at[j, pl.ds(0, ZS - 1)], z_send.at[j]
        ).wait()
    pltpu.make_async_copy(fin.at[pl.ds(0, 3)], fin.at[pl.ds(0, 3)], f_send.at[0]).wait()
    for out in outs:
        out.wait()


def finish(
    fin_hbm, line_hbm, found_hbm, scores_hbm, update_hbm,
    fin_ref, line_ref, found_ref, scores_ref, insert, rows, buf, in_sem, out_sem,
):
    loads = [
        pltpu.make_async_copy(src, dst, in_sem.at[i])
        for i, (src, dst) in enumerate(
            ((line_hbm, line_ref), (fin_hbm, fin_ref), (found_hbm, found_ref))
        )
    ]
    for load in loads:
        load.start()
    loads[0].wait()
    insert[...] = (iota((2 * LINES, 128), 0) == line_ref[0:1]).astype(F32).astype(BF16)
    loads[1].wait()
    for o in range(ORIENT):
        for r in range(2):
            got = fin_ref[r * 2 + o // 2, o % 2].astype(F32)
            for part in range(2):
                first = part * 64 + o * OWNED + r * 8
                rows[first : first + 8] = got[part * 8 : part * 8 + 8]
    rows_bf16 = rows[...].astype(BF16)
    outs = []
    for piece in range(4):
        of = pl.ds(piece * 256, 256)
        at = slice(piece * 512, piece * 512 + 512)
        placed = dot(insert[at], rows_bf16).astype(BF16)
        for j in range(2):
            buf.at[j, of].reshape(512, 128)[...] = placed[:, j * 128 : j * 128 + 128]
            outs.append(
                pltpu.make_async_copy(
                    buf.at[j, of],
                    update_hbm.at[of, :, pl.ds(j * 128, 128)],
                    out_sem.at[piece * 2 + j],
                )
            )
            outs[-1].start()
    loads[2].wait()
    for o in range(ORIENT):
        scores_ref[:, o] = found_ref[:, :, o * NT : (o + 1) * NT]
    outs.append(pltpu.make_async_copy(scores_ref, scores_hbm, out_sem.at[8]))
    outs[-1].start()
    for out in outs:
        out.wait()


def body(volume, images, defocus, soft_weights, slice_lines, shift_y, shift_x):
    hbm = pl.BlockSpec(memory_space=pltpu.HBM)
    dma = pltpu.SemaphoreType.DMA
    found, rows, line = pl.pallas_call(
        kernel,
        out_shape=(
            jax.ShapeDtypeStruct((P_DEV, NT, ORIENT * NT), F32),
            jax.ShapeDtypeStruct((4, 2, 16, KS), BF16),
            jax.ShapeDtypeStruct((8, 128), jnp.int32),
        ),
        in_specs=[hbm] * 7,
        out_specs=(hbm, hbm, hbm),
        scratch_shapes=[
            pltpu.VMEM((P_DEV, NT, ORIENT * NT), F32),
            pltpu.VMEM((8, 128), jnp.int32),
            pltpu.VMEM((ORIENT, KS), jnp.int32),
            pltpu.VMEM((P_DEV * ORIENT * NT, NT), F32),
            pltpu.SMEM((P_DEV,), F32),
            pltpu.SMEM((NT,), jnp.int32),
            pltpu.SMEM((NT,), jnp.int32),
            pltpu.VMEM((2, LINES, 2, 128), BF16),
            pltpu.VMEM((2, P_DEV, KS, 2, 128), BF16),
            pltpu.VMEM((2 * KS, 128), F32),
            pltpu.VMEM((OWNED, 2 * KS), BF16),
            pltpu.VMEM((ORIENT, SLABS, OWNED, 2 * KS), BF16),
            pltpu.VMEM((2 * OWNED, 2 * LINES), BF16),
            pltpu.VMEM((ORIENT, KS, KS), BF16),
            pltpu.VMEM((ORIENT, KS, KS), BF16),
            pltpu.VMEM((2, 4 * KS, 256), BF16),
            pltpu.VMEM((2 * KS, 2 * NT), BF16),
            pltpu.VMEM((2 * NT, 2 * KS), BF16),
            pltpu.VMEM((P_DEV * ORIENT, 2 * NT, KS), BF16),
            pltpu.VMEM((P_DEV, 2, KS, KS), F32),
            pltpu.VMEM((KS, 2 * KS), BF16),
            pltpu.VMEM((2, KS, 2 * KS), BF16),
            pltpu.VMEM((2, KS, 2 * KS), BF16),
            pltpu.VMEM((2, 4, 64, 2 * KS), BF16),
            pltpu.VMEM((2, 4, 64, 2 * KS), BF16),
            pltpu.VMEM((2, YS, 16, KS), BF16),
            pltpu.VMEM((2, YS, 16, KS), BF16),
            pltpu.VMEM((2, 16, KS), BF16),
            pltpu.VMEM((2, ZS, 16, KS), BF16),
            pltpu.VMEM((4, 2, 16, KS), BF16),
            pltpu.VMEM((YS, 16, KS), F32),
            pltpu.VMEM((P_DEV, KS, 256), F32),
            pltpu.VMEM((2, KS, 2 * KS), F32),
            dma((5,)),
            dma((4,)),
            dma((3,)),
            dma((5,)),
            dma((5,)),
            dma((2,)),
            dma((2,)),
            dma((2,)),
            dma((2,)),
            dma((2,)),
            dma((2,)),
            dma((2,)),
            dma((2,)),
            dma((1,)),
            dma((1,)),
        ],
        compiler_params=pltpu.CompilerParams(
            collective_id=0, has_side_effects=True, vmem_limit_bytes=60 * 1024 * 1024
        ),
        name="cryo",
    )(
        slice_lines,
        soft_weights.reshape(P_DEV * ORIENT * NT, NT),
        defocus,
        shift_y,
        shift_x,
        volume,
        images,
    )
    return pl.pallas_call(
        finish,
        out_shape=(
            jax.ShapeDtypeStruct((P_DEV, ORIENT, NT, NT), F32),
            jax.ShapeDtypeStruct((LINES, 2, KS), BF16),
        ),
        in_specs=[hbm] * 3,
        out_specs=(hbm, hbm),
        scratch_shapes=[
            pltpu.VMEM((4, 2, 16, KS), BF16),
            pltpu.VMEM((8, 128), jnp.int32),
            pltpu.VMEM((P_DEV, NT, ORIENT * NT), F32),
            pltpu.VMEM((P_DEV, ORIENT, NT, NT), F32),
            pltpu.VMEM((2 * LINES, 2 * ORIENT * OWNED), BF16),
            pltpu.VMEM((2 * ORIENT * OWNED, KS), F32),
            pltpu.VMEM((2, LINES, 2, 128), BF16),
            dma((3,)),
            dma((9,)),
        ],
        compiler_params=pltpu.CompilerParams(vmem_limit_bytes=60 * 1024 * 1024),
        name="finish",
    )(rows, line, found)


def solution(mesh):
    placed = (
        P("slab", None, None),
        P(("dom", "slab"), None, None, None),
        P(("dom", "slab")),
        P(("dom", "slab"), None, None, None),
        P(),
        P(),
        P(),
    )
    return jax.shard_map(
        body,
        mesh=mesh,
        in_specs=placed,
        out_specs=(P(("dom", "slab"), None, None, None), P("slab", None, None)),
        check_vma=False,
    )
```

```python
import math

import jax
import jax.numpy as jnp
from jax import lax
from jax.experimental import pallas as pl
from jax.experimental.pallas import tpu as pltpu
from jax.sharding import PartitionSpec as P

KS = 256
HALF = KS // 2
P_DEV = 4
LINES = 1024
ORIENT = 4
NT = 32
OWNED = 16
PARTICLES = 2048
SLABS = 16
ZS = 8
YS = 8
XLO = 2
SCALE = 1.0 / math.sqrt(NT * NT * PARTICLES)
F32 = jnp.float32
BF16 = jnp.bfloat16
MESH = pl.DeviceIdType.MESH


def dot(a, b):
    return jnp.dot(a, b, preferred_element_type=F32)


def dot_t(a, b):
    return lax.dot_general(a, b, (((0,), (0,)), ((), ())), preferred_element_type=F32)


def poly_sin_cos(r):
    s = r * r
    sin = r * (1.0 + s * (-1 / 6 + s * (1 / 120 + s * (-1 / 5040 + s * (1 / 362880)))))
    cos = 1.0 + s * (-0.5 + s * (1 / 24 + s * (-1 / 720 + s * (1 / 40320))))
    return sin, cos


def rotate(quadrant, sin, cos):
    q = quadrant & 3
    odd = (q & 1) == 1
    s = jnp.where(odd, cos, sin)
    c = jnp.where(odd, sin, cos)
    s = jnp.where(q >= 2, -s, s)
    c = jnp.where((q == 1) | (q == 2), -c, c)
    return s, c


def turns_sin_cos(turns):
    t = turns & (KS - 1)
    q = (t + KS // 8) >> 6
    r = (t - (q << 6)).astype(F32) * (2.0 * math.pi / KS)
    return rotate(q, *poly_sin_cos(r))


def angle_sin_cos(x):
    n = jnp.floor(x * (2.0 / math.pi) + 0.5)
    r = x - n * 1.5703125
    r = r - n * 4.837512969970703e-4
    r = r - n * 7.549789948768648e-8
    return rotate(n.astype(jnp.int32), *poly_sin_cos(r))


def iota(shape, dim):
    return lax.broadcasted_iota(jnp.int32, shape, dim)


def kernel(
    lines_hbm, weights_hbm, defocus_hbm, sy_hbm, sx_hbm, volume_hbm, images_hbm,
    scores_hbm, rows_hbm, line_hbm,
    scores_ref, line_ref, lines_ref, weights_ref, defocus_ref, sy_ref, sx_ref,
    vbuf, ibuf, split, own, arrived, gather, place_s, place_t,
    fx, ephase, fy, hs, cx, term, sent, landed, xsend, xrecv, ysend, yrecv, zsend, zrecv,
    fin, tile_y, zacc, su,
    small_sem, in_sem, out_sem, s_send, s_recv, p_send, p_recv, x_send, x_recv, z_send, z_recv,
    y_send, y_recv, f_send, f_recv,
):
    dom = lax.axis_index("dom")
    slab = lax.axis_index("slab")
    x_lo = dom // 16
    z = (dom // 2) % 8
    c = dom % 2
    zc = z * 2 + c
    partner = (dom + 1 - 2 * c, slab)
    y = slab // 2
    x_hi = slab % 2
    x = x_hi * 2 + x_lo

    small = [
        pltpu.make_async_copy(src, dst, small_sem.at[i])
        for i, (src, dst) in enumerate(
            (
                (lines_hbm, lines_ref),
                (sx_hbm, sx_ref),
                (sy_hbm, sy_ref),
                (defocus_hbm, defocus_ref),
                (weights_hbm, weights_ref),
            )
        )
    ]
    for load in small:
        load.start()
    loads = []
    for j in range(2):
        cols = pl.ds(j * 128, 128)
        loads.append(pltpu.make_async_copy(volume_hbm.at[:, :, cols], vbuf.at[j], in_sem.at[j]))
    for j in range(2):
        cols = pl.ds(j * 128, 128)
        loads.append(
            pltpu.make_async_copy(images_hbm.at[:, :, :, cols], ibuf.at[j], in_sem.at[2 + j])
        )
    for load in loads:
        load.start()

    barrier = pltpu.get_barrier_semaphore()

    def slab_peer(k):
        to = lax.rem(slab + k, SLABS)
        flip = (to % 2 + x_hi) % 2
        return ((x_lo + flip) % 2) * 16 + zc, to

    def x_peer(k):
        to = lax.rem(x + k, 4)
        return (to % 2) * 16 + zc, y * 2 + to // 2

    def y_peer(k):
        return dom, lax.rem(y + k, YS) * 2 + x_hi

    def z_peer(k):
        return x_lo * 16 + lax.rem(z + k, ZS) * 2 + c, slab

    def group_peer(k):
        to = lax.rem(x_lo * 2 + c + k, 4)
        return (to // 2) * 16 + z * 2 + to % 2, slab

    def greet(peer):
        pl.semaphore_signal(barrier, inc=1, device_id=peer, device_id_type=MESH)

    def greet_slab(k, carry):
        greet(slab_peer(k))
        return carry

    def greet_z(k, carry):
        greet(z_peer(k))
        return carry

    lax.fori_loop(1, SLABS, greet_slab, 0, unroll=True)
    lax.fori_loop(1, ZS, greet_z, 0, unroll=True)
    for k in range(1, 4):
        greet(group_peer(k))
    greet((dom, y * 2 + 1 - x_hi))

    small[0].wait()
    lines = lines_ref[...]
    owner = lines >> 10
    local = (lines & (LINES - 1)).astype(F32)
    slab_rows = iota((SLABS, KS), 0)
    marks = jnp.concatenate(
        [(owner[o : o + 1] == slab_rows).astype(F32) for o in range(ORIENT)], 0
    )
    before = (iota((KS, KS), 0) < iota((KS, KS), 1)).astype(F32).astype(BF16)
    earlier = dot(marks.astype(BF16), before) * marks
    ranks = [
        jnp.sum(earlier[o * SLABS : (o + 1) * SLABS], axis=0, keepdims=True).astype(jnp.int32)
        for o in range(ORIENT)
    ]
    own_line = []
    for o in range(ORIENT):
        mine = (owner[o : o + 1] == slab) & (ranks[o] == slab_rows)
        own_line.append(
            jnp.sum(jnp.where(mine, local[o : o + 1], 0.0), axis=1, keepdims=True)
        )
    own_line = jnp.concatenate(own_line, 0).astype(jnp.int32)
    o_own = 2 * c + z % 2
    first_line = own_line[0:OWNED]
    for o in range(1, ORIENT):
        first_line = jnp.where(o_own == o, own_line[o * OWNED : (o + 1) * OWNED], first_line)
    column = iota((OWNED, 2 * LINES), 1)
    gather[0:OWNED] = (column == 2 * first_line).astype(F32).astype(BF16)
    gather[OWNED:] = (column == 2 * first_line + 1).astype(F32).astype(BF16)

    for j in range(2):
        loads[j].wait()
        picked = dot(gather[...], vbuf.at[j].reshape(2 * LINES, 128)[...]).astype(BF16)
        for part in range(2):
            at = slice(part * KS + j * 128, part * KS + j * 128 + 128)
            own[:, at] = picked[part * OWNED : part * OWNED + OWNED]

    pl.semaphore_wait(barrier, SLABS - 1 + ZS - 1 + 3 + 1)

    def slab_copy(k):
        return pltpu.make_async_remote_copy(
            src_ref=own,
            dst_ref=arrived.at[o_own, slab],
            send_sem=s_send.at[0],
            recv_sem=s_recv.at[0],
            device_id=slab_peer(k),
            device_id_type=MESH,
        )

    def send_slab(k, carry):
        slab_copy(k).start()
        return carry

    lax.fori_loop(1, SLABS, send_slab, 0, unroll=True)
    arrived[o_own, slab] = own[...]

    small[1].wait()
    small[2].wait()
    lane = iota((8, 128), 1) % NT
    row_x = jnp.zeros((8, 128), jnp.int32)
    row_y = jnp.zeros((8, 128), jnp.int32)
    for t in range(NT):
        row_x = jnp.where(lane == t, sx_ref[t], row_x)
        row_y = jnp.where(lane == t, sy_ref[t], row_y)
    freq = iota((KS, 128), 0) - HALF
    sin_x, cos_x = turns_sin_cos(freq * row_x[0:1])
    sin_y, cos_y = turns_sin_cos(freq * row_y[0:1])
    wide_lane = iota((KS, 128), 1)
    ephase[0:KS] = jnp.where(wide_lane < NT, cos_y, -sin_y)[:, : 2 * NT].astype(BF16)
    ephase[KS:] = jnp.where(wide_lane < NT, sin_y, cos_y)[:, : 2 * NT].astype(BF16)
    t_cos = cos_x.T[0:NT]
    t_sin = sin_x.T[0:NT]
    table = jnp.concatenate([t_cos, t_sin], 1)
    table_hi = table.astype(BF16)
    table_lo = (table - table_hi.astype(F32)).astype(BF16)
    small[4].wait()
    weights = weights_ref[...]
    weights_hi = weights.astype(BF16)
    weights_lo = (weights - weights_hi.astype(F32)).astype(BF16)
    h = dot(weights_hi, table_hi) + dot(weights_lo, table_hi) + dot(weights_hi, table_lo)
    h = h.astype(BF16).reshape(P_DEV * ORIENT, NT, 2 * KS)
    hs[:, 0:NT] = h[:, :, 0:KS]
    hs[:, NT:] = h[:, :, KS:]
    for o in range(ORIENT):
        rank = ranks[o]
        row = owner[o : o + 1]
        at_t = (row & 1) * 128 + (rank >> 3) * 64 + (row >> 1) * 8 + (rank & 7)
        place_t[o] = (iota((KS, KS), 0) == at_t).astype(F32).astype(BF16)

    freq_row = (iota((8, KS), 1) - HALF).astype(F32)
    which = iota((8, KS), 0)
    focus = jnp.zeros((8, KS), F32)
    small[3].wait()
    for p in range(P_DEV):
        focus = jnp.where(which == p, defocus_ref[p], focus)
    sin_d, cos_d = angle_sin_cos(focus * (freq_row * freq_row * (1.0 / (HALF * HALF))))
    sin_col = sin_d.T
    cos_col = cos_d.T
    u_row = 0.1 * sin_d - 0.995 * cos_d
    v_row = -0.995 * sin_d - 0.1 * cos_d
    loads[2].wait()
    loads[3].wait()
    for p in range(P_DEV):
        for j in range(2):
            at = slice(j * 128, j * 128 + 128)
            split[...] = ibuf.at[j, p].reshape(2 * KS, 128)[...].astype(F32)
            ctf = (
                sin_col[:, p : p + 1] * u_row[p : p + 1, at]
                + cos_col[:, p : p + 1] * v_row[p : p + 1, at]
            )
            cx[p, 0, :, at] = ctf * split[pl.ds(0, KS, stride=2), :]
            cx[p, 1, :, at] = ctf * split[pl.ds(1, KS, stride=2), :]

    def placed_term(o):
        for block in range(2):
            at = slice(block * 128, block * 128 + 128)
            low = slice(KS + block * 128, KS + block * 128 + 128)
            t_re = None
            for p in range(P_DEV):
                table_h = hs[p * ORIENT + o]
                g_re = dot(ephase[at], table_h)
                g_im = dot(ephase[low], table_h)
                c_re = cx[p, 0, at]
                c_im = cx[p, 1, at]
                if t_re is None:
                    t_re = c_re * g_re - c_im * g_im
                    t_im = c_re * g_im + c_im * g_re
                else:
                    t_re += c_re * g_re - c_im * g_im
                    t_im += c_re * g_im + c_im * g_re
            term[at, 0:KS] = t_re.astype(BF16)
            term[at, KS:] = t_im.astype(BF16)
        return dot(place_t[o], term[...])

    def pair_copy(j):
        return pltpu.make_async_remote_copy(
            src_ref=sent.at[j],
            dst_ref=landed.at[j],
            send_sem=p_send.at[j],
            recv_sem=p_recv.at[j],
            device_id=partner,
            device_id_type=MESH,
        )

    def x_copy(j, k):
        return pltpu.make_async_remote_copy(
            src_ref=xsend.at[j, lax.rem(x + k, 4)],
            dst_ref=xrecv.at[j, x],
            send_sem=x_send.at[j],
            recv_sem=x_recv.at[j],
            device_id=x_peer(k),
            device_id_type=MESH,
        )

    def y_copy(j, k):
        return pltpu.make_async_remote_copy(
            src_ref=ysend.at[j, lax.rem(y + k, YS)],
            dst_ref=yrecv.at[j, y],
            send_sem=y_send.at[j],
            recv_sem=y_recv.at[j],
            device_id=y_peer(k),
            device_id_type=MESH,
        )

    def z_copy(j, k):
        return pltpu.make_async_remote_copy(
            src_ref=zsend.at[j],
            dst_ref=zrecv.at[j, z],
            send_sem=z_send.at[j],
            recv_sem=z_recv.at[j],
            device_id=z_peer(k),
            device_id_type=MESH,
        )

    def give(j, carry):
        sent[j] = placed_term(2 * (1 - c) + j).astype(BF16)
        pair_copy(j).start()
        return carry

    lax.fori_loop(0, 2, give, 0)

    def keep(j, carry):
        mine = placed_term(2 * c + j)
        pair_copy(j).wait_recv()
        both = (mine + landed[j].astype(F32)).astype(BF16)
        xsend[j] = both.reshape(4, 64, 2 * KS)

        def send_x(k, inner):
            x_copy(j, k).start()
            return inner

        lax.fori_loop(1, 4, send_x, 0, unroll=True)
        xrecv[j, x] = xsend[j, x]
        return carry

    lax.fori_loop(0, 2, keep, 0)

    def wait_rows(n, sem):
        part = arrived.at[0, pl.ds(0, n)]
        pltpu.make_async_copy(part, part, sem).wait()

    def pass_rows(o, sem, first=0, n=SLABS, to=partner):
        part = arrived.at[o, pl.ds(first, n)]
        return pltpu.make_async_remote_copy(
            src_ref=part,
            dst_ref=part,
            send_sem=s_send.at[sem],
            recv_sem=s_recv.at[sem],
            device_id=to,
            device_id_type=MESH,
        )

    wait_rows(SLABS - 1, s_recv.at[0])
    to_up = pass_rows(o_own, 2, 0, 8, z_peer(1))
    to_down = pass_rows(o_own, 3, 8, 8, z_peer(ZS - 1))
    to_partner = pass_rows(o_own, 1)
    to_up.start()
    to_down.start()
    to_partner.start()

    for o in range(ORIENT):
        at_s = owner[o : o + 1] * OWNED + ranks[o]
        place_s[o] = (iota((KS, KS), 0) == at_s).astype(F32).astype(BF16)
    group = wide_lane // NT
    for o in range(ORIENT):
        cos_o = jnp.where(group == o, cos_x, 0.0).astype(BF16)
        sin_o = jnp.where(group == o, sin_x, 0.0).astype(BF16)
        at = (o // 2) * 2 * KS
        fx[o % 2, at : at + KS, 0:128] = cos_o
        fx[o % 2, at : at + KS, 128:] = -sin_o
        fx[o % 2, at + KS : at + 2 * KS, 0:128] = sin_o
        fx[o % 2, at + KS : at + 2 * KS, 128:] = cos_o
    table_y = jnp.concatenate([cos_y.T[0:NT], sin_y.T[0:NT]], 1) * (1.0 / KS)
    fy_hi = table_y.astype(BF16)
    fy[0:NT] = fy_hi
    fy[NT:] = (table_y - fy_hi.astype(F32)).astype(BF16)

    def correlate(parity, first):
        for j in range(2):
            o = 2 * j + parity
            su[j] = dot_t(place_s[o], arrived[o].reshape(KS, 2 * KS))
        for block in range(2):
            at = slice(block * 128, block * 128 + 128)
            for p in range(P_DEV):
                c_re = cx[p, 0, at]
                c_im = cx[p, 1, at]
                q = []
                for j in range(2):
                    s_re = su[j, at, 0:KS]
                    s_im = su[j, at, KS:]
                    q.append((s_re * c_re + s_im * c_im).astype(BF16))
                    q.append((s_re * c_im - s_im * c_re).astype(BF16))
                part = dot(jnp.concatenate(q, 1), fx[parity])
                if first:
                    zacc[p, at] = part
                else:
                    zacc[p, at] += part

    line_row = jnp.concatenate([2 * own_line, 2 * own_line + 1], 0).astype(F32)
    line_row = jnp.broadcast_to(line_row, (128, 128)).T[0:8].astype(jnp.int32)
    line_ref[...] = line_row
    outs = [pltpu.make_async_copy(line_ref, line_hbm, out_sem.at[0])]
    outs[0].start()
    wait_rows(SLABS, s_recv.at[1])
    correlate(z % 2, True)
    def pass_on(j, carry):
        pltpu.make_async_copy(
            xrecv.at[j, pl.ds(0, 3)], xrecv.at[j, pl.ds(0, 3)], x_recv.at[j]
        ).wait()
        for part in range(2):
            at = slice(part * KS, part * KS + KS)
            total = xrecv[j, 0, :, at].astype(F32)
            for other in range(1, 4):
                total += xrecv[j, other, :, at].astype(F32)
            tile_y[:, part * 8 : part * 8 + 8] = total.reshape(YS, 8, KS)
        ysend[j] = tile_y[...].astype(BF16)

        def send_y(k, inner):
            y_copy(j, k).start()
            return inner

        lax.fori_loop(1, YS, send_y, 0, unroll=True)
        yrecv[j, y] = ysend[j, y]
        return carry

    lax.fori_loop(0, 2, pass_on, 0)
    wait_rows(8, s_recv.at[2])
    wait_rows(8, s_recv.at[3])
    to_partner_too = pass_rows(2 * c + 1 - z % 2, 4)
    to_partner_too.start()

    def spread(j, carry):
        pltpu.make_async_copy(
            yrecv.at[j, pl.ds(0, YS - 1)], yrecv.at[j, pl.ds(0, YS - 1)], y_recv.at[j]
        ).wait()
        total = yrecv[j, 0].astype(F32)
        for other in range(1, YS):
            total += yrecv[j, other].astype(F32)
        zsend[j] = total.astype(BF16)

        def send_z(k, inner):
            z_copy(j, k).start()
            return inner

        lax.fori_loop(1, ZS, send_z, 0, unroll=True)
        zrecv[j, z] = zsend[j]
        return carry

    lax.fori_loop(0, 2, spread, 0)
    wait_rows(SLABS, s_recv.at[4])
    correlate(1 - z % 2, False)

    place = x_lo * 2 + c
    for j in range(2):
        pltpu.make_async_copy(
            zrecv.at[j, pl.ds(0, ZS - 1)], zrecv.at[j, pl.ds(0, ZS - 1)], z_recv.at[j]
        ).wait()
        total = zrecv[j, 0].astype(F32)
        for other in range(1, ZS):
            total += zrecv[j, other].astype(F32)
        fin[place, j] = (total * SCALE).astype(BF16)

    def group_copy(k):
        return pltpu.make_async_remote_copy(
            src_ref=fin.at[place],
            dst_ref=fin.at[place],
            send_sem=f_send.at[0],
            recv_sem=f_recv.at[0],
            device_id=group_peer(k),
            device_id_type=MESH,
        )

    for k in range(1, 4):
        group_copy(k).start()
    for p in range(P_DEV):
        full = jnp.concatenate([zacc[p, :, 0:128], zacc[p, :, 128:]], 0)
        full_hi = full.astype(BF16)
        full_lo = (full - full_hi.astype(F32)).astype(BF16)
        both = dot(fy[...], full_hi)
        scores_ref[p] = both[0:NT] + both[NT:] + dot(fy[0:NT], full_lo)
    outs.append(pltpu.make_async_copy(scores_ref, scores_hbm, out_sem.at[1]))
    outs[1].start()

    pltpu.make_async_copy(fin.at[pl.ds(0, 3)], fin.at[pl.ds(0, 3)], f_recv.at[0]).wait()
    outs.append(pltpu.make_async_copy(fin, rows_hbm, out_sem.at[2]))
    outs[2].start()

    wait_rows(SLABS - 1, s_send.at[0])
    for sent_rows in (to_partner, to_up, to_down, to_partner_too):
        sent_rows.wait_send()
    for j in range(2):
        pair_copy(j).wait_send()
    for j in range(2):
        pltpu.make_async_copy(
            xrecv.at[j, pl.ds(0, 3)], xrecv.at[j, pl.ds(0, 3)], x_send.at[j]
        ).wait()
    for j in range(2):
        pltpu.make_async_copy(
            yrecv.at[j, pl.ds(0, YS - 1)], yrecv.at[j, pl.ds(0, YS - 1)], y_send.at[j]
        ).wait()
        pltpu.make_async_copy(
            zrecv.at[j, pl.ds(0, ZS - 1)], zrecv.at[j, pl.ds(0, ZS - 1)], z_send.at[j]
        ).wait()
    pltpu.make_async_copy(fin.at[pl.ds(0, 3)], fin.at[pl.ds(0, 3)], f_send.at[0]).wait()
    for out in outs:
        out.wait()


def finish(
    fin_hbm, line_hbm, found_hbm, scores_hbm, update_hbm,
    fin_ref, line_ref, found_ref, scores_ref, insert, rows, buf, in_sem, out_sem,
):
    loads = [
        pltpu.make_async_copy(src, dst, in_sem.at[i])
        for i, (src, dst) in enumerate(
            ((line_hbm, line_ref), (fin_hbm, fin_ref), (found_hbm, found_ref))
        )
    ]
    for load in loads:
        load.start()
    loads[0].wait()
    insert[...] = (iota((2 * LINES, 128), 0) == line_ref[0:1]).astype(F32).astype(BF16)
    loads[1].wait()
    for o in range(ORIENT):
        for r in range(2):
            got = fin_ref[r * 2 + o // 2, o % 2].astype(F32)
            for part in range(2):
                first = part * 64 + o * OWNED + r * 8
                rows[first : first + 8] = got[part * 8 : part * 8 + 8]
    rows_bf16 = rows[...].astype(BF16)
    outs = []
    for piece in range(4):
        of = pl.ds(piece * 256, 256)
        at = slice(piece * 512, piece * 512 + 512)
        placed = dot(insert[at], rows_bf16).astype(BF16)
        for j in range(2):
            buf.at[j, of].reshape(512, 128)[...] = placed[:, j * 128 : j * 128 + 128]
            outs.append(
                pltpu.make_async_copy(
                    buf.at[j, of],
                    update_hbm.at[of, :, pl.ds(j * 128, 128)],
                    out_sem.at[piece * 2 + j],
                )
            )
            outs[-1].start()
    loads[2].wait()
    for o in range(ORIENT):
        scores_ref[:, o] = found_ref[:, :, o * NT : (o + 1) * NT]
    outs.append(pltpu.make_async_copy(scores_ref, scores_hbm, out_sem.at[8]))
    outs[-1].start()
    for out in outs:
        out.wait()


def body(volume, images, defocus, soft_weights, slice_lines, shift_y, shift_x):
    hbm = pl.BlockSpec(memory_space=pltpu.HBM)
    dma = pltpu.SemaphoreType.DMA
    found, rows, line = pl.pallas_call(
        kernel,
        out_shape=(
            jax.ShapeDtypeStruct((P_DEV, NT, ORIENT * NT), F32),
            jax.ShapeDtypeStruct((4, 2, 16, KS), BF16),
            jax.ShapeDtypeStruct((8, 128), jnp.int32),
        ),
        in_specs=[hbm] * 7,
        out_specs=(hbm, hbm, hbm),
        scratch_shapes=[
            pltpu.VMEM((P_DEV, NT, ORIENT * NT), F32),
            pltpu.VMEM((8, 128), jnp.int32),
            pltpu.VMEM((ORIENT, KS), jnp.int32),
            pltpu.VMEM((P_DEV * ORIENT * NT, NT), F32),
            pltpu.SMEM((P_DEV,), F32),
            pltpu.SMEM((NT,), jnp.int32),
            pltpu.SMEM((NT,), jnp.int32),
            pltpu.VMEM((2, LINES, 2, 128), BF16),
            pltpu.VMEM((2, P_DEV, KS, 2, 128), BF16),
            pltpu.VMEM((2 * KS, 128), F32),
            pltpu.VMEM((OWNED, 2 * KS), BF16),
            pltpu.VMEM((ORIENT, SLABS, OWNED, 2 * KS), BF16),
            pltpu.VMEM((2 * OWNED, 2 * LINES), BF16),
            pltpu.VMEM((ORIENT, KS, KS), BF16),
            pltpu.VMEM((ORIENT, KS, KS), BF16),
            pltpu.VMEM((2, 4 * KS, 256), BF16),
            pltpu.VMEM((2 * KS, 2 * NT), BF16),
            pltpu.VMEM((2 * NT, 2 * KS), BF16),
            pltpu.VMEM((P_DEV * ORIENT, 2 * NT, KS), BF16),
            pltpu.VMEM((P_DEV, 2, KS, KS), F32),
            pltpu.VMEM((KS, 2 * KS), BF16),
            pltpu.VMEM((2, KS, 2 * KS), BF16),
            pltpu.VMEM((2, KS, 2 * KS), BF16),
            pltpu.VMEM((2, 4, 64, 2 * KS), BF16),
            pltpu.VMEM((2, 4, 64, 2 * KS), BF16),
            pltpu.VMEM((2, YS, 16, KS), BF16),
            pltpu.VMEM((2, YS, 16, KS), BF16),
            pltpu.VMEM((2, 16, KS), BF16),
            pltpu.VMEM((2, ZS, 16, KS), BF16),
            pltpu.VMEM((4, 2, 16, KS), BF16),
            pltpu.VMEM((YS, 16, KS), F32),
            pltpu.VMEM((P_DEV, KS, 256), F32),
            pltpu.VMEM((2, KS, 2 * KS), F32),
            dma((5,)),
            dma((4,)),
            dma((3,)),
            dma((5,)),
            dma((5,)),
            dma((2,)),
            dma((2,)),
            dma((2,)),
            dma((2,)),
            dma((2,)),
            dma((2,)),
            dma((2,)),
            dma((2,)),
            dma((1,)),
            dma((1,)),
        ],
        compiler_params=pltpu.CompilerParams(
            collective_id=0, has_side_effects=True, vmem_limit_bytes=60 * 1024 * 1024
        ),
        name="cryo",
    )(
        slice_lines,
        soft_weights.reshape(P_DEV * ORIENT * NT, NT),
        defocus,
        shift_y,
        shift_x,
        volume,
        images,
    )
    return pl.pallas_call(
        finish,
        out_shape=(
            jax.ShapeDtypeStruct((P_DEV, ORIENT, NT, NT), F32),
            jax.ShapeDtypeStruct((LINES, 2, KS), BF16),
        ),
        in_specs=[hbm] * 3,
        out_specs=(hbm, hbm),
        scratch_shapes=[
            pltpu.VMEM((4, 2, 16, KS), BF16),
            pltpu.VMEM((8, 128), jnp.int32),
            pltpu.VMEM((P_DEV, NT, ORIENT * NT), F32),
            pltpu.VMEM((P_DEV, ORIENT, NT, NT), F32),
            pltpu.VMEM((2 * LINES, 2 * ORIENT * OWNED), BF16),
            pltpu.VMEM((2 * ORIENT * OWNED, KS), F32),
            pltpu.VMEM((2, LINES, 2, 128), BF16),
            dma((3,)),
            dma((9,)),
        ],
        compiler_params=pltpu.CompilerParams(vmem_limit_bytes=60 * 1024 * 1024),
        name="finish",
    )(rows, line, found)


def solution(mesh):
    placed = (
        P("slab", None, None),
        P(("dom", "slab"), None, None, None),
        P(("dom", "slab")),
        P(("dom", "slab"), None, None, None),
        P(),
        P(),
        P(),
    )
    return jax.shard_map(
        body,
        mesh=mesh,
        in_specs=placed,
        out_specs=(P(("dom", "slab"), None, None, None), P("slab", None, None)),
        check_vma=False,
    )
```

```python
import math

import jax
import jax.numpy as jnp
from jax import lax
from jax.experimental import pallas as pl
from jax.experimental.pallas import tpu as pltpu
from jax.sharding import PartitionSpec as P

KS = 256
HALF = KS // 2
P_DEV = 4
LINES = 1024
ORIENT = 4
NT = 32
OWNED = 16
PARTICLES = 2048
SLABS = 16
ZS = 8
YS = 8
XLO = 2
SCALE = 1.0 / math.sqrt(NT * NT * PARTICLES)
F32 = jnp.float32
BF16 = jnp.bfloat16
MESH = pl.DeviceIdType.MESH


def dot(a, b):
    return jnp.dot(a, b, preferred_element_type=F32)


def dot_t(a, b):
    return lax.dot_general(a, b, (((0,), (0,)), ((), ())), preferred_element_type=F32)


def poly_sin_cos(r):
    s = r * r
    sin = r * (1.0 + s * (-1 / 6 + s * (1 / 120 + s * (-1 / 5040 + s * (1 / 362880)))))
    cos = 1.0 + s * (-0.5 + s * (1 / 24 + s * (-1 / 720 + s * (1 / 40320))))
    return sin, cos


def rotate(quadrant, sin, cos):
    q = quadrant & 3
    odd = (q & 1) == 1
    s = jnp.where(odd, cos, sin)
    c = jnp.where(odd, sin, cos)
    s = jnp.where(q >= 2, -s, s)
    c = jnp.where((q == 1) | (q == 2), -c, c)
    return s, c


def turns_sin_cos(turns):
    t = turns & (KS - 1)
    q = (t + KS // 8) >> 6
    r = (t - (q << 6)).astype(F32) * (2.0 * math.pi / KS)
    return rotate(q, *poly_sin_cos(r))


def angle_sin_cos(x):
    n = jnp.floor(x * (2.0 / math.pi) + 0.5)
    r = x - n * 1.5703125
    r = r - n * 4.837512969970703e-4
    r = r - n * 7.549789948768648e-8
    return rotate(n.astype(jnp.int32), *poly_sin_cos(r))


def iota(shape, dim):
    return lax.broadcasted_iota(jnp.int32, shape, dim)


def kernel(
    lines_hbm, weights_hbm, defocus_hbm, sy_hbm, sx_hbm, volume_hbm, images_hbm,
    scores_hbm, rows_hbm, line_hbm,
    scores_ref, line_ref, lines_ref, weights_ref, defocus_ref, sy_ref, sx_ref,
    vbuf, ibuf, split, own, arrived, gather, place_s, place_t,
    fx, ephase, fy, hs, cx, term, sent, landed, xsend, xrecv, ysend, yrecv, zsend, zrecv,
    fin, tile_y, zacc, su,
    small_sem, in_sem, out_sem, s_send, s_recv, p_send, p_recv, x_send, x_recv, z_send, z_recv,
    y_send, y_recv, f_send, f_recv,
):
    dom = lax.axis_index("dom")
    slab = lax.axis_index("slab")
    x_lo = dom // 16
    z = (dom // 2) % 8
    c = dom % 2
    zc = z * 2 + c
    partner = (dom + 1 - 2 * c, slab)
    y = slab // 2
    x_hi = slab % 2
    x = x_hi * 2 + x_lo

    small = [
        pltpu.make_async_copy(src, dst, small_sem.at[i])
        for i, (src, dst) in enumerate(
            (
                (lines_hbm, lines_ref),
                (sx_hbm, sx_ref),
                (sy_hbm, sy_ref),
                (defocus_hbm, defocus_ref),
                (weights_hbm, weights_ref),
            )
        )
    ]
    for load in small:
        load.start()
    loads = []
    for j in range(2):
        cols = pl.ds(j * 128, 128)
        loads.append(pltpu.make_async_copy(volume_hbm.at[:, :, cols], vbuf.at[j], in_sem.at[j]))
    for j in range(2):
        cols = pl.ds(j * 128, 128)
        loads.append(
            pltpu.make_async_copy(images_hbm.at[:, :, :, cols], ibuf.at[j], in_sem.at[2 + j])
        )
    for load in loads:
        load.start()

    barrier = pltpu.get_barrier_semaphore()

    def slab_peer(k):
        to = lax.rem(slab + k, SLABS)
        flip = (to % 2 + x_hi) % 2
        return ((x_lo + flip) % 2) * 16 + zc, to

    def x_peer(k):
        to = lax.rem(x + k, 4)
        return (to % 2) * 16 + zc, y * 2 + to // 2

    def y_peer(k):
        return dom, lax.rem(y + k, YS) * 2 + x_hi

    def z_peer(k):
        return x_lo * 16 + lax.rem(z + k, ZS) * 2 + c, slab

    def group_peer(k):
        to = lax.rem(x_lo * 2 + c + k, 4)
        return (to // 2) * 16 + z * 2 + to % 2, slab

    def greet(peer):
        pl.semaphore_signal(barrier, inc=1, device_id=peer, device_id_type=MESH)

    def greet_slab(k, carry):
        greet(slab_peer(k))
        return carry

    def greet_z(k, carry):
        greet(z_peer(k))
        return carry

    lax.fori_loop(1, SLABS, greet_slab, 0)
    lax.fori_loop(1, ZS, greet_z, 0)
    for k in range(1, 4):
        greet(group_peer(k))
    greet((dom, y * 2 + 1 - x_hi))

    small[0].wait()
    lines = lines_ref[...]
    owner = lines >> 10
    local = (lines & (LINES - 1)).astype(F32)
    slab_rows = iota((SLABS, KS), 0)
    marks = jnp.concatenate(
        [(owner[o : o + 1] == slab_rows).astype(F32) for o in range(ORIENT)], 0
    )
    before = (iota((KS, KS), 0) < iota((KS, KS), 1)).astype(F32).astype(BF16)
    earlier = dot(marks.astype(BF16), before) * marks
    ranks = [
        jnp.sum(earlier[o * SLABS : (o + 1) * SLABS], axis=0, keepdims=True).astype(jnp.int32)
        for o in range(ORIENT)
    ]
    own_line = []
    for o in range(ORIENT):
        mine = (owner[o : o + 1] == slab) & (ranks[o] == slab_rows)
        own_line.append(
            jnp.sum(jnp.where(mine, local[o : o + 1], 0.0), axis=1, keepdims=True)
        )
    own_line = jnp.concatenate(own_line, 0).astype(jnp.int32)
    o_own = 2 * c + z % 2
    first_line = own_line[0:OWNED]
    for o in range(1, ORIENT):
        first_line = jnp.where(o_own == o, own_line[o * OWNED : (o + 1) * OWNED], first_line)
    column = iota((OWNED, 2 * LINES), 1)
    gather[0:OWNED] = (column == 2 * first_line).astype(F32).astype(BF16)
    gather[OWNED:] = (column == 2 * first_line + 1).astype(F32).astype(BF16)

    for j in range(2):
        loads[j].wait()
        picked = dot(gather[...], vbuf.at[j].reshape(2 * LINES, 128)[...]).astype(BF16)
        for part in range(2):
            at = slice(part * KS + j * 128, part * KS + j * 128 + 128)
            own[:, at] = picked[part * OWNED : part * OWNED + OWNED]

    small[1].wait()
    small[2].wait()
    lane = iota((8, 128), 1) % NT
    row_x = jnp.zeros((8, 128), jnp.int32)
    row_y = jnp.zeros((8, 128), jnp.int32)
    for t in range(NT):
        row_x = jnp.where(lane == t, sx_ref[t], row_x)
        row_y = jnp.where(lane == t, sy_ref[t], row_y)
    freq = iota((KS, 128), 0) - HALF
    sin_x, cos_x = turns_sin_cos(freq * row_x[0:1])
    sin_y, cos_y = turns_sin_cos(freq * row_y[0:1])
    wide_lane = iota((KS, 128), 1)
    ephase[0:KS] = jnp.where(wide_lane < NT, cos_y, -sin_y)[:, : 2 * NT].astype(BF16)
    ephase[KS:] = jnp.where(wide_lane < NT, sin_y, cos_y)[:, : 2 * NT].astype(BF16)
    t_cos = cos_x.T[0:NT]
    t_sin = sin_x.T[0:NT]
    table = jnp.concatenate([t_cos, t_sin], 1)
    table_hi = table.astype(BF16)
    table_lo = (table - table_hi.astype(F32)).astype(BF16)
    small[4].wait()
    weights = weights_ref[...]
    weights_hi = weights.astype(BF16)
    weights_lo = (weights - weights_hi.astype(F32)).astype(BF16)
    h = dot(weights_hi, table_hi) + dot(weights_lo, table_hi) + dot(weights_hi, table_lo)
    h = h.astype(BF16).reshape(P_DEV * ORIENT, NT, 2 * KS)
    hs[:, 0:NT] = h[:, :, 0:KS]
    hs[:, NT:] = h[:, :, KS:]
    for o in range(ORIENT):
        rank = ranks[o]
        row = owner[o : o + 1]
        at_t = (row & 1) * 128 + (rank >> 3) * 64 + (row >> 1) * 8 + (rank & 7)
        place_t[o] = (iota((KS, KS), 0) == at_t).astype(F32).astype(BF16)

    freq_row = (iota((8, KS), 1) - HALF).astype(F32)
    which = iota((8, KS), 0)
    focus = jnp.zeros((8, KS), F32)
    small[3].wait()
    for p in range(P_DEV):
        focus = jnp.where(which == p, defocus_ref[p], focus)
    sin_d, cos_d = angle_sin_cos(focus * (freq_row * freq_row * (1.0 / (HALF * HALF))))
    sin_col = sin_d.T
    cos_col = cos_d.T
    u_row = 0.1 * sin_d - 0.995 * cos_d
    v_row = -0.995 * sin_d - 0.1 * cos_d
    loads[2].wait()
    loads[3].wait()
    for p in range(P_DEV):
        for j in range(2):
            at = slice(j * 128, j * 128 + 128)
            split[...] = ibuf.at[j, p].reshape(2 * KS, 128)[...].astype(F32)
            ctf = (
                sin_col[:, p : p + 1] * u_row[p : p + 1, at]
                + cos_col[:, p : p + 1] * v_row[p : p + 1, at]
            )
            cx[p, 0, :, at] = ctf * split[pl.ds(0, KS, stride=2), :]
            cx[p, 1, :, at] = ctf * split[pl.ds(1, KS, stride=2), :]

    def placed_term(o):
        for block in range(2):
            at = slice(block * 128, block * 128 + 128)
            low = slice(KS + block * 128, KS + block * 128 + 128)
            t_re = None
            for p in range(P_DEV):
                table_h = hs[p * ORIENT + o]
                g_re = dot(ephase[at], table_h)
                g_im = dot(ephase[low], table_h)
                c_re = cx[p, 0, at]
                c_im = cx[p, 1, at]
                if t_re is None:
                    t_re = c_re * g_re - c_im * g_im
                    t_im = c_re * g_im + c_im * g_re
                else:
                    t_re += c_re * g_re - c_im * g_im
                    t_im += c_re * g_im + c_im * g_re
            term[at, 0:KS] = t_re.astype(BF16)
            term[at, KS:] = t_im.astype(BF16)
        return dot(place_t[o], term[...])

    def pair_copy(j):
        return pltpu.make_async_remote_copy(
            src_ref=sent.at[j],
            dst_ref=landed.at[j],
            send_sem=p_send.at[j],
            recv_sem=p_recv.at[j],
            device_id=partner,
            device_id_type=MESH,
        )

    def x_copy(j, k):
        return pltpu.make_async_remote_copy(
            src_ref=xsend.at[j, lax.rem(x + k, 4)],
            dst_ref=xrecv.at[j, x],
            send_sem=x_send.at[j],
            recv_sem=x_recv.at[j],
            device_id=x_peer(k),
            device_id_type=MESH,
        )

    def y_copy(j, k):
        return pltpu.make_async_remote_copy(
            src_ref=ysend.at[j, lax.rem(y + k, YS)],
            dst_ref=yrecv.at[j, y],
            send_sem=y_send.at[j],
            recv_sem=y_recv.at[j],
            device_id=y_peer(k),
            device_id_type=MESH,
        )

    def z_copy(j, k):
        return pltpu.make_async_remote_copy(
            src_ref=zsend.at[j],
            dst_ref=zrecv.at[j, z],
            send_sem=z_send.at[j],
            recv_sem=z_recv.at[j],
            device_id=z_peer(k),
            device_id_type=MESH,
        )

    def give(j, carry):
        sent[j] = placed_term(2 * (1 - c) + j).astype(BF16)
        return carry

    lax.fori_loop(0, 2, give, 0)

    pl.semaphore_wait(barrier, SLABS - 1 + ZS - 1 + 3 + 1)

    pair_copy(0).start()
    pair_copy(1).start()

    def slab_copy(k):
        return pltpu.make_async_remote_copy(
            src_ref=own,
            dst_ref=arrived.at[o_own, slab],
            send_sem=s_send.at[0],
            recv_sem=s_recv.at[0],
            device_id=slab_peer(k),
            device_id_type=MESH,
        )

    def send_slab(k, carry):
        slab_copy(k).start()
        return carry

    lax.fori_loop(1, SLABS, send_slab, 0)
    arrived[o_own, slab] = own[...]


    def keep(j, carry):
        mine = placed_term(2 * c + j)
        pair_copy(j).wait_recv()
        both = (mine + landed[j].astype(F32)).astype(BF16)
        xsend[j] = both.reshape(4, 64, 2 * KS)

        def send_x(k, inner):
            x_copy(j, k).start()
            return inner

        lax.fori_loop(1, 4, send_x, 0)
        xrecv[j, x] = xsend[j, x]
        return carry

    lax.fori_loop(0, 2, keep, 0)

    def wait_rows(n, sem):
        part = arrived.at[0, pl.ds(0, n)]
        pltpu.make_async_copy(part, part, sem).wait()

    def pass_rows(o, sem, first=0, n=SLABS, to=partner):
        part = arrived.at[o, pl.ds(first, n)]
        return pltpu.make_async_remote_copy(
            src_ref=part,
            dst_ref=part,
            send_sem=s_send.at[sem],
            recv_sem=s_recv.at[sem],
            device_id=to,
            device_id_type=MESH,
        )

    wait_rows(SLABS - 1, s_recv.at[0])
    to_up = pass_rows(o_own, 2, 0, 8, z_peer(1))
    to_down = pass_rows(o_own, 3, 8, 8, z_peer(ZS - 1))
    to_partner = pass_rows(o_own, 1)
    to_up.start()
    to_down.start()
    to_partner.start()

    for o in range(ORIENT):
        at_s = owner[o : o + 1] * OWNED + ranks[o]
        place_s[o] = (iota((KS, KS), 0) == at_s).astype(F32).astype(BF16)
    group = wide_lane // NT
    for o in range(ORIENT):
        cos_o = jnp.where(group == o, cos_x, 0.0).astype(BF16)
        sin_o = jnp.where(group == o, sin_x, 0.0).astype(BF16)
        at = (o // 2) * 2 * KS
        fx[o % 2, at : at + KS, 0:128] = cos_o
        fx[o % 2, at : at + KS, 128:] = -sin_o
        fx[o % 2, at + KS : at + 2 * KS, 0:128] = sin_o
        fx[o % 2, at + KS : at + 2 * KS, 128:] = cos_o
    table_y = jnp.concatenate([cos_y.T[0:NT], sin_y.T[0:NT]], 1) * (1.0 / KS)
    fy_hi = table_y.astype(BF16)
    fy[0:NT] = fy_hi
    fy[NT:] = (table_y - fy_hi.astype(F32)).astype(BF16)

    def correlate(parity, first):
        for j in range(2):
            o = 2 * j + parity
            su[j] = dot_t(place_s[o], arrived[o].reshape(KS, 2 * KS))
        for block in range(2):
            at = slice(block * 128, block * 128 + 128)
            for p in range(P_DEV):
                c_re = cx[p, 0, at]
                c_im = cx[p, 1, at]
                q = []
                for j in range(2):
                    s_re = su[j, at, 0:KS]
                    s_im = su[j, at, KS:]
                    q.append((s_re * c_re + s_im * c_im).astype(BF16))
                    q.append((s_re * c_im - s_im * c_re).astype(BF16))
                part = dot(jnp.concatenate(q, 1), fx[parity])
                if first:
                    zacc[p, at] = part
                else:
                    zacc[p, at] += part

    line_row = jnp.concatenate([2 * own_line, 2 * own_line + 1], 0).astype(F32)
    line_row = jnp.broadcast_to(line_row, (128, 128)).T[0:8].astype(jnp.int32)
    line_ref[...] = line_row
    outs = [pltpu.make_async_copy(line_ref, line_hbm, out_sem.at[0])]
    outs[0].start()
    wait_rows(SLABS, s_recv.at[1])
    correlate(z % 2, True)
    def pass_on(j, carry):
        pltpu.make_async_copy(
            xrecv.at[j, pl.ds(0, 3)], xrecv.at[j, pl.ds(0, 3)], x_recv.at[j]
        ).wait()
        for part in range(2):
            at = slice(part * KS, part * KS + KS)
            total = xrecv[j, 0, :, at].astype(F32)
            for other in range(1, 4):
                total += xrecv[j, other, :, at].astype(F32)
            tile_y[:, part * 8 : part * 8 + 8] = total.reshape(YS, 8, KS)
        ysend[j] = tile_y[...].astype(BF16)

        def send_y(k, inner):
            y_copy(j, k).start()
            return inner

        lax.fori_loop(1, YS, send_y, 0)
        yrecv[j, y] = ysend[j, y]
        return carry

    lax.fori_loop(0, 2, pass_on, 0)
    wait_rows(8, s_recv.at[2])
    wait_rows(8, s_recv.at[3])
    to_partner_too = pass_rows(2 * c + 1 - z % 2, 4)
    to_partner_too.start()

    def spread(j, carry):
        pltpu.make_async_copy(
            yrecv.at[j, pl.ds(0, YS - 1)], yrecv.at[j, pl.ds(0, YS - 1)], y_recv.at[j]
        ).wait()
        total = yrecv[j, 0].astype(F32)
        for other in range(1, YS):
            total += yrecv[j, other].astype(F32)
        zsend[j] = total.astype(BF16)

        def send_z(k, inner):
            z_copy(j, k).start()
            return inner

        lax.fori_loop(1, ZS, send_z, 0)
        zrecv[j, z] = zsend[j]
        return carry

    lax.fori_loop(0, 2, spread, 0)
    wait_rows(SLABS, s_recv.at[4])
    correlate(1 - z % 2, False)

    place = x_lo * 2 + c
    for j in range(2):
        pltpu.make_async_copy(
            zrecv.at[j, pl.ds(0, ZS - 1)], zrecv.at[j, pl.ds(0, ZS - 1)], z_recv.at[j]
        ).wait()
        total = zrecv[j, 0].astype(F32)
        for other in range(1, ZS):
            total += zrecv[j, other].astype(F32)
        fin[place, j] = (total * SCALE).astype(BF16)

    def group_copy(k):
        return pltpu.make_async_remote_copy(
            src_ref=fin.at[place],
            dst_ref=fin.at[place],
            send_sem=f_send.at[0],
            recv_sem=f_recv.at[0],
            device_id=group_peer(k),
            device_id_type=MESH,
        )

    for k in range(1, 4):
        group_copy(k).start()
    for p in range(P_DEV):
        full = jnp.concatenate([zacc[p, :, 0:128], zacc[p, :, 128:]], 0)
        full_hi = full.astype(BF16)
        full_lo = (full - full_hi.astype(F32)).astype(BF16)
        both = dot(fy[...], full_hi)
        scores_ref[p] = both[0:NT] + both[NT:] + dot(fy[0:NT], full_lo)
    outs.append(pltpu.make_async_copy(scores_ref, scores_hbm, out_sem.at[1]))
    outs[1].start()

    pltpu.make_async_copy(fin.at[pl.ds(0, 3)], fin.at[pl.ds(0, 3)], f_recv.at[0]).wait()
    outs.append(pltpu.make_async_copy(fin, rows_hbm, out_sem.at[2]))
    outs[2].start()

    wait_rows(SLABS - 1, s_send.at[0])
    for sent_rows in (to_partner, to_up, to_down, to_partner_too):
        sent_rows.wait_send()
    for j in range(2):
        pair_copy(j).wait_send()
    for j in range(2):
        pltpu.make_async_copy(
            xrecv.at[j, pl.ds(0, 3)], xrecv.at[j, pl.ds(0, 3)], x_send.at[j]
        ).wait()
    for j in range(2):
        pltpu.make_async_copy(
            yrecv.at[j, pl.ds(0, YS - 1)], yrecv.at[j, pl.ds(0, YS - 1)], y_send.at[j]
        ).wait()
        pltpu.make_async_copy(
            zrecv.at[j, pl.ds(0, ZS - 1)], zrecv.at[j, pl.ds(0, ZS - 1)], z_send.at[j]
        ).wait()
    pltpu.make_async_copy(fin.at[pl.ds(0, 3)], fin.at[pl.ds(0, 3)], f_send.at[0]).wait()
    for out in outs:
        out.wait()


def finish(
    fin_hbm, line_hbm, found_hbm, scores_hbm, update_hbm,
    fin_ref, line_ref, found_ref, scores_ref, insert, rows, buf, in_sem, out_sem,
):
    loads = [
        pltpu.make_async_copy(src, dst, in_sem.at[i])
        for i, (src, dst) in enumerate(
            ((line_hbm, line_ref), (fin_hbm, fin_ref), (found_hbm, found_ref))
        )
    ]
    for load in loads:
        load.start()
    loads[0].wait()
    insert[...] = (iota((2 * LINES, 128), 0) == line_ref[0:1]).astype(F32).astype(BF16)
    loads[1].wait()
    for o in range(ORIENT):
        for r in range(2):
            got = fin_ref[r * 2 + o // 2, o % 2].astype(F32)
            for part in range(2):
                first = part * 64 + o * OWNED + r * 8
                rows[first : first + 8] = got[part * 8 : part * 8 + 8]
    rows_bf16 = rows[...].astype(BF16)
    outs = []
    for piece in range(4):
        of = pl.ds(piece * 256, 256)
        at = slice(piece * 512, piece * 512 + 512)
        placed = dot(insert[at], rows_bf16).astype(BF16)
        for j in range(2):
            buf.at[j, of].reshape(512, 128)[...] = placed[:, j * 128 : j * 128 + 128]
            outs.append(
                pltpu.make_async_copy(
                    buf.at[j, of],
                    update_hbm.at[of, :, pl.ds(j * 128, 128)],
                    out_sem.at[piece * 2 + j],
                )
            )
            outs[-1].start()
    loads[2].wait()
    for o in range(ORIENT):
        scores_ref[:, o] = found_ref[:, :, o * NT : (o + 1) * NT]
    outs.append(pltpu.make_async_copy(scores_ref, scores_hbm, out_sem.at[8]))
    outs[-1].start()
    for out in outs:
        out.wait()


def body(volume, images, defocus, soft_weights, slice_lines, shift_y, shift_x):
    hbm = pl.BlockSpec(memory_space=pltpu.HBM)
    dma = pltpu.SemaphoreType.DMA
    found, rows, line = pl.pallas_call(
        kernel,
        out_shape=(
            jax.ShapeDtypeStruct((P_DEV, NT, ORIENT * NT), F32),
            jax.ShapeDtypeStruct((4, 2, 16, KS), BF16),
            jax.ShapeDtypeStruct((8, 128), jnp.int32),
        ),
        in_specs=[hbm] * 7,
        out_specs=(hbm, hbm, hbm),
        scratch_shapes=[
            pltpu.VMEM((P_DEV, NT, ORIENT * NT), F32),
            pltpu.VMEM((8, 128), jnp.int32),
            pltpu.VMEM((ORIENT, KS), jnp.int32),
            pltpu.VMEM((P_DEV * ORIENT * NT, NT), F32),
            pltpu.SMEM((P_DEV,), F32),
            pltpu.SMEM((NT,), jnp.int32),
            pltpu.SMEM((NT,), jnp.int32),
            pltpu.VMEM((2, LINES, 2, 128), BF16),
            pltpu.VMEM((2, P_DEV, KS, 2, 128), BF16),
            pltpu.VMEM((2 * KS, 128), F32),
            pltpu.VMEM((OWNED, 2 * KS), BF16),
            pltpu.VMEM((ORIENT, SLABS, OWNED, 2 * KS), BF16),
            pltpu.VMEM((2 * OWNED, 2 * LINES), BF16),
            pltpu.VMEM((ORIENT, KS, KS), BF16),
            pltpu.VMEM((ORIENT, KS, KS), BF16),
            pltpu.VMEM((2, 4 * KS, 256), BF16),
            pltpu.VMEM((2 * KS, 2 * NT), BF16),
            pltpu.VMEM((2 * NT, 2 * KS), BF16),
            pltpu.VMEM((P_DEV * ORIENT, 2 * NT, KS), BF16),
            pltpu.VMEM((P_DEV, 2, KS, KS), F32),
            pltpu.VMEM((KS, 2 * KS), BF16),
            pltpu.VMEM((2, KS, 2 * KS), BF16),
            pltpu.VMEM((2, KS, 2 * KS), BF16),
            pltpu.VMEM((2, 4, 64, 2 * KS), BF16),
            pltpu.VMEM((2, 4, 64, 2 * KS), BF16),
            pltpu.VMEM((2, YS, 16, KS), BF16),
            pltpu.VMEM((2, YS, 16, KS), BF16),
            pltpu.VMEM((2, 16, KS), BF16),
            pltpu.VMEM((2, ZS, 16, KS), BF16),
            pltpu.VMEM((4, 2, 16, KS), BF16),
            pltpu.VMEM((YS, 16, KS), F32),
            pltpu.VMEM((P_DEV, KS, 256), F32),
            pltpu.VMEM((2, KS, 2 * KS), F32),
            dma((5,)),
            dma((4,)),
            dma((3,)),
            dma((5,)),
            dma((5,)),
            dma((2,)),
            dma((2,)),
            dma((2,)),
            dma((2,)),
            dma((2,)),
            dma((2,)),
            dma((2,)),
            dma((2,)),
            dma((1,)),
            dma((1,)),
        ],
        compiler_params=pltpu.CompilerParams(
            collective_id=0, has_side_effects=True, vmem_limit_bytes=60 * 1024 * 1024
        ),
        name="cryo",
    )(
        slice_lines,
        soft_weights.reshape(P_DEV * ORIENT * NT, NT),
        defocus,
        shift_y,
        shift_x,
        volume,
        images,
    )
    return pl.pallas_call(
        finish,
        out_shape=(
            jax.ShapeDtypeStruct((P_DEV, ORIENT, NT, NT), F32),
            jax.ShapeDtypeStruct((LINES, 2, KS), BF16),
        ),
        in_specs=[hbm] * 3,
        out_specs=(hbm, hbm),
        scratch_shapes=[
            pltpu.VMEM((4, 2, 16, KS), BF16),
            pltpu.VMEM((8, 128), jnp.int32),
            pltpu.VMEM((P_DEV, NT, ORIENT * NT), F32),
            pltpu.VMEM((P_DEV, ORIENT, NT, NT), F32),
            pltpu.VMEM((2 * LINES, 2 * ORIENT * OWNED), BF16),
            pltpu.VMEM((2 * ORIENT * OWNED, KS), F32),
            pltpu.VMEM((2, LINES, 2, 128), BF16),
            dma((3,)),
            dma((9,)),
        ],
        compiler_params=pltpu.CompilerParams(vmem_limit_bytes=60 * 1024 * 1024),
        name="finish",
    )(rows, line, found)


def solution(mesh):
    placed = (
        P("slab", None, None),
        P(("dom", "slab"), None, None, None),
        P(("dom", "slab")),
        P(("dom", "slab"), None, None, None),
        P(),
        P(),
        P(),
    )
    return jax.shard_map(
        body,
        mesh=mesh,
        in_specs=placed,
        out_specs=(P(("dom", "slab"), None, None, None), P("slab", None, None)),
        check_vma=False,
    )
```

```python
import math

import jax
import jax.numpy as jnp
from jax import lax
from jax.experimental import pallas as pl
from jax.experimental.pallas import tpu as pltpu
from jax.sharding import PartitionSpec as P

KS = 256
HALF = KS // 2
P_DEV = 4
LINES = 1024
ORIENT = 4
NT = 32
OWNED = 16
PARTICLES = 2048
SLABS = 16
ZS = 8
YS = 8
XLO = 2
SCALE = 1.0 / math.sqrt(NT * NT * PARTICLES)
F32 = jnp.float32
BF16 = jnp.bfloat16
MESH = pl.DeviceIdType.MESH


def dot(a, b):
    return jnp.dot(a, b, preferred_element_type=F32)


def dot_t(a, b):
    return lax.dot_general(a, b, (((0,), (0,)), ((), ())), preferred_element_type=F32)


def poly_sin_cos(r):
    s = r * r
    sin = r * (1.0 + s * (-1 / 6 + s * (1 / 120 + s * (-1 / 5040 + s * (1 / 362880)))))
    cos = 1.0 + s * (-0.5 + s * (1 / 24 + s * (-1 / 720 + s * (1 / 40320))))
    return sin, cos


def rotate(quadrant, sin, cos):
    q = quadrant & 3
    odd = (q & 1) == 1
    s = jnp.where(odd, cos, sin)
    c = jnp.where(odd, sin, cos)
    s = jnp.where(q >= 2, -s, s)
    c = jnp.where((q == 1) | (q == 2), -c, c)
    return s, c


def turns_sin_cos(turns):
    t = turns & (KS - 1)
    q = (t + KS // 8) >> 6
    r = (t - (q << 6)).astype(F32) * (2.0 * math.pi / KS)
    return rotate(q, *poly_sin_cos(r))


def angle_sin_cos(x):
    n = jnp.floor(x * (2.0 / math.pi) + 0.5)
    r = x - n * 1.5703125
    r = r - n * 4.837512969970703e-4
    r = r - n * 7.549789948768648e-8
    return rotate(n.astype(jnp.int32), *poly_sin_cos(r))


def iota(shape, dim):
    return lax.broadcasted_iota(jnp.int32, shape, dim)


def kernel(
    lines_hbm, weights_hbm, defocus_hbm, sy_hbm, sx_hbm, volume_hbm, images_hbm,
    scores_hbm, rows_hbm, line_hbm,
    scores_ref, line_ref, lines_ref, weights_ref, defocus_ref, sy_ref, sx_ref,
    vbuf, ibuf, split, own, arrived, gather, place_s, place_t,
    fx, ephase, fy, hs, cx, term, sent, landed, xsend, xrecv, ysend, yrecv, zsend, zrecv,
    fin, tile_y, zacc, su,
    small_sem, in_sem, out_sem, s_send, s_recv, p_send, p_recv, x_send, x_recv, z_send, z_recv,
    y_send, y_recv, f_send, f_recv,
):
    dom = lax.axis_index("dom")
    slab = lax.axis_index("slab")
    x_lo = dom // 16
    z = (dom // 2) % 8
    c = dom % 2
    zc = z * 2 + c
    partner = (dom + 1 - 2 * c, slab)
    y = slab // 2
    x_hi = slab % 2
    x = x_hi * 2 + x_lo

    small = [
        pltpu.make_async_copy(src, dst, small_sem.at[i])
        for i, (src, dst) in enumerate(
            (
                (lines_hbm, lines_ref),
                (sx_hbm, sx_ref),
                (sy_hbm, sy_ref),
                (defocus_hbm, defocus_ref),
                (weights_hbm, weights_ref),
            )
        )
    ]
    for load in small:
        load.start()
    loads = []
    for j in range(2):
        cols = pl.ds(j * 128, 128)
        loads.append(pltpu.make_async_copy(volume_hbm.at[:, :, cols], vbuf.at[j], in_sem.at[j]))
    for j in range(2):
        cols = pl.ds(j * 128, 128)
        loads.append(
            pltpu.make_async_copy(images_hbm.at[:, :, :, cols], ibuf.at[j], in_sem.at[2 + j])
        )
    for load in loads:
        load.start()

    barrier = pltpu.get_barrier_semaphore()

    def slab_peer(k):
        to = lax.rem(slab + k, SLABS)
        flip = (to % 2 + x_hi) % 2
        return ((x_lo + flip) % 2) * 16 + zc, to

    def x_peer(k):
        to = lax.rem(x + k, 4)
        return (to % 2) * 16 + zc, y * 2 + to // 2

    def y_peer(k):
        return dom, lax.rem(y + k, YS) * 2 + x_hi

    def z_peer(k):
        return x_lo * 16 + lax.rem(z + k, ZS) * 2 + c, slab

    def group_peer(k):
        to = lax.rem(x_lo * 2 + c + k, 4)
        return (to // 2) * 16 + z * 2 + to % 2, slab

    def greet(peer):
        pl.semaphore_signal(barrier, inc=1, device_id=peer, device_id_type=MESH)

    def greet_slab(k, carry):
        greet(slab_peer(k))
        return carry

    def greet_z(k, carry):
        greet(z_peer(k))
        return carry

    lax.fori_loop(1, SLABS, greet_slab, 0)
    lax.fori_loop(1, ZS, greet_z, 0)
    for k in range(1, 4):
        greet(group_peer(k))
    greet((dom, y * 2 + 1 - x_hi))

    small[0].wait()
    lines = lines_ref[...]
    owner = lines >> 10
    local = (lines & (LINES - 1)).astype(F32)
    slab_rows = iota((SLABS, KS), 0)
    marks = jnp.concatenate(
        [(owner[o : o + 1] == slab_rows).astype(F32) for o in range(ORIENT)], 0
    )
    before = (iota((KS, KS), 0) < iota((KS, KS), 1)).astype(F32).astype(BF16)
    earlier = dot(marks.astype(BF16), before) * marks
    ranks = [
        jnp.sum(earlier[o * SLABS : (o + 1) * SLABS], axis=0, keepdims=True).astype(jnp.int32)
        for o in range(ORIENT)
    ]
    own_line = []
    for o in range(ORIENT):
        mine = (owner[o : o + 1] == slab) & (ranks[o] == slab_rows)
        own_line.append(
            jnp.sum(jnp.where(mine, local[o : o + 1], 0.0), axis=1, keepdims=True)
        )
    own_line = jnp.concatenate(own_line, 0).astype(jnp.int32)
    o_own = 2 * c + z % 2
    first_line = own_line[0:OWNED]
    for o in range(1, ORIENT):
        first_line = jnp.where(o_own == o, own_line[o * OWNED : (o + 1) * OWNED], first_line)
    column = iota((OWNED, 2 * LINES), 1)
    gather[0:OWNED] = (column == 2 * first_line).astype(F32).astype(BF16)
    gather[OWNED:] = (column == 2 * first_line + 1).astype(F32).astype(BF16)

    for j in range(2):
        loads[j].wait()
        picked = dot(gather[...], vbuf.at[j].reshape(2 * LINES, 128)[...]).astype(BF16)
        for part in range(2):
            at = slice(part * KS + j * 128, part * KS + j * 128 + 128)
            own[:, at] = picked[part * OWNED : part * OWNED + OWNED]

    small[1].wait()
    small[2].wait()
    lane = iota((8, 128), 1) % NT
    row_x = jnp.zeros((8, 128), jnp.int32)
    row_y = jnp.zeros((8, 128), jnp.int32)
    for t in range(NT):
        row_x = jnp.where(lane == t, sx_ref[t], row_x)
        row_y = jnp.where(lane == t, sy_ref[t], row_y)
    freq = iota((KS, 128), 0) - HALF
    sin_x, cos_x = turns_sin_cos(freq * row_x[0:1])
    sin_y, cos_y = turns_sin_cos(freq * row_y[0:1])
    wide_lane = iota((KS, 128), 1)
    ephase[0:KS] = jnp.where(wide_lane < NT, cos_y, -sin_y)[:, : 2 * NT].astype(BF16)
    ephase[KS:] = jnp.where(wide_lane < NT, sin_y, cos_y)[:, : 2 * NT].astype(BF16)
    t_cos = cos_x.T[0:NT]
    t_sin = sin_x.T[0:NT]
    table = jnp.concatenate([t_cos, t_sin], 1)
    table_hi = table.astype(BF16)
    table_lo = (table - table_hi.astype(F32)).astype(BF16)
    small[4].wait()
    weights = weights_ref[...]
    weights_hi = weights.astype(BF16)
    weights_lo = (weights - weights_hi.astype(F32)).astype(BF16)
    h = dot(weights_hi, table_hi) + dot(weights_lo, table_hi) + dot(weights_hi, table_lo)
    h = h.astype(BF16).reshape(P_DEV * ORIENT, NT, 2 * KS)
    hs[:, 0:NT] = h[:, :, 0:KS]
    hs[:, NT:] = h[:, :, KS:]
    for o in range(ORIENT):
        rank = ranks[o]
        row = owner[o : o + 1]
        at_t = (row & 1) * 128 + (rank >> 3) * 64 + (row >> 1) * 8 + (rank & 7)
        place_t[o] = (iota((KS, KS), 0) == at_t).astype(F32).astype(BF16)

    freq_row = (iota((8, KS), 1) - HALF).astype(F32)
    which = iota((8, KS), 0)
    focus = jnp.zeros((8, KS), F32)
    small[3].wait()
    for p in range(P_DEV):
        focus = jnp.where(which == p, defocus_ref[p], focus)
    sin_d, cos_d = angle_sin_cos(focus * (freq_row * freq_row * (1.0 / (HALF * HALF))))
    sin_col = sin_d.T
    cos_col = cos_d.T
    u_row = 0.1 * sin_d - 0.995 * cos_d
    v_row = -0.995 * sin_d - 0.1 * cos_d
    loads[2].wait()
    loads[3].wait()
    for p in range(P_DEV):
        for j in range(2):
            at = slice(j * 128, j * 128 + 128)
            split[...] = ibuf.at[j, p].reshape(2 * KS, 128)[...].astype(F32)
            ctf = (
                sin_col[:, p : p + 1] * u_row[p : p + 1, at]
                + cos_col[:, p : p + 1] * v_row[p : p + 1, at]
            )
            cx[p, 0, :, at] = ctf * split[pl.ds(0, KS, stride=2), :]
            cx[p, 1, :, at] = ctf * split[pl.ds(1, KS, stride=2), :]

    def placed_term(o):
        for block in range(2):
            at = slice(block * 128, block * 128 + 128)
            low = slice(KS + block * 128, KS + block * 128 + 128)
            t_re = None
            for p in range(P_DEV):
                table_h = hs[p * ORIENT + o]
                g_re = dot(ephase[at], table_h)
                g_im = dot(ephase[low], table_h)
                c_re = cx[p, 0, at]
                c_im = cx[p, 1, at]
                if t_re is None:
                    t_re = c_re * g_re - c_im * g_im
                    t_im = c_re * g_im + c_im * g_re
                else:
                    t_re += c_re * g_re - c_im * g_im
                    t_im += c_re * g_im + c_im * g_re
            term[at, 0:KS] = t_re.astype(BF16)
            term[at, KS:] = t_im.astype(BF16)
        return dot(place_t[o], term[...])

    def pair_copy(j):
        return pltpu.make_async_remote_copy(
            src_ref=sent.at[j],
            dst_ref=landed.at[j],
            send_sem=p_send.at[j],
            recv_sem=p_recv.at[j],
            device_id=partner,
            device_id_type=MESH,
        )

    def x_copy(j, k):
        return pltpu.make_async_remote_copy(
            src_ref=xsend.at[j, lax.rem(x + k, 4)],
            dst_ref=xrecv.at[j, x],
            send_sem=x_send.at[j],
            recv_sem=x_recv.at[j],
            device_id=x_peer(k),
            device_id_type=MESH,
        )

    def y_copy(j, k):
        return pltpu.make_async_remote_copy(
            src_ref=ysend.at[j, lax.rem(y + k, YS)],
            dst_ref=yrecv.at[j, y],
            send_sem=y_send.at[j],
            recv_sem=y_recv.at[j],
            device_id=y_peer(k),
            device_id_type=MESH,
        )

    def z_copy(j, k):
        return pltpu.make_async_remote_copy(
            src_ref=zsend.at[j],
            dst_ref=zrecv.at[j, z],
            send_sem=z_send.at[j],
            recv_sem=z_recv.at[j],
            device_id=z_peer(k),
            device_id_type=MESH,
        )

    def give(j, carry):
        sent[j] = placed_term(2 * (1 - c) + j).astype(BF16)
        return carry

    lax.fori_loop(0, 2, give, 0)

    pl.semaphore_wait(barrier, SLABS - 1 + ZS - 1 + 3 + 1)

    pair_copy(0).start()
    pair_copy(1).start()

    def slab_copy(k):
        return pltpu.make_async_remote_copy(
            src_ref=own,
            dst_ref=arrived.at[o_own, slab],
            send_sem=s_send.at[0],
            recv_sem=s_recv.at[0],
            device_id=slab_peer(k),
            device_id_type=MESH,
        )

    def send_slab(k, carry):
        slab_copy(k).start()
        return carry

    lax.fori_loop(1, SLABS, send_slab, 0)
    arrived[o_own, slab] = own[...]


    def keep(j, carry):
        mine = placed_term(2 * c + j)
        pair_copy(j).wait_recv()
        both = (mine + landed[j].astype(F32)).astype(BF16)
        xsend[j] = both.reshape(4, 64, 2 * KS)

        def send_x(k, inner):
            x_copy(j, k).start()
            return inner

        lax.fori_loop(1, 4, send_x, 0)
        xrecv[j, x] = xsend[j, x]
        return carry

    lax.fori_loop(0, 2, keep, 0)

    def wait_rows(n, sem):
        part = arrived.at[0, pl.ds(0, n)]
        pltpu.make_async_copy(part, part, sem).wait()

    def pass_rows(o, sem, first=0, n=SLABS, to=partner):
        part = arrived.at[o, pl.ds(first, n)]
        return pltpu.make_async_remote_copy(
            src_ref=part,
            dst_ref=part,
            send_sem=s_send.at[sem],
            recv_sem=s_recv.at[sem],
            device_id=to,
            device_id_type=MESH,
        )

    for o in range(ORIENT):
        at_s = owner[o : o + 1] * OWNED + ranks[o]
        place_s[o] = (iota((KS, KS), 0) == at_s).astype(F32).astype(BF16)
    group = wide_lane // NT
    for o in range(ORIENT):
        cos_o = jnp.where(group == o, cos_x, 0.0).astype(BF16)
        sin_o = jnp.where(group == o, sin_x, 0.0).astype(BF16)
        at = (o // 2) * 2 * KS
        fx[o % 2, at : at + KS, 0:128] = cos_o
        fx[o % 2, at : at + KS, 128:] = -sin_o
        fx[o % 2, at + KS : at + 2 * KS, 0:128] = sin_o
        fx[o % 2, at + KS : at + 2 * KS, 128:] = cos_o
    table_y = jnp.concatenate([cos_y.T[0:NT], sin_y.T[0:NT]], 1) * (1.0 / KS)
    fy_hi = table_y.astype(BF16)
    fy[0:NT] = fy_hi
    fy[NT:] = (table_y - fy_hi.astype(F32)).astype(BF16)

    def correlate(parity, first):
        for j in range(2):
            o = 2 * j + parity
            su[j] = dot_t(place_s[o], arrived[o].reshape(KS, 2 * KS))
        for block in range(2):
            at = slice(block * 128, block * 128 + 128)
            for p in range(P_DEV):
                c_re = cx[p, 0, at]
                c_im = cx[p, 1, at]
                q = []
                for j in range(2):
                    s_re = su[j, at, 0:KS]
                    s_im = su[j, at, KS:]
                    q.append((s_re * c_re + s_im * c_im).astype(BF16))
                    q.append((s_re * c_im - s_im * c_re).astype(BF16))
                part = dot(jnp.concatenate(q, 1), fx[parity])
                if first:
                    zacc[p, at] = part
                else:
                    zacc[p, at] += part

    line_row = jnp.concatenate([2 * own_line, 2 * own_line + 1], 0).astype(F32)
    line_row = jnp.broadcast_to(line_row, (128, 128)).T[0:8].astype(jnp.int32)
    line_ref[...] = line_row
    outs = [pltpu.make_async_copy(line_ref, line_hbm, out_sem.at[0])]
    outs[0].start()
    wait_rows(SLABS - 1, s_recv.at[0])
    to_up = pass_rows(o_own, 2, 0, 8, z_peer(1))
    to_down = pass_rows(o_own, 3, 8, 8, z_peer(ZS - 1))
    to_partner = pass_rows(o_own, 1)
    to_up.start()
    to_down.start()
    to_partner.start()

    def pass_on(j, carry):
        pltpu.make_async_copy(
            xrecv.at[j, pl.ds(0, 3)], xrecv.at[j, pl.ds(0, 3)], x_recv.at[j]
        ).wait()
        for part in range(2):
            at = slice(part * KS, part * KS + KS)
            total = xrecv[j, 0, :, at].astype(F32)
            for other in range(1, 4):
                total += xrecv[j, other, :, at].astype(F32)
            tile_y[:, part * 8 : part * 8 + 8] = total.reshape(YS, 8, KS)
        ysend[j] = tile_y[...].astype(BF16)

        def send_y(k, inner):
            y_copy(j, k).start()
            return inner

        lax.fori_loop(1, YS, send_y, 0)
        yrecv[j, y] = ysend[j, y]
        return carry

    lax.fori_loop(0, 2, pass_on, 0)
    wait_rows(SLABS, s_recv.at[1])
    correlate(z % 2, True)
    wait_rows(8, s_recv.at[2])
    wait_rows(8, s_recv.at[3])
    to_partner_too = pass_rows(2 * c + 1 - z % 2, 4)
    to_partner_too.start()

    def spread(j, carry):
        pltpu.make_async_copy(
            yrecv.at[j, pl.ds(0, YS - 1)], yrecv.at[j, pl.ds(0, YS - 1)], y_recv.at[j]
        ).wait()
        total = yrecv[j, 0].astype(F32)
        for other in range(1, YS):
            total += yrecv[j, other].astype(F32)
        zsend[j] = total.astype(BF16)

        def send_z(k, inner):
            z_copy(j, k).start()
            return inner

        lax.fori_loop(1, ZS, send_z, 0)
        zrecv[j, z] = zsend[j]
        return carry

    lax.fori_loop(0, 2, spread, 0)
    wait_rows(SLABS, s_recv.at[4])
    correlate(1 - z % 2, False)

    place = x_lo * 2 + c
    for j in range(2):
        pltpu.make_async_copy(
            zrecv.at[j, pl.ds(0, ZS - 1)], zrecv.at[j, pl.ds(0, ZS - 1)], z_recv.at[j]
        ).wait()
        total = zrecv[j, 0].astype(F32)
        for other in range(1, ZS):
            total += zrecv[j, other].astype(F32)
        fin[place, j] = (total * SCALE).astype(BF16)

    def group_copy(k):
        return pltpu.make_async_remote_copy(
            src_ref=fin.at[place],
            dst_ref=fin.at[place],
            send_sem=f_send.at[0],
            recv_sem=f_recv.at[0],
            device_id=group_peer(k),
            device_id_type=MESH,
        )

    for k in range(1, 4):
        group_copy(k).start()
    for p in range(P_DEV):
        full = jnp.concatenate([zacc[p, :, 0:128], zacc[p, :, 128:]], 0)
        full_hi = full.astype(BF16)
        full_lo = (full - full_hi.astype(F32)).astype(BF16)
        both = dot(fy[...], full_hi)
        scores_ref[p] = both[0:NT] + both[NT:] + dot(fy[0:NT], full_lo)
    outs.append(pltpu.make_async_copy(scores_ref, scores_hbm, out_sem.at[1]))
    outs[1].start()

    pltpu.make_async_copy(fin.at[pl.ds(0, 3)], fin.at[pl.ds(0, 3)], f_recv.at[0]).wait()
    outs.append(pltpu.make_async_copy(fin, rows_hbm, out_sem.at[2]))
    outs[2].start()

    wait_rows(SLABS - 1, s_send.at[0])
    for sent_rows in (to_partner, to_up, to_down, to_partner_too):
        sent_rows.wait_send()
    for j in range(2):
        pair_copy(j).wait_send()
    for j in range(2):
        pltpu.make_async_copy(
            xrecv.at[j, pl.ds(0, 3)], xrecv.at[j, pl.ds(0, 3)], x_send.at[j]
        ).wait()
    for j in range(2):
        pltpu.make_async_copy(
            yrecv.at[j, pl.ds(0, YS - 1)], yrecv.at[j, pl.ds(0, YS - 1)], y_send.at[j]
        ).wait()
        pltpu.make_async_copy(
            zrecv.at[j, pl.ds(0, ZS - 1)], zrecv.at[j, pl.ds(0, ZS - 1)], z_send.at[j]
        ).wait()
    pltpu.make_async_copy(fin.at[pl.ds(0, 3)], fin.at[pl.ds(0, 3)], f_send.at[0]).wait()
    for out in outs:
        out.wait()


def finish(
    fin_hbm, line_hbm, found_hbm, scores_hbm, update_hbm,
    fin_ref, line_ref, found_ref, scores_ref, insert, rows, buf, in_sem, out_sem,
):
    loads = [
        pltpu.make_async_copy(src, dst, in_sem.at[i])
        for i, (src, dst) in enumerate(
            ((line_hbm, line_ref), (fin_hbm, fin_ref), (found_hbm, found_ref))
        )
    ]
    for load in loads:
        load.start()
    loads[0].wait()
    insert[...] = (iota((2 * LINES, 128), 0) == line_ref[0:1]).astype(F32).astype(BF16)
    loads[1].wait()
    for o in range(ORIENT):
        for r in range(2):
            got = fin_ref[r * 2 + o // 2, o % 2].astype(F32)
            for part in range(2):
                first = part * 64 + o * OWNED + r * 8
                rows[first : first + 8] = got[part * 8 : part * 8 + 8]
    rows_bf16 = rows[...].astype(BF16)
    outs = []
    for piece in range(4):
        of = pl.ds(piece * 256, 256)
        at = slice(piece * 512, piece * 512 + 512)
        placed = dot(insert[at], rows_bf16).astype(BF16)
        for j in range(2):
            buf.at[j, of].reshape(512, 128)[...] = placed[:, j * 128 : j * 128 + 128]
            outs.append(
                pltpu.make_async_copy(
                    buf.at[j, of],
                    update_hbm.at[of, :, pl.ds(j * 128, 128)],
                    out_sem.at[piece * 2 + j],
                )
            )
            outs[-1].start()
    loads[2].wait()
    for o in range(ORIENT):
        scores_ref[:, o] = found_ref[:, :, o * NT : (o + 1) * NT]
    outs.append(pltpu.make_async_copy(scores_ref, scores_hbm, out_sem.at[8]))
    outs[-1].start()
    for out in outs:
        out.wait()


def body(volume, images, defocus, soft_weights, slice_lines, shift_y, shift_x):
    hbm = pl.BlockSpec(memory_space=pltpu.HBM)
    dma = pltpu.SemaphoreType.DMA
    found, rows, line = pl.pallas_call(
        kernel,
        out_shape=(
            jax.ShapeDtypeStruct((P_DEV, NT, ORIENT * NT), F32),
            jax.ShapeDtypeStruct((4, 2, 16, KS), BF16),
            jax.ShapeDtypeStruct((8, 128), jnp.int32),
        ),
        in_specs=[hbm] * 7,
        out_specs=(hbm, hbm, hbm),
        scratch_shapes=[
            pltpu.VMEM((P_DEV, NT, ORIENT * NT), F32),
            pltpu.VMEM((8, 128), jnp.int32),
            pltpu.VMEM((ORIENT, KS), jnp.int32),
            pltpu.VMEM((P_DEV * ORIENT * NT, NT), F32),
            pltpu.SMEM((P_DEV,), F32),
            pltpu.SMEM((NT,), jnp.int32),
            pltpu.SMEM((NT,), jnp.int32),
            pltpu.VMEM((2, LINES, 2, 128), BF16),
            pltpu.VMEM((2, P_DEV, KS, 2, 128), BF16),
            pltpu.VMEM((2 * KS, 128), F32),
            pltpu.VMEM((OWNED, 2 * KS), BF16),
            pltpu.VMEM((ORIENT, SLABS, OWNED, 2 * KS), BF16),
            pltpu.VMEM((2 * OWNED, 2 * LINES), BF16),
            pltpu.VMEM((ORIENT, KS, KS), BF16),
            pltpu.VMEM((ORIENT, KS, KS), BF16),
            pltpu.VMEM((2, 4 * KS, 256), BF16),
            pltpu.VMEM((2 * KS, 2 * NT), BF16),
            pltpu.VMEM((2 * NT, 2 * KS), BF16),
            pltpu.VMEM((P_DEV * ORIENT, 2 * NT, KS), BF16),
            pltpu.VMEM((P_DEV, 2, KS, KS), F32),
            pltpu.VMEM((KS, 2 * KS), BF16),
            pltpu.VMEM((2, KS, 2 * KS), BF16),
            pltpu.VMEM((2, KS, 2 * KS), BF16),
            pltpu.VMEM((2, 4, 64, 2 * KS), BF16),
            pltpu.VMEM((2, 4, 64, 2 * KS), BF16),
            pltpu.VMEM((2, YS, 16, KS), BF16),
            pltpu.VMEM((2, YS, 16, KS), BF16),
            pltpu.VMEM((2, 16, KS), BF16),
            pltpu.VMEM((2, ZS, 16, KS), BF16),
            pltpu.VMEM((4, 2, 16, KS), BF16),
            pltpu.VMEM((YS, 16, KS), F32),
            pltpu.VMEM((P_DEV, KS, 256), F32),
            pltpu.VMEM((2, KS, 2 * KS), F32),
            dma((5,)),
            dma((4,)),
            dma((3,)),
            dma((5,)),
            dma((5,)),
            dma((2,)),
            dma((2,)),
            dma((2,)),
            dma((2,)),
            dma((2,)),
            dma((2,)),
            dma((2,)),
            dma((2,)),
            dma((1,)),
            dma((1,)),
        ],
        compiler_params=pltpu.CompilerParams(
            collective_id=0, has_side_effects=True, vmem_limit_bytes=60 * 1024 * 1024
        ),
        name="cryo",
    )(
        slice_lines,
        soft_weights.reshape(P_DEV * ORIENT * NT, NT),
        defocus,
        shift_y,
        shift_x,
        volume,
        images,
    )
    return pl.pallas_call(
        finish,
        out_shape=(
            jax.ShapeDtypeStruct((P_DEV, ORIENT, NT, NT), F32),
            jax.ShapeDtypeStruct((LINES, 2, KS), BF16),
        ),
        in_specs=[hbm] * 3,
        out_specs=(hbm, hbm),
        scratch_shapes=[
            pltpu.VMEM((4, 2, 16, KS), BF16),
            pltpu.VMEM((8, 128), jnp.int32),
            pltpu.VMEM((P_DEV, NT, ORIENT * NT), F32),
            pltpu.VMEM((P_DEV, ORIENT, NT, NT), F32),
            pltpu.VMEM((2 * LINES, 2 * ORIENT * OWNED), BF16),
            pltpu.VMEM((2 * ORIENT * OWNED, KS), F32),
            pltpu.VMEM((2, LINES, 2, 128), BF16),
            dma((3,)),
            dma((9,)),
        ],
        compiler_params=pltpu.CompilerParams(vmem_limit_bytes=60 * 1024 * 1024),
        name="finish",
    )(rows, line, found)


def solution(mesh):
    placed = (
        P("slab", None, None),
        P(("dom", "slab"), None, None, None),
        P(("dom", "slab")),
        P(("dom", "slab"), None, None, None),
        P(),
        P(),
        P(),
    )
    return jax.shard_map(
        body,
        mesh=mesh,
        in_specs=placed,
        out_specs=(P(("dom", "slab"), None, None, None), P("slab", None, None)),
        check_vma=False,
    )
```

```python
import math

import jax
import jax.numpy as jnp
from jax import lax
from jax.experimental import pallas as pl
from jax.experimental.pallas import tpu as pltpu
from jax.sharding import PartitionSpec as P

KS = 256
HALF = KS // 2
P_DEV = 4
LINES = 1024
ORIENT = 4
NT = 32
OWNED = 16
PARTICLES = 2048
SLABS = 16
ZS = 8
YS = 8
XLO = 2
SCALE = 1.0 / math.sqrt(NT * NT * PARTICLES)
F32 = jnp.float32
BF16 = jnp.bfloat16
MESH = pl.DeviceIdType.MESH


def dot(a, b):
    return jnp.dot(a, b, preferred_element_type=F32)


def poly_sin_cos(r):
    s = r * r
    sin = r * (1.0 + s * (-1 / 6 + s * (1 / 120 + s * (-1 / 5040 + s * (1 / 362880)))))
    cos = 1.0 + s * (-0.5 + s * (1 / 24 + s * (-1 / 720 + s * (1 / 40320))))
    return sin, cos


def rotate(quadrant, sin, cos):
    q = quadrant & 3
    odd = (q & 1) == 1
    s = jnp.where(odd, cos, sin)
    c = jnp.where(odd, sin, cos)
    s = jnp.where(q >= 2, -s, s)
    c = jnp.where((q == 1) | (q == 2), -c, c)
    return s, c


def turns_sin_cos(turns):
    t = turns & (KS - 1)
    q = (t + KS // 8) >> 6
    r = (t - (q << 6)).astype(F32) * (2.0 * math.pi / KS)
    return rotate(q, *poly_sin_cos(r))


def angle_sin_cos(x):
    n = jnp.floor(x * (2.0 / math.pi) + 0.5)
    r = x - n * 1.5703125
    r = r - n * 4.837512969970703e-4
    r = r - n * 7.549789948768648e-8
    return rotate(n.astype(jnp.int32), *poly_sin_cos(r))


def iota(shape, dim):
    return lax.broadcasted_iota(jnp.int32, shape, dim)


def kernel(
    lines_hbm, weights_hbm, defocus_hbm, sy_hbm, sx_hbm, volume_hbm, images_hbm,
    scores_hbm, rows_hbm, line_hbm,
    scores_ref, line_ref, lines_ref, weights_ref, defocus_ref, sy_ref, sx_ref,
    vbuf, ibuf, split, own, arrived, gather, place_s, place_t,
    fx, ephase, fy, hs, cx, term, sent, landed, xsend, xrecv, x1send, x1recv, ysend, yrecv,
    y1send, y1recv, zsend, zrecv,
    fin, tile_y, zacc, su,
    small_sem, in_sem, out_sem, s_send, s_recv, p_send, p_recv, x_send, x_recv, z_send, z_recv,
    y_send, y_recv, f_send, f_recv,
):
    dom = lax.axis_index("dom")
    slab = lax.axis_index("slab")
    x_lo = dom // 16
    z = (dom // 2) % 8
    c = dom % 2
    zc = z * 2 + c
    partner = (dom + 1 - 2 * c, slab)
    y = slab // 2
    x_hi = slab % 2
    x = x_hi * 2 + x_lo

    small = [
        pltpu.make_async_copy(src, dst, small_sem.at[i])
        for i, (src, dst) in enumerate(
            (
                (lines_hbm, lines_ref),
                (sx_hbm, sx_ref),
                (sy_hbm, sy_ref),
                (defocus_hbm, defocus_ref),
                (weights_hbm, weights_ref),
            )
        )
    ]
    for load in small:
        load.start()
    loads = []
    for j in range(2):
        cols = pl.ds(j * 128, 128)
        loads.append(pltpu.make_async_copy(volume_hbm.at[:, :, cols], vbuf.at[j], in_sem.at[j]))
    for j in range(2):
        cols = pl.ds(j * 128, 128)
        loads.append(
            pltpu.make_async_copy(images_hbm.at[:, :, :, cols], ibuf.at[j], in_sem.at[2 + j])
        )
    for load in loads:
        load.start()

    barrier = pltpu.get_barrier_semaphore()

    def slab_peer(k):
        to = lax.rem(slab + k, SLABS)
        flip = (to % 2 + x_hi) % 2
        return ((x_lo + flip) % 2) * 16 + zc, to

    def x_peer(k):
        to = lax.rem(x + k, 4)
        return (to % 2) * 16 + zc, y * 2 + to // 2

    def y_peer(k):
        return dom, lax.rem(y + k, YS) * 2 + x_hi

    def z_peer(k):
        return x_lo * 16 + lax.rem(z + k, ZS) * 2 + c, slab

    def group_peer(k):
        to = lax.rem(x_lo * 2 + c + k, 4)
        return (to // 2) * 16 + z * 2 + to % 2, slab

    def greet(peer):
        pl.semaphore_signal(barrier, inc=1, device_id=peer, device_id_type=MESH)

    def greet_slab(k, carry):
        greet(slab_peer(k))
        return carry

    def greet_z(k, carry):
        greet(z_peer(k))
        return carry

    lax.fori_loop(1, SLABS, greet_slab, 0)
    lax.fori_loop(1, ZS, greet_z, 0)
    for k in range(1, 4):
        greet(group_peer(k))
    greet((dom, y * 2 + 1 - x_hi))

    small[0].wait()
    lines = lines_ref[...]
    owner = lines >> 10
    local = (lines & (LINES - 1)).astype(F32)
    slab_rows = iota((SLABS, KS), 0)
    marks = jnp.concatenate(
        [(owner[o : o + 1] == slab_rows).astype(F32) for o in range(ORIENT)], 0
    )
    before = (iota((KS, KS), 0) < iota((KS, KS), 1)).astype(F32).astype(BF16)
    earlier = dot(marks.astype(BF16), before) * marks
    ranks = [
        jnp.sum(earlier[o * SLABS : (o + 1) * SLABS], axis=0, keepdims=True).astype(jnp.int32)
        for o in range(ORIENT)
    ]
    own_line = []
    for o in range(ORIENT):
        mine = (owner[o : o + 1] == slab) & (ranks[o] == slab_rows)
        own_line.append(
            jnp.sum(jnp.where(mine, local[o : o + 1], 0.0), axis=1, keepdims=True)
        )
    own_line = jnp.concatenate(own_line, 0).astype(jnp.int32)
    o_own = 2 * c + z % 2
    first_line = own_line[0:OWNED]
    for o in range(1, ORIENT):
        first_line = jnp.where(o_own == o, own_line[o * OWNED : (o + 1) * OWNED], first_line)
    column = iota((OWNED, 2 * LINES), 1)
    gather[0:OWNED] = (column == 2 * first_line).astype(F32).astype(BF16)
    gather[OWNED:] = (column == 2 * first_line + 1).astype(F32).astype(BF16)

    for j in range(2):
        loads[j].wait()
        picked = dot(gather[...], vbuf.at[j].reshape(2 * LINES, 128)[...]).astype(BF16)
        for part in range(2):
            at = slice(part * KS + j * 128, part * KS + j * 128 + 128)
            own[:, at] = picked[part * OWNED : part * OWNED + OWNED]

    small[1].wait()
    small[2].wait()
    lane = iota((8, 128), 1) % NT
    row_x = jnp.zeros((8, 128), jnp.int32)
    row_y = jnp.zeros((8, 128), jnp.int32)
    for t in range(NT):
        row_x = jnp.where(lane == t, sx_ref[t], row_x)
        row_y = jnp.where(lane == t, sy_ref[t], row_y)
    freq = iota((KS, 128), 0) - HALF
    sin_x, cos_x = turns_sin_cos(freq * row_x[0:1])
    sin_y, cos_y = turns_sin_cos(freq * row_y[0:1])
    wide_lane = iota((KS, 128), 1)
    e_re = jnp.where(wide_lane < NT, cos_y, -sin_y)[:, : 2 * NT].astype(BF16)
    e_im = jnp.where(wide_lane < NT, sin_y, cos_y)[:, : 2 * NT].astype(BF16)
    for block in range(2):
        ephase[block, 0:128] = e_re[block * 128 : block * 128 + 128]
        ephase[block, 128:] = e_im[block * 128 : block * 128 + 128]
    t_cos = cos_x.T[0:NT]
    t_sin = sin_x.T[0:NT]
    table = jnp.concatenate([t_cos, t_sin], 1)
    table_hi = table.astype(BF16)
    table_lo = (table - table_hi.astype(F32)).astype(BF16)
    small[4].wait()
    weights = weights_ref[...]
    weights_hi = weights.astype(BF16)
    weights_lo = (weights - weights_hi.astype(F32)).astype(BF16)
    h = dot(weights_hi, table_hi) + dot(weights_lo, table_hi) + dot(weights_hi, table_lo)
    h = h.astype(BF16).reshape(P_DEV * ORIENT, NT, 2 * KS)
    hs[:, 0:NT] = h[:, :, 0:KS]
    hs[:, NT:] = h[:, :, KS:]
    for o in range(ORIENT):
        rank = ranks[o]
        row = owner[o : o + 1]
        if o % 2 == 0:
            at_t = (row & 1) * 128 + (rank >> 3) * 64 + (row >> 1) * 8 + (rank & 7)
        else:
            at_t = (row >> 1) * 32 + (row & 1) * 16 + (rank >> 3) * 8 + (rank & 7)
        place_t[o] = (iota((KS, KS), 0) == at_t).astype(F32).astype(BF16)

    freq_row = (iota((8, KS), 1) - HALF).astype(F32)
    which = iota((8, KS), 0)
    focus = jnp.zeros((8, KS), F32)
    small[3].wait()
    for p in range(P_DEV):
        focus = jnp.where(which == p, defocus_ref[p], focus)
    sin_d, cos_d = angle_sin_cos(focus * (freq_row * freq_row * (1.0 / (HALF * HALF))))
    sin_col = sin_d.T
    cos_col = cos_d.T
    u_row = 0.1 * sin_d - 0.995 * cos_d
    v_row = -0.995 * sin_d - 0.1 * cos_d
    loads[2].wait()
    loads[3].wait()
    for p in range(P_DEV):
        sin_p = jnp.broadcast_to(sin_col[:, p : p + 1], (KS, 128))
        cos_p = jnp.broadcast_to(cos_col[:, p : p + 1], (KS, 128))
        for j in range(2):
            at = slice(j * 128, j * 128 + 128)
            split[...] = ibuf.at[j, p].reshape(2 * KS, 128)[...].astype(F32)
            ctf = (
                sin_p * u_row[p : p + 1, at]
                + cos_p * v_row[p : p + 1, at]
            )
            cx[p, 0, :, at] = ctf * split[pl.ds(0, KS, stride=2), :]
            cx[p, 1, :, at] = ctf * split[pl.ds(1, KS, stride=2), :]

    def placed_term(o):
        for block in range(2):
            at = slice(block * 128, block * 128 + 128)
            t_re = None
            for p in range(P_DEV):
                table_h = hs[p * ORIENT + o]
                g = dot(ephase[block], table_h)
                g_re = g[0:128]
                g_im = g[128:]
                c_re = cx[p, 0, at]
                c_im = cx[p, 1, at]
                if t_re is None:
                    t_re = c_re * g_re - c_im * g_im
                    t_im = c_re * g_im + c_im * g_re
                else:
                    t_re += c_re * g_re - c_im * g_im
                    t_im += c_re * g_im + c_im * g_re
            term[at, 0:KS] = t_re.astype(BF16)
            term[at, KS:] = t_im.astype(BF16)
        return dot(place_t[o], term[...])

    def pair_copy(j):
        return pltpu.make_async_remote_copy(
            src_ref=sent.at[j],
            dst_ref=landed.at[j],
            send_sem=p_send.at[j],
            recv_sem=p_recv.at[j],
            device_id=partner,
            device_id_type=MESH,
        )

    def x_copy(j, send, recv, k):
        return pltpu.make_async_remote_copy(
            src_ref=send.at[lax.rem(x + k, 4)],
            dst_ref=recv.at[x],
            send_sem=x_send.at[j],
            recv_sem=x_recv.at[j],
            device_id=x_peer(k),
            device_id_type=MESH,
        )

    def y_copy(j, send, recv, k):
        return pltpu.make_async_remote_copy(
            src_ref=send.at[lax.rem(y + k, YS)],
            dst_ref=recv.at[y],
            send_sem=y_send.at[j],
            recv_sem=y_recv.at[j],
            device_id=y_peer(k),
            device_id_type=MESH,
        )

    def send_x(j, send, recv):
        def start(k, carry):
            x_copy(j, send, recv, k).start()
            return carry

        lax.fori_loop(1, 4, start, 0)
        recv[x] = send[x]

    def send_y(j, send, recv):
        def start(k, carry):
            y_copy(j, send, recv, k).start()
            return carry

        lax.fori_loop(1, YS, start, 0)
        recv[y] = send[y]

    def sum_of(ref, n, sem, *at):
        part = ref.at[pl.ds(0, n - 1)]
        pltpu.make_async_copy(part, part, sem).wait()
        return sum_over(ref, n, *at)

    def sum_over(ref, n, *at):
        total = ref[(0,) + at].astype(F32)
        for other in range(1, n):
            total += ref[(other,) + at].astype(F32)
        return total

    def z_copy(j, k):
        return pltpu.make_async_remote_copy(
            src_ref=zsend.at[j],
            dst_ref=zrecv.at[j, z],
            send_sem=z_send.at[j],
            recv_sem=z_recv.at[j],
            device_id=z_peer(k),
            device_id_type=MESH,
        )

    def give(j, carry):
        sent[j] = placed_term(2 * (1 - c) + j).astype(BF16)
        return carry

    lax.fori_loop(0, 2, give, 0)

    pl.semaphore_wait(barrier, SLABS - 1 + ZS - 1 + 3 + 1)

    pair_copy(0).start()
    pair_copy(1).start()

    def slab_copy(k):
        return pltpu.make_async_remote_copy(
            src_ref=own,
            dst_ref=arrived.at[o_own, slab],
            send_sem=s_send.at[0],
            recv_sem=s_recv.at[0],
            device_id=slab_peer(k),
            device_id_type=MESH,
        )

    def send_slab(k, carry):
        slab_copy(k).start()
        return carry

    lax.fori_loop(1, SLABS, send_slab, 0)
    arrived[o_own, slab] = own[...]


    for j in range(2):
        mine = placed_term(2 * c + j)
        pair_copy(j).wait_recv()
        both = (mine + landed[j].astype(F32)).astype(BF16)
        if j == 0:
            xsend[...] = both.reshape(4, 64, 2 * KS)
            send_x(0, xsend, xrecv)
        else:
            y1send[...] = both.reshape(YS, NT, 2 * KS)
            send_y(1, y1send, y1recv)

    def wait_rows(n, sem):
        part = arrived.at[0, pl.ds(0, n)]
        pltpu.make_async_copy(part, part, sem).wait()

    def pass_rows(o, sem, first=0, n=SLABS, to=partner):
        part = arrived.at[o, pl.ds(first, n)]
        return pltpu.make_async_remote_copy(
            src_ref=part,
            dst_ref=part,
            send_sem=s_send.at[sem],
            recv_sem=s_recv.at[sem],
            device_id=to,
            device_id_type=MESH,
        )

    at_s = [owner[o : o + 1] * OWNED + ranks[o] for o in range(ORIENT)]
    at_s = jnp.concatenate(at_s + at_s, 0).astype(F32).T.astype(jnp.int32)
    for o in range(ORIENT):
        place_s[o] = (iota((KS, KS), 1) == at_s[:, o : o + 1]).astype(F32).astype(BF16)
    group = wide_lane // NT
    for o in range(ORIENT):
        cos_o = jnp.where(group == o, cos_x, 0.0).astype(BF16)
        sin_o = jnp.where(group == o, sin_x, 0.0).astype(BF16)
        at = (o // 2) * 2 * KS
        fx[o % 2, at : at + KS, 0:128] = cos_o
        fx[o % 2, at : at + KS, 128:] = -sin_o
        fx[o % 2, at + KS : at + 2 * KS, 0:128] = sin_o
        fx[o % 2, at + KS : at + 2 * KS, 128:] = cos_o
    table_y = jnp.concatenate([cos_y.T[0:NT], sin_y.T[0:NT]], 1) * (1.0 / KS)
    fy_hi = table_y.astype(BF16)
    fy[0:NT] = fy_hi
    fy[NT:] = (table_y - fy_hi.astype(F32)).astype(BF16)

    def correlate(parity, first):
        for j in range(2):
            o = 2 * j + parity
            su[j] = dot(place_s[o], arrived[o].reshape(KS, 2 * KS))
        for block in range(2):
            at = slice(block * 128, block * 128 + 128)
            for p in range(P_DEV):
                c_re = cx[p, 0, at]
                c_im = cx[p, 1, at]
                q = []
                for j in range(2):
                    s_re = su[j, at, 0:KS]
                    s_im = su[j, at, KS:]
                    q.append((s_re * c_re + s_im * c_im).astype(BF16))
                    q.append((s_re * c_im - s_im * c_re).astype(BF16))
                part = dot(jnp.concatenate(q, 1), fx[parity])
                if first:
                    zacc[p, at] = part
                else:
                    zacc[p, at] += part

    line_row = jnp.concatenate([2 * own_line, 2 * own_line + 1], 0).astype(F32)
    line_row = jnp.broadcast_to(line_row, (128, 128)).T[0:8].astype(jnp.int32)
    line_ref[...] = line_row
    outs = [pltpu.make_async_copy(line_ref, line_hbm, out_sem.at[0])]
    outs[0].start()
    wait_rows(SLABS - 1, s_recv.at[0])
    to_up = pass_rows(o_own, 2, 0, 8, z_peer(1))
    to_down = pass_rows(o_own, 3, 8, 8, z_peer(ZS - 1))
    to_partner = pass_rows(o_own, 1)
    to_up.start()
    to_down.start()
    to_partner.start()

    everything = slice(None)
    part = xrecv.at[pl.ds(0, 3)]
    pltpu.make_async_copy(part, part, x_recv.at[0]).wait()
    for part in range(2):
        total = sum_over(xrecv, 4, everything, slice(part * KS, part * KS + KS))
        tile_y[:, part * 8 : part * 8 + 8] = total.reshape(YS, 8, KS)
    ysend[...] = tile_y[...].astype(BF16)
    send_y(0, ysend, yrecv)
    part = y1recv.at[pl.ds(0, YS - 1)]
    pltpu.make_async_copy(part, part, y_recv.at[1]).wait()
    for part in range(2):
        total = sum_over(y1recv, YS, everything, slice(part * KS, part * KS + KS))
        tile_y[0:4, part * 8 : part * 8 + 8] = total.reshape(4, 8, KS)
    x1send[...] = tile_y[0:4].astype(BF16)
    send_x(1, x1send, x1recv)
    wait_rows(SLABS, s_recv.at[1])
    correlate(z % 2, True)
    wait_rows(8, s_recv.at[2])
    wait_rows(8, s_recv.at[3])
    to_partner_too = pass_rows(2 * c + 1 - z % 2, 4)
    to_partner_too.start()

    for j in range(2):
        if j == 0:
            total = sum_of(yrecv, YS, y_recv.at[0])
        else:
            total = sum_of(x1recv, 4, x_recv.at[1])
        zsend[j] = total.astype(BF16)

        def send_z(k, carry):
            z_copy(j, k).start()
            return carry

        lax.fori_loop(1, ZS, send_z, 0)
        zrecv[j, z] = zsend[j]
    wait_rows(SLABS, s_recv.at[4])
    correlate(1 - z % 2, False)

    place = x_lo * 2 + c
    for j in range(2):
        pltpu.make_async_copy(
            zrecv.at[j, pl.ds(0, ZS - 1)], zrecv.at[j, pl.ds(0, ZS - 1)], z_recv.at[j]
        ).wait()
        total = zrecv[j, 0].astype(F32)
        for other in range(1, ZS):
            total += zrecv[j, other].astype(F32)
        fin[place, j] = (total * SCALE).astype(BF16)

    def group_copy(k):
        return pltpu.make_async_remote_copy(
            src_ref=fin.at[place],
            dst_ref=fin.at[place],
            send_sem=f_send.at[0],
            recv_sem=f_recv.at[0],
            device_id=group_peer(k),
            device_id_type=MESH,
        )

    for k in range(1, 4):
        group_copy(k).start()
    for p in range(P_DEV):
        full = jnp.concatenate([zacc[p, :, 0:128], zacc[p, :, 128:]], 0)
        full_hi = full.astype(BF16)
        full_lo = (full - full_hi.astype(F32)).astype(BF16)
        both = dot(fy[...], full_hi)
        scores_ref[p] = both[0:NT] + both[NT:] + dot(fy[0:NT], full_lo)
    outs.append(pltpu.make_async_copy(scores_ref, scores_hbm, out_sem.at[1]))
    outs[1].start()

    pltpu.make_async_copy(fin.at[pl.ds(0, 3)], fin.at[pl.ds(0, 3)], f_recv.at[0]).wait()
    outs.append(pltpu.make_async_copy(fin, rows_hbm, out_sem.at[2]))
    outs[2].start()

    wait_rows(SLABS - 1, s_send.at[0])
    for sent_rows in (to_partner, to_up, to_down, to_partner_too):
        sent_rows.wait_send()
    for j in range(2):
        pair_copy(j).wait_send()
    for ref, n, sem in (
        (xrecv, 4, x_send.at[0]),
        (x1recv, 4, x_send.at[1]),
        (yrecv, YS, y_send.at[0]),
        (y1recv, YS, y_send.at[1]),
        (zrecv.at[0], ZS, z_send.at[0]),
        (zrecv.at[1], ZS, z_send.at[1]),
    ):
        part = ref.at[pl.ds(0, n - 1)]
        pltpu.make_async_copy(part, part, sem).wait()
    pltpu.make_async_copy(fin.at[pl.ds(0, 3)], fin.at[pl.ds(0, 3)], f_send.at[0]).wait()
    for out in outs:
        out.wait()


def finish(
    fin_hbm, line_hbm, found_hbm, scores_hbm, update_hbm,
    fin_ref, line_ref, found_ref, scores_ref, insert, rows, buf, in_sem, out_sem,
):
    loads = [
        pltpu.make_async_copy(src, dst, in_sem.at[i])
        for i, (src, dst) in enumerate(
            ((line_hbm, line_ref), (fin_hbm, fin_ref), (found_hbm, found_ref))
        )
    ]
    for load in loads:
        load.start()
    loads[0].wait()
    insert[...] = (iota((2 * LINES, 128), 0) == line_ref[0:1]).astype(F32).astype(BF16)
    loads[1].wait()
    for o in range(ORIENT):
        for r in range(2):
            got = fin_ref[r * 2 + o // 2, o % 2].astype(F32)
            for part in range(2):
                first = part * 64 + o * OWNED + r * 8
                rows[first : first + 8] = got[part * 8 : part * 8 + 8]
    rows_bf16 = rows[...].astype(BF16)
    outs = []
    for piece in range(4):
        of = pl.ds(piece * 256, 256)
        at = slice(piece * 512, piece * 512 + 512)
        placed = dot(insert[at], rows_bf16).astype(BF16)
        for j in range(2):
            buf.at[j, of].reshape(512, 128)[...] = placed[:, j * 128 : j * 128 + 128]
            outs.append(
                pltpu.make_async_copy(
                    buf.at[j, of],
                    update_hbm.at[of, :, pl.ds(j * 128, 128)],
                    out_sem.at[piece * 2 + j],
                )
            )
            outs[-1].start()
    loads[2].wait()
    for o in range(ORIENT):
        scores_ref[:, o] = found_ref[:, :, o * NT : (o + 1) * NT]
    outs.append(pltpu.make_async_copy(scores_ref, scores_hbm, out_sem.at[8]))
    outs[-1].start()
    for out in outs:
        out.wait()


def body(volume, images, defocus, soft_weights, slice_lines, shift_y, shift_x):
    hbm = pl.BlockSpec(memory_space=pltpu.HBM)
    dma = pltpu.SemaphoreType.DMA
    found, rows, line = pl.pallas_call(
        kernel,
        out_shape=(
            jax.ShapeDtypeStruct((P_DEV, NT, ORIENT * NT), F32),
            jax.ShapeDtypeStruct((4, 2, 16, KS), BF16),
            jax.ShapeDtypeStruct((8, 128), jnp.int32),
        ),
        in_specs=[hbm] * 7,
        out_specs=(hbm, hbm, hbm),
        scratch_shapes=[
            pltpu.VMEM((P_DEV, NT, ORIENT * NT), F32),
            pltpu.VMEM((8, 128), jnp.int32),
            pltpu.VMEM((ORIENT, KS), jnp.int32),
            pltpu.VMEM((P_DEV * ORIENT * NT, NT), F32),
            pltpu.SMEM((P_DEV,), F32),
            pltpu.SMEM((NT,), jnp.int32),
            pltpu.SMEM((NT,), jnp.int32),
            pltpu.VMEM((2, LINES, 2, 128), BF16),
            pltpu.VMEM((2, P_DEV, KS, 2, 128), BF16),
            pltpu.VMEM((2 * KS, 128), F32),
            pltpu.VMEM((OWNED, 2 * KS), BF16),
            pltpu.VMEM((ORIENT, SLABS, OWNED, 2 * KS), BF16),
            pltpu.VMEM((2 * OWNED, 2 * LINES), BF16),
            pltpu.VMEM((ORIENT, KS, KS), BF16),
            pltpu.VMEM((ORIENT, KS, KS), BF16),
            pltpu.VMEM((2, 4 * KS, 256), BF16),
            pltpu.VMEM((2, KS, 2 * NT), BF16),
            pltpu.VMEM((2 * NT, 2 * KS), BF16),
            pltpu.VMEM((P_DEV * ORIENT, 2 * NT, KS), BF16),
            pltpu.VMEM((P_DEV, 2, KS, KS), F32),
            pltpu.VMEM((KS, 2 * KS), BF16),
            pltpu.VMEM((2, KS, 2 * KS), BF16),
            pltpu.VMEM((2, KS, 2 * KS), BF16),
            pltpu.VMEM((4, 64, 2 * KS), BF16),
            pltpu.VMEM((4, 64, 2 * KS), BF16),
            pltpu.VMEM((4, 16, KS), BF16),
            pltpu.VMEM((4, 16, KS), BF16),
            pltpu.VMEM((YS, 16, KS), BF16),
            pltpu.VMEM((YS, 16, KS), BF16),
            pltpu.VMEM((YS, NT, 2 * KS), BF16),
            pltpu.VMEM((YS, NT, 2 * KS), BF16),
            pltpu.VMEM((2, 16, KS), BF16),
            pltpu.VMEM((2, ZS, 16, KS), BF16),
            pltpu.VMEM((4, 2, 16, KS), BF16),
            pltpu.VMEM((YS, 16, KS), F32),
            pltpu.VMEM((P_DEV, KS, 256), F32),
            pltpu.VMEM((2, KS, 2 * KS), F32),
            dma((5,)),
            dma((4,)),
            dma((3,)),
            dma((5,)),
            dma((5,)),
            dma((2,)),
            dma((2,)),
            dma((2,)),
            dma((2,)),
            dma((2,)),
            dma((2,)),
            dma((2,)),
            dma((2,)),
            dma((1,)),
            dma((1,)),
        ],
        compiler_params=pltpu.CompilerParams(
            collective_id=0, has_side_effects=True, vmem_limit_bytes=60 * 1024 * 1024
        ),
        name="cryo",
    )(
        slice_lines,
        soft_weights.reshape(P_DEV * ORIENT * NT, NT),
        defocus,
        shift_y,
        shift_x,
        volume,
        images,
    )
    return pl.pallas_call(
        finish,
        out_shape=(
            jax.ShapeDtypeStruct((P_DEV, ORIENT, NT, NT), F32),
            jax.ShapeDtypeStruct((LINES, 2, KS), BF16),
        ),
        in_specs=[hbm] * 3,
        out_specs=(hbm, hbm),
        scratch_shapes=[
            pltpu.VMEM((4, 2, 16, KS), BF16),
            pltpu.VMEM((8, 128), jnp.int32),
            pltpu.VMEM((P_DEV, NT, ORIENT * NT), F32),
            pltpu.VMEM((P_DEV, ORIENT, NT, NT), F32),
            pltpu.VMEM((2 * LINES, 2 * ORIENT * OWNED), BF16),
            pltpu.VMEM((2 * ORIENT * OWNED, KS), F32),
            pltpu.VMEM((2, LINES, 2, 128), BF16),
            dma((3,)),
            dma((9,)),
        ],
        compiler_params=pltpu.CompilerParams(vmem_limit_bytes=60 * 1024 * 1024),
        name="finish",
    )(rows, line, found)


def solution(mesh):
    placed = (
        P("slab", None, None),
        P(("dom", "slab"), None, None, None),
        P(("dom", "slab")),
        P(("dom", "slab"), None, None, None),
        P(),
        P(),
        P(),
    )
    return jax.shard_map(
        body,
        mesh=mesh,
        in_specs=placed,
        out_specs=(P(("dom", "slab"), None, None, None), P("slab", None, None)),
        check_vma=False,
    )
```

```python
import math

import jax
import jax.numpy as jnp
from jax import lax
from jax.experimental import pallas as pl
from jax.experimental.pallas import tpu as pltpu
from jax.sharding import PartitionSpec as P

KS = 256
HALF = KS // 2
P_DEV = 4
LINES = 1024
ORIENT = 4
NT = 32
OWNED = 16
PARTICLES = 2048
SLABS = 16
ZS = 8
YS = 8
XLO = 2
SCALE = 1.0 / math.sqrt(NT * NT * PARTICLES)
F32 = jnp.float32
BF16 = jnp.bfloat16
MESH = pl.DeviceIdType.MESH


def dot(a, b):
    return jnp.dot(a, b, preferred_element_type=F32)


def poly_sin_cos(r):
    s = r * r
    sin = r * (1.0 + s * (-1 / 6 + s * (1 / 120 + s * (-1 / 5040 + s * (1 / 362880)))))
    cos = 1.0 + s * (-0.5 + s * (1 / 24 + s * (-1 / 720 + s * (1 / 40320))))
    return sin, cos


def rotate(quadrant, sin, cos):
    q = quadrant & 3
    odd = (q & 1) == 1
    s = jnp.where(odd, cos, sin)
    c = jnp.where(odd, sin, cos)
    s = jnp.where(q >= 2, -s, s)
    c = jnp.where((q == 1) | (q == 2), -c, c)
    return s, c


def turns_sin_cos(turns):
    t = turns & (KS - 1)
    q = (t + KS // 8) >> 6
    r = (t - (q << 6)).astype(F32) * (2.0 * math.pi / KS)
    return rotate(q, *poly_sin_cos(r))


def angle_sin_cos(x):
    n = jnp.floor(x * (2.0 / math.pi) + 0.5)
    r = x - n * 1.5703125
    r = r - n * 4.837512969970703e-4
    r = r - n * 7.549789948768648e-8
    return rotate(n.astype(jnp.int32), *poly_sin_cos(r))


def iota(shape, dim):
    return lax.broadcasted_iota(jnp.int32, shape, dim)


def kernel(
    lines_hbm, weights_hbm, defocus_hbm, sy_hbm, sx_hbm, volume_hbm, images_hbm,
    scores_hbm, rows_hbm, line_hbm,
    scores_ref, line_ref, lines_ref, weights_ref, defocus_ref, sy_ref, sx_ref,
    vbuf, ibuf, split, own, arrived, gather, place_s, place_t,
    fx, ephase, fy, hs, cx, term, sent, landed, xsend, xsum, xrecv, ysend, yrecv, zsend, zrecv,
    fin, tile_y, zacc, su,
    small_sem, in_sem, out_sem, s_send, s_recv, p_send, p_recv, x_send, x_recv, z_send, z_recv,
    y_send, y_recv, f_send, f_recv,
):
    dom = lax.axis_index("dom")
    slab = lax.axis_index("slab")
    x_lo = dom // 16
    z = (dom // 2) % 8
    c = dom % 2
    zc = z * 2 + c
    partner = (dom + 1 - 2 * c, slab)
    y = slab // 2
    x_hi = slab % 2
    x = x_hi * 2 + x_lo

    small = [
        pltpu.make_async_copy(src, dst, small_sem.at[i])
        for i, (src, dst) in enumerate(
            (
                (lines_hbm, lines_ref),
                (sx_hbm, sx_ref),
                (sy_hbm, sy_ref),
                (defocus_hbm, defocus_ref),
                (weights_hbm, weights_ref),
            )
        )
    ]
    for load in small:
        load.start()
    loads = []
    for j in range(2):
        cols = pl.ds(j * 128, 128)
        loads.append(pltpu.make_async_copy(volume_hbm.at[:, :, cols], vbuf.at[j], in_sem.at[j]))
    for j in range(2):
        cols = pl.ds(j * 128, 128)
        loads.append(
            pltpu.make_async_copy(images_hbm.at[:, :, :, cols], ibuf.at[j], in_sem.at[2 + j])
        )
    for load in loads:
        load.start()

    barrier = pltpu.get_barrier_semaphore()

    def slab_peer(k):
        to = lax.rem(slab + k, SLABS)
        flip = (to % 2 + x_hi) % 2
        return ((x_lo + flip) % 2) * 16 + zc, to

    def x_peer(k):
        to = lax.rem(x + k, 4)
        return (to % 2) * 16 + zc, y * 2 + to // 2

    def y_peer(k):
        return dom, lax.rem(y + k, YS) * 2 + x_hi

    def z_peer(k):
        return x_lo * 16 + lax.rem(z + k, ZS) * 2 + c, slab

    def group_peer(k):
        to = lax.rem(x_lo * 2 + c + k, 4)
        return (to // 2) * 16 + z * 2 + to % 2, slab

    def greet(peer):
        pl.semaphore_signal(barrier, inc=1, device_id=peer, device_id_type=MESH)

    def greet_slab(k, carry):
        greet(slab_peer(k))
        return carry

    def greet_z(k, carry):
        greet(z_peer(k))
        return carry

    lax.fori_loop(1, SLABS, greet_slab, 0)
    lax.fori_loop(1, ZS, greet_z, 0)
    for k in range(1, 4):
        greet(group_peer(k))
    greet((dom, y * 2 + 1 - x_hi))

    small[0].wait()
    lines = lines_ref[...]
    owner = lines >> 10
    local = (lines & (LINES - 1)).astype(F32)
    slab_rows = iota((SLABS, KS), 0)
    marks = jnp.concatenate(
        [(owner[o : o + 1] == slab_rows).astype(F32) for o in range(ORIENT)], 0
    )
    before = (iota((KS, KS), 0) < iota((KS, KS), 1)).astype(F32).astype(BF16)
    earlier = dot(marks.astype(BF16), before) * marks
    ranks = [
        jnp.sum(earlier[o * SLABS : (o + 1) * SLABS], axis=0, keepdims=True).astype(jnp.int32)
        for o in range(ORIENT)
    ]
    own_line = []
    for o in range(ORIENT):
        mine = (owner[o : o + 1] == slab) & (ranks[o] == slab_rows)
        own_line.append(
            jnp.sum(jnp.where(mine, local[o : o + 1], 0.0), axis=1, keepdims=True)
        )
    own_line = jnp.concatenate(own_line, 0).astype(jnp.int32)
    o_own = 2 * c + z % 2
    first_line = own_line[0:OWNED]
    for o in range(1, ORIENT):
        first_line = jnp.where(o_own == o, own_line[o * OWNED : (o + 1) * OWNED], first_line)
    column = iota((OWNED, 2 * LINES), 1)
    gather[0:OWNED] = (column == 2 * first_line).astype(F32).astype(BF16)
    gather[OWNED:] = (column == 2 * first_line + 1).astype(F32).astype(BF16)

    for j in range(2):
        loads[j].wait()
        picked = dot(gather[...], vbuf.at[j].reshape(2 * LINES, 128)[...]).astype(BF16)
        for part in range(2):
            at = slice(part * KS + j * 128, part * KS + j * 128 + 128)
            own[:, at] = picked[part * OWNED : part * OWNED + OWNED]

    small[1].wait()
    small[2].wait()
    lane = iota((8, 128), 1) % NT
    row_x = jnp.zeros((8, 128), jnp.int32)
    row_y = jnp.zeros((8, 128), jnp.int32)
    for t in range(NT):
        row_x = jnp.where(lane == t, sx_ref[t], row_x)
        row_y = jnp.where(lane == t, sy_ref[t], row_y)
    freq = iota((KS, 128), 0) - HALF
    sin_x, cos_x = turns_sin_cos(freq * row_x[0:1])
    sin_y, cos_y = turns_sin_cos(freq * row_y[0:1])
    wide_lane = iota((KS, 128), 1)
    e_re = jnp.where(wide_lane < NT, cos_y, -sin_y)[:, : 2 * NT].astype(BF16)
    e_im = jnp.where(wide_lane < NT, sin_y, cos_y)[:, : 2 * NT].astype(BF16)
    for block in range(2):
        ephase[block, 0:128] = e_re[block * 128 : block * 128 + 128]
        ephase[block, 128:] = e_im[block * 128 : block * 128 + 128]
    t_cos = cos_x.T[0:NT]
    t_sin = sin_x.T[0:NT]
    table = jnp.concatenate([t_cos, t_sin], 1)
    table_hi = table.astype(BF16)
    table_lo = (table - table_hi.astype(F32)).astype(BF16)
    small[4].wait()
    weights = weights_ref[...]
    weights_hi = weights.astype(BF16)
    weights_lo = (weights - weights_hi.astype(F32)).astype(BF16)
    h = dot(weights_hi, table_hi) + dot(weights_lo, table_hi) + dot(weights_hi, table_lo)
    h = h.astype(BF16).reshape(P_DEV * ORIENT, NT, 2 * KS)
    hs[:, 0:NT] = h[:, :, 0:KS]
    hs[:, NT:] = h[:, :, KS:]
    for o in range(ORIENT):
        rank = ranks[o]
        row = owner[o : o + 1]
        at_t = (row & 1) * 128 + (rank >> 3) * 64 + (row >> 1) * 8 + (rank & 7)
        place_t[o] = (iota((KS, KS), 0) == at_t).astype(F32).astype(BF16)

    freq_row = (iota((8, KS), 1) - HALF).astype(F32)
    which = iota((8, KS), 0)
    focus = jnp.zeros((8, KS), F32)
    small[3].wait()
    for p in range(P_DEV):
        focus = jnp.where(which == p, defocus_ref[p], focus)
    sin_d, cos_d = angle_sin_cos(focus * (freq_row * freq_row * (1.0 / (HALF * HALF))))
    sin_col = sin_d.T
    cos_col = cos_d.T
    u_row = 0.1 * sin_d - 0.995 * cos_d
    v_row = -0.995 * sin_d - 0.1 * cos_d
    loads[2].wait()
    loads[3].wait()
    for p in range(P_DEV):
        sin_p = jnp.broadcast_to(sin_col[:, p : p + 1], (KS, 128))
        cos_p = jnp.broadcast_to(cos_col[:, p : p + 1], (KS, 128))
        for j in range(2):
            at = slice(j * 128, j * 128 + 128)
            split[...] = ibuf.at[j, p].reshape(2 * KS, 128)[...].astype(F32)
            ctf = (
                sin_p * u_row[p : p + 1, at]
                + cos_p * v_row[p : p + 1, at]
            )
            cx[p, 0, :, at] = ctf * split[pl.ds(0, KS, stride=2), :]
            cx[p, 1, :, at] = ctf * split[pl.ds(1, KS, stride=2), :]

    def placed_term(o):
        for block in range(2):
            at = slice(block * 128, block * 128 + 128)
            t_re = None
            for p in range(P_DEV):
                table_h = hs[p * ORIENT + o]
                g = dot(ephase[block], table_h)
                g_re = g[0:128]
                g_im = g[128:]
                c_re = cx[p, 0, at]
                c_im = cx[p, 1, at]
                if t_re is None:
                    t_re = c_re * g_re - c_im * g_im
                    t_im = c_re * g_im + c_im * g_re
                else:
                    t_re += c_re * g_re - c_im * g_im
                    t_im += c_re * g_im + c_im * g_re
            term[at, 0:KS] = t_re.astype(BF16)
            term[at, KS:] = t_im.astype(BF16)
        return dot(place_t[o], term[...])

    def pair_copy(j):
        return pltpu.make_async_remote_copy(
            src_ref=sent.at[j],
            dst_ref=landed.at[j],
            send_sem=p_send.at[j],
            recv_sem=p_recv.at[j],
            device_id=partner,
            device_id_type=MESH,
        )

    def x_copy(j, step):
        ahead = 1 + 2 * j
        back = 3 - 2 * j
        src, dst, k = (
            (xsend.at[j, lax.rem(x + 2, 4)], xrecv.at[j, 0], ahead),
            (xsend.at[j, lax.rem(x + back, 4)], xrecv.at[j, 1], back),
            (xsum.at[j], xrecv.at[j, 2], ahead),
        )[step]
        return pltpu.make_async_remote_copy(
            src_ref=src,
            dst_ref=dst,
            send_sem=x_send.at[j, step],
            recv_sem=x_recv.at[j, step],
            device_id=x_peer(k),
            device_id_type=MESH,
        )

    def y_copy(j, k):
        return pltpu.make_async_remote_copy(
            src_ref=ysend.at[j, lax.rem(y + k, YS)],
            dst_ref=yrecv.at[j, y],
            send_sem=y_send.at[j],
            recv_sem=y_recv.at[j],
            device_id=y_peer(k),
            device_id_type=MESH,
        )

    def z_copy(j, k):
        return pltpu.make_async_remote_copy(
            src_ref=zsend.at[j],
            dst_ref=zrecv.at[j, z],
            send_sem=z_send.at[j],
            recv_sem=z_recv.at[j],
            device_id=z_peer(k),
            device_id_type=MESH,
        )

    def give(j, carry):
        sent[j] = placed_term(2 * (1 - c) + j).astype(BF16)
        return carry

    lax.fori_loop(0, 2, give, 0)

    pl.semaphore_wait(barrier, SLABS - 1 + ZS - 1 + 3 + 1)

    pair_copy(0).start()
    pair_copy(1).start()

    def slab_copy(k):
        return pltpu.make_async_remote_copy(
            src_ref=own,
            dst_ref=arrived.at[o_own, slab],
            send_sem=s_send.at[0],
            recv_sem=s_recv.at[0],
            device_id=slab_peer(k),
            device_id_type=MESH,
        )

    def send_slab(k, carry):
        slab_copy(k).start()
        return carry

    lax.fori_loop(1, SLABS, send_slab, 0)
    arrived[o_own, slab] = own[...]


    def keep(j, carry):
        mine = placed_term(2 * c + j)
        pair_copy(j).wait_recv()
        both = (mine + landed[j].astype(F32)).astype(BF16)
        xsend[j] = both.reshape(4, 64, 2 * KS)

        x_copy(j, 0).start()
        x_copy(j, 1).start()
        return carry

    lax.fori_loop(0, 2, keep, 0)

    def relay(j, carry):
        x_copy(j, 0).wait_recv()
        mine = xsend[j, lax.rem(x + 1 + 2 * j, 4)]
        xsum[j] = (mine.astype(F32) + xrecv[j, 0].astype(F32)).astype(BF16)
        x_copy(j, 2).start()
        return carry

    lax.fori_loop(0, 2, relay, 0)

    def wait_rows(n, sem):
        part = arrived.at[0, pl.ds(0, n)]
        pltpu.make_async_copy(part, part, sem).wait()

    def pass_rows(o, sem, first=0, n=SLABS, to=partner):
        part = arrived.at[o, pl.ds(first, n)]
        return pltpu.make_async_remote_copy(
            src_ref=part,
            dst_ref=part,
            send_sem=s_send.at[sem],
            recv_sem=s_recv.at[sem],
            device_id=to,
            device_id_type=MESH,
        )

    at_s = [owner[o : o + 1] * OWNED + ranks[o] for o in range(ORIENT)]
    at_s = jnp.concatenate(at_s + at_s, 0).astype(F32).T.astype(jnp.int32)
    for o in range(ORIENT):
        place_s[o] = (iota((KS, KS), 1) == at_s[:, o : o + 1]).astype(F32).astype(BF16)
    group = wide_lane // NT
    for o in range(ORIENT):
        cos_o = jnp.where(group == o, cos_x, 0.0).astype(BF16)
        sin_o = jnp.where(group == o, sin_x, 0.0).astype(BF16)
        at = (o // 2) * 2 * KS
        fx[o % 2, at : at + KS, 0:128] = cos_o
        fx[o % 2, at : at + KS, 128:] = -sin_o
        fx[o % 2, at + KS : at + 2 * KS, 0:128] = sin_o
        fx[o % 2, at + KS : at + 2 * KS, 128:] = cos_o
    table_y = jnp.concatenate([cos_y.T[0:NT], sin_y.T[0:NT]], 1) * (1.0 / KS)
    fy_hi = table_y.astype(BF16)
    fy[0:NT] = fy_hi
    fy[NT:] = (table_y - fy_hi.astype(F32)).astype(BF16)

    def correlate(parity, first):
        for j in range(2):
            o = 2 * j + parity
            su[j] = dot(place_s[o], arrived[o].reshape(KS, 2 * KS))
        for block in range(2):
            at = slice(block * 128, block * 128 + 128)
            for p in range(P_DEV):
                c_re = cx[p, 0, at]
                c_im = cx[p, 1, at]
                q = []
                for j in range(2):
                    s_re = su[j, at, 0:KS]
                    s_im = su[j, at, KS:]
                    q.append((s_re * c_re + s_im * c_im).astype(BF16))
                    q.append((s_re * c_im - s_im * c_re).astype(BF16))
                part = dot(jnp.concatenate(q, 1), fx[parity])
                if first:
                    zacc[p, at] = part
                else:
                    zacc[p, at] += part

    line_row = jnp.concatenate([2 * own_line, 2 * own_line + 1], 0).astype(F32)
    line_row = jnp.broadcast_to(line_row, (128, 128)).T[0:8].astype(jnp.int32)
    line_ref[...] = line_row
    outs = [pltpu.make_async_copy(line_ref, line_hbm, out_sem.at[0])]
    outs[0].start()
    wait_rows(SLABS - 1, s_recv.at[0])
    to_up = pass_rows(o_own, 2, 0, 8, z_peer(1))
    to_down = pass_rows(o_own, 3, 8, 8, z_peer(ZS - 1))
    to_partner = pass_rows(o_own, 1)
    to_up.start()
    to_down.start()
    to_partner.start()

    def pass_on(j, carry):
        x_copy(j, 1).wait_recv()
        x_copy(j, 2).wait_recv()
        for part in range(2):
            at = slice(part * KS, part * KS + KS)
            total = xsend[j, x, :, at].astype(F32)
            for other in range(1, 3):
                total += xrecv[j, other, :, at].astype(F32)
            tile_y[:, part * 8 : part * 8 + 8] = total.reshape(YS, 8, KS)
        ysend[j] = tile_y[...].astype(BF16)

        def send_y(k, inner):
            y_copy(j, k).start()
            return inner

        lax.fori_loop(1, YS, send_y, 0)
        yrecv[j, y] = ysend[j, y]
        return carry

    lax.fori_loop(0, 2, pass_on, 0)
    wait_rows(SLABS, s_recv.at[1])
    correlate(z % 2, True)
    wait_rows(8, s_recv.at[2])
    wait_rows(8, s_recv.at[3])
    to_partner_too = pass_rows(2 * c + 1 - z % 2, 4)
    to_partner_too.start()

    def spread(j, carry):
        pltpu.make_async_copy(
            yrecv.at[j, pl.ds(0, YS - 1)], yrecv.at[j, pl.ds(0, YS - 1)], y_recv.at[j]
        ).wait()
        total = yrecv[j, 0].astype(F32)
        for other in range(1, YS):
            total += yrecv[j, other].astype(F32)
        zsend[j] = total.astype(BF16)

        def send_z(k, inner):
            z_copy(j, k).start()
            return inner

        lax.fori_loop(1, ZS, send_z, 0)
        zrecv[j, z] = zsend[j]
        return carry

    lax.fori_loop(0, 2, spread, 0)
    wait_rows(SLABS, s_recv.at[4])
    correlate(1 - z % 2, False)

    place = x_lo * 2 + c
    for j in range(2):
        pltpu.make_async_copy(
            zrecv.at[j, pl.ds(0, ZS - 1)], zrecv.at[j, pl.ds(0, ZS - 1)], z_recv.at[j]
        ).wait()
        total = zrecv[j, 0].astype(F32)
        for other in range(1, ZS):
            total += zrecv[j, other].astype(F32)
        fin[place, j] = (total * SCALE).astype(BF16)

    def group_copy(k):
        return pltpu.make_async_remote_copy(
            src_ref=fin.at[place],
            dst_ref=fin.at[place],
            send_sem=f_send.at[0],
            recv_sem=f_recv.at[0],
            device_id=group_peer(k),
            device_id_type=MESH,
        )

    for k in range(1, 4):
        group_copy(k).start()
    for p in range(P_DEV):
        full = jnp.concatenate([zacc[p, :, 0:128], zacc[p, :, 128:]], 0)
        full_hi = full.astype(BF16)
        full_lo = (full - full_hi.astype(F32)).astype(BF16)
        both = dot(fy[...], full_hi)
        scores_ref[p] = both[0:NT] + both[NT:] + dot(fy[0:NT], full_lo)
    outs.append(pltpu.make_async_copy(scores_ref, scores_hbm, out_sem.at[1]))
    outs[1].start()

    pltpu.make_async_copy(fin.at[pl.ds(0, 3)], fin.at[pl.ds(0, 3)], f_recv.at[0]).wait()
    outs.append(pltpu.make_async_copy(fin, rows_hbm, out_sem.at[2]))
    outs[2].start()

    wait_rows(SLABS - 1, s_send.at[0])
    for sent_rows in (to_partner, to_up, to_down, to_partner_too):
        sent_rows.wait_send()
    for j in range(2):
        pair_copy(j).wait_send()
    for j in range(2):
        for step in range(3):
            x_copy(j, step).wait_send()
    for j in range(2):
        pltpu.make_async_copy(
            yrecv.at[j, pl.ds(0, YS - 1)], yrecv.at[j, pl.ds(0, YS - 1)], y_send.at[j]
        ).wait()
        pltpu.make_async_copy(
            zrecv.at[j, pl.ds(0, ZS - 1)], zrecv.at[j, pl.ds(0, ZS - 1)], z_send.at[j]
        ).wait()
    pltpu.make_async_copy(fin.at[pl.ds(0, 3)], fin.at[pl.ds(0, 3)], f_send.at[0]).wait()
    for out in outs:
        out.wait()


def finish(
    fin_hbm, line_hbm, found_hbm, scores_hbm, update_hbm,
    fin_ref, line_ref, found_ref, scores_ref, insert, rows, buf, in_sem, out_sem,
):
    loads = [
        pltpu.make_async_copy(src, dst, in_sem.at[i])
        for i, (src, dst) in enumerate(
            ((line_hbm, line_ref), (fin_hbm, fin_ref), (found_hbm, found_ref))
        )
    ]
    for load in loads:
        load.start()
    loads[0].wait()
    insert[...] = (iota((2 * LINES, 128), 0) == line_ref[0:1]).astype(F32).astype(BF16)
    loads[1].wait()
    for o in range(ORIENT):
        for r in range(2):
            got = fin_ref[r * 2 + o // 2, o % 2].astype(F32)
            for part in range(2):
                first = part * 64 + o * OWNED + r * 8
                rows[first : first + 8] = got[part * 8 : part * 8 + 8]
    rows_bf16 = rows[...].astype(BF16)
    outs = []
    for piece in range(4):
        of = pl.ds(piece * 256, 256)
        at = slice(piece * 512, piece * 512 + 512)
        placed = dot(insert[at], rows_bf16).astype(BF16)
        for j in range(2):
            buf.at[j, of].reshape(512, 128)[...] = placed[:, j * 128 : j * 128 + 128]
            outs.append(
                pltpu.make_async_copy(
                    buf.at[j, of],
                    update_hbm.at[of, :, pl.ds(j * 128, 128)],
                    out_sem.at[piece * 2 + j],
                )
            )
            outs[-1].start()
    loads[2].wait()
    for o in range(ORIENT):
        scores_ref[:, o] = found_ref[:, :, o * NT : (o + 1) * NT]
    outs.append(pltpu.make_async_copy(scores_ref, scores_hbm, out_sem.at[8]))
    outs[-1].start()
    for out in outs:
        out.wait()


def body(volume, images, defocus, soft_weights, slice_lines, shift_y, shift_x):
    hbm = pl.BlockSpec(memory_space=pltpu.HBM)
    dma = pltpu.SemaphoreType.DMA
    found, rows, line = pl.pallas_call(
        kernel,
        out_shape=(
            jax.ShapeDtypeStruct((P_DEV, NT, ORIENT * NT), F32),
            jax.ShapeDtypeStruct((4, 2, 16, KS), BF16),
            jax.ShapeDtypeStruct((8, 128), jnp.int32),
        ),
        in_specs=[hbm] * 7,
        out_specs=(hbm, hbm, hbm),
        scratch_shapes=[
            pltpu.VMEM((P_DEV, NT, ORIENT * NT), F32),
            pltpu.VMEM((8, 128), jnp.int32),
            pltpu.VMEM((ORIENT, KS), jnp.int32),
            pltpu.VMEM((P_DEV * ORIENT * NT, NT), F32),
            pltpu.SMEM((P_DEV,), F32),
            pltpu.SMEM((NT,), jnp.int32),
            pltpu.SMEM((NT,), jnp.int32),
            pltpu.VMEM((2, LINES, 2, 128), BF16),
            pltpu.VMEM((2, P_DEV, KS, 2, 128), BF16),
            pltpu.VMEM((2 * KS, 128), F32),
            pltpu.VMEM((OWNED, 2 * KS), BF16),
            pltpu.VMEM((ORIENT, SLABS, OWNED, 2 * KS), BF16),
            pltpu.VMEM((2 * OWNED, 2 * LINES), BF16),
            pltpu.VMEM((ORIENT, KS, KS), BF16),
            pltpu.VMEM((ORIENT, KS, KS), BF16),
            pltpu.VMEM((2, 4 * KS, 256), BF16),
            pltpu.VMEM((2, KS, 2 * NT), BF16),
            pltpu.VMEM((2 * NT, 2 * KS), BF16),
            pltpu.VMEM((P_DEV * ORIENT, 2 * NT, KS), BF16),
            pltpu.VMEM((P_DEV, 2, KS, KS), F32),
            pltpu.VMEM((KS, 2 * KS), BF16),
            pltpu.VMEM((2, KS, 2 * KS), BF16),
            pltpu.VMEM((2, KS, 2 * KS), BF16),
            pltpu.VMEM((2, 4, 64, 2 * KS), BF16),
            pltpu.VMEM((2, 64, 2 * KS), BF16),
            pltpu.VMEM((2, 3, 64, 2 * KS), BF16),
            pltpu.VMEM((2, YS, 16, KS), BF16),
            pltpu.VMEM((2, YS, 16, KS), BF16),
            pltpu.VMEM((2, 16, KS), BF16),
            pltpu.VMEM((2, ZS, 16, KS), BF16),
            pltpu.VMEM((4, 2, 16, KS), BF16),
            pltpu.VMEM((YS, 16, KS), F32),
            pltpu.VMEM((P_DEV, KS, 256), F32),
            pltpu.VMEM((2, KS, 2 * KS), F32),
            dma((5,)),
            dma((4,)),
            dma((3,)),
            dma((5,)),
            dma((5,)),
            dma((2,)),
            dma((2,)),
            dma((2, 3)),
            dma((2, 3)),
            dma((2,)),
            dma((2,)),
            dma((2,)),
            dma((2,)),
            dma((1,)),
            dma((1,)),
        ],
        compiler_params=pltpu.CompilerParams(
            collective_id=0, has_side_effects=True, vmem_limit_bytes=60 * 1024 * 1024
        ),
        name="cryo",
    )(
        slice_lines,
        soft_weights.reshape(P_DEV * ORIENT * NT, NT),
        defocus,
        shift_y,
        shift_x,
        volume,
        images,
    )
    return pl.pallas_call(
        finish,
        out_shape=(
            jax.ShapeDtypeStruct((P_DEV, ORIENT, NT, NT), F32),
            jax.ShapeDtypeStruct((LINES, 2, KS), BF16),
        ),
        in_specs=[hbm] * 3,
        out_specs=(hbm, hbm),
        scratch_shapes=[
            pltpu.VMEM((4, 2, 16, KS), BF16),
            pltpu.VMEM((8, 128), jnp.int32),
            pltpu.VMEM((P_DEV, NT, ORIENT * NT), F32),
            pltpu.VMEM((P_DEV, ORIENT, NT, NT), F32),
            pltpu.VMEM((2 * LINES, 2 * ORIENT * OWNED), BF16),
            pltpu.VMEM((2 * ORIENT * OWNED, KS), F32),
            pltpu.VMEM((2, LINES, 2, 128), BF16),
            dma((3,)),
            dma((9,)),
        ],
        compiler_params=pltpu.CompilerParams(vmem_limit_bytes=60 * 1024 * 1024),
        name="finish",
    )(rows, line, found)


def solution(mesh):
    placed = (
        P("slab", None, None),
        P(("dom", "slab"), None, None, None),
        P(("dom", "slab")),
        P(("dom", "slab"), None, None, None),
        P(),
        P(),
        P(),
    )
    return jax.shard_map(
        body,
        mesh=mesh,
        in_specs=placed,
        out_specs=(P(("dom", "slab"), None, None, None), P("slab", None, None)),
        check_vma=False,
    )
```

```python
import math

import jax
import jax.numpy as jnp
from jax import lax
from jax.experimental import pallas as pl
from jax.experimental.pallas import tpu as pltpu
from jax.sharding import PartitionSpec as P

KS = 256
HALF = KS // 2
P_DEV = 4
LINES = 1024
ORIENT = 4
NT = 32
OWNED = 16
PARTICLES = 2048
SLABS = 16
ZS = 8
YS = 8
XLO = 2
SCALE = 1.0 / math.sqrt(NT * NT * PARTICLES)
F32 = jnp.float32
BF16 = jnp.bfloat16
MESH = pl.DeviceIdType.MESH


def dot(a, b):
    return jnp.dot(a, b, preferred_element_type=F32)


def poly_sin_cos(r):
    s = r * r
    sin = r * (1.0 + s * (-1 / 6 + s * (1 / 120 + s * (-1 / 5040 + s * (1 / 362880)))))
    cos = 1.0 + s * (-0.5 + s * (1 / 24 + s * (-1 / 720 + s * (1 / 40320))))
    return sin, cos


def rotate(quadrant, sin, cos):
    q = quadrant & 3
    odd = (q & 1) == 1
    s = jnp.where(odd, cos, sin)
    c = jnp.where(odd, sin, cos)
    s = jnp.where(q >= 2, -s, s)
    c = jnp.where((q == 1) | (q == 2), -c, c)
    return s, c


def turns_sin_cos(turns):
    t = turns & (KS - 1)
    q = (t + KS // 8) >> 6
    r = (t - (q << 6)).astype(F32) * (2.0 * math.pi / KS)
    return rotate(q, *poly_sin_cos(r))


def angle_sin_cos(x):
    n = jnp.floor(x * (2.0 / math.pi) + 0.5)
    r = x - n * 1.5703125
    r = r - n * 4.837512969970703e-4
    r = r - n * 7.549789948768648e-8
    return rotate(n.astype(jnp.int32), *poly_sin_cos(r))


def iota(shape, dim):
    return lax.broadcasted_iota(jnp.int32, shape, dim)


def kernel(
    lines_hbm, weights_hbm, defocus_hbm, sy_hbm, sx_hbm, volume_hbm, images_hbm,
    scores_hbm, rows_hbm, line_hbm,
    scores_ref, line_ref, lines_ref, weights_ref, defocus_ref, sy_ref, sx_ref,
    vbuf, ibuf, split, own, arrived, gather, place_s, place_t,
    fx, ephase, fy, hs, cx, term, sent, landed, xsend, xrecv, ysend, yrecv, zsend, zrecv,
    fin, tile_y, zacc, su, cq, q,
    small_sem, in_sem, out_sem, s_send, s_recv, p_send, p_recv, x_send, x_recv, z_send, z_recv,
    y_send, y_recv, f_send, f_recv,
):
    dom = lax.axis_index("dom")
    slab = lax.axis_index("slab")
    x_lo = dom // 16
    z = (dom // 2) % 8
    c = dom % 2
    zc = z * 2 + c
    partner = (dom + 1 - 2 * c, slab)
    y = slab // 2
    x_hi = slab % 2
    x = x_hi * 2 + x_lo

    small = [
        pltpu.make_async_copy(src, dst, small_sem.at[i])
        for i, (src, dst) in enumerate(
            (
                (lines_hbm, lines_ref),
                (sx_hbm, sx_ref),
                (sy_hbm, sy_ref),
                (defocus_hbm, defocus_ref),
                (weights_hbm, weights_ref),
            )
        )
    ]
    for load in small:
        load.start()
    loads = []
    for j in range(2):
        cols = pl.ds(j * 128, 128)
        loads.append(pltpu.make_async_copy(volume_hbm.at[:, :, cols], vbuf.at[j], in_sem.at[j]))
    for j in range(2):
        cols = pl.ds(j * 128, 128)
        loads.append(
            pltpu.make_async_copy(images_hbm.at[:, :, :, cols], ibuf.at[j], in_sem.at[2 + j])
        )
    for load in loads:
        load.start()

    barrier = pltpu.get_barrier_semaphore()

    def slab_peer(k):
        to = lax.rem(slab + k, SLABS)
        flip = (to % 2 + x_hi) % 2
        return ((x_lo + flip) % 2) * 16 + zc, to

    def x_peer(k):
        to = lax.rem(x + k, 4)
        return (to % 2) * 16 + zc, y * 2 + to // 2

    def y_peer(k):
        return dom, lax.rem(y + k, YS) * 2 + x_hi

    def z_peer(k):
        return x_lo * 16 + lax.rem(z + k, ZS) * 2 + c, slab

    def group_peer(k):
        to = lax.rem(x_lo * 2 + c + k, 4)
        return (to // 2) * 16 + z * 2 + to % 2, slab

    def greet(peer):
        pl.semaphore_signal(barrier, inc=1, device_id=peer, device_id_type=MESH)

    def greet_slab(k, carry):
        greet(slab_peer(k))
        return carry

    def greet_z(k, carry):
        greet(z_peer(k))
        return carry

    lax.fori_loop(1, SLABS, greet_slab, 0)
    lax.fori_loop(1, ZS, greet_z, 0)
    for k in range(1, 4):
        greet(group_peer(k))
    greet((dom, y * 2 + 1 - x_hi))

    small[0].wait()
    lines = lines_ref[...]
    owner = lines >> 10
    local = (lines & (LINES - 1)).astype(F32)
    slab_rows = iota((SLABS, KS), 0)
    marks = jnp.concatenate(
        [(owner[o : o + 1] == slab_rows).astype(F32) for o in range(ORIENT)], 0
    )
    before = (iota((KS, KS), 0) < iota((KS, KS), 1)).astype(F32).astype(BF16)
    earlier = dot(marks.astype(BF16), before) * marks
    ranks = [
        jnp.sum(earlier[o * SLABS : (o + 1) * SLABS], axis=0, keepdims=True).astype(jnp.int32)
        for o in range(ORIENT)
    ]
    own_line = []
    for o in range(ORIENT):
        mine = (owner[o : o + 1] == slab) & (ranks[o] == slab_rows)
        own_line.append(
            jnp.sum(jnp.where(mine, local[o : o + 1], 0.0), axis=1, keepdims=True)
        )
    own_line = jnp.concatenate(own_line, 0).astype(jnp.int32)
    o_own = 2 * c + z % 2
    first_line = own_line[0:OWNED]
    for o in range(1, ORIENT):
        first_line = jnp.where(o_own == o, own_line[o * OWNED : (o + 1) * OWNED], first_line)
    column = iota((OWNED, 2 * LINES), 1)
    gather[0:OWNED] = (column == 2 * first_line).astype(F32).astype(BF16)
    gather[OWNED:] = (column == 2 * first_line + 1).astype(F32).astype(BF16)

    for j in range(2):
        loads[j].wait()
        picked = dot(gather[...], vbuf.at[j].reshape(2 * LINES, 128)[...]).astype(BF16)
        for part in range(2):
            at = slice(part * KS + j * 128, part * KS + j * 128 + 128)
            own[:, at] = picked[part * OWNED : part * OWNED + OWNED]

    small[1].wait()
    small[2].wait()
    lane = iota((8, 128), 1) % NT
    row_x = jnp.zeros((8, 128), jnp.int32)
    row_y = jnp.zeros((8, 128), jnp.int32)
    for t in range(NT):
        row_x = jnp.where(lane == t, sx_ref[t], row_x)
        row_y = jnp.where(lane == t, sy_ref[t], row_y)
    freq = iota((KS, 128), 0) - HALF
    sin_x, cos_x = turns_sin_cos(freq * row_x[0:1])
    sin_y, cos_y = turns_sin_cos(freq * row_y[0:1])
    wide_lane = iota((KS, 128), 1)
    e_re = jnp.where(wide_lane < NT, cos_y, -sin_y)[:, : 2 * NT].astype(BF16)
    e_im = jnp.where(wide_lane < NT, sin_y, cos_y)[:, : 2 * NT].astype(BF16)
    for block in range(2):
        ephase[block, 0:128] = e_re[block * 128 : block * 128 + 128]
        ephase[block, 128:] = e_im[block * 128 : block * 128 + 128]
    t_cos = cos_x.T[0:NT]
    t_sin = sin_x.T[0:NT]
    table = jnp.concatenate([t_cos, t_sin], 1)
    table_hi = table.astype(BF16)
    table_lo = (table - table_hi.astype(F32)).astype(BF16)
    small[4].wait()
    weights = weights_ref[...]
    weights_hi = weights.astype(BF16)
    weights_lo = (weights - weights_hi.astype(F32)).astype(BF16)
    h = dot(weights_hi, table_hi) + dot(weights_lo, table_hi) + dot(weights_hi, table_lo)
    h = h.astype(BF16).reshape(P_DEV * ORIENT, NT, 2 * KS)
    hs[:, 0:NT] = h[:, :, 0:KS]
    hs[:, NT:] = h[:, :, KS:]
    for o in range(ORIENT):
        rank = ranks[o]
        row = owner[o : o + 1]
        at_t = (row & 1) * 128 + (rank >> 3) * 64 + (row >> 1) * 8 + (rank & 7)
        place_t[o] = (iota((KS, KS), 0) == at_t).astype(F32).astype(BF16)

    freq_row = (iota((8, KS), 1) - HALF).astype(F32)
    which = iota((8, KS), 0)
    focus = jnp.zeros((8, KS), F32)
    small[3].wait()
    for p in range(P_DEV):
        focus = jnp.where(which == p, defocus_ref[p], focus)
    sin_d, cos_d = angle_sin_cos(focus * (freq_row * freq_row * (1.0 / (HALF * HALF))))
    sin_col = sin_d.T
    cos_col = cos_d.T
    u_row = 0.1 * sin_d - 0.995 * cos_d
    v_row = -0.995 * sin_d - 0.1 * cos_d
    loads[2].wait()
    loads[3].wait()
    for p in range(P_DEV):
        sin_p = jnp.broadcast_to(sin_col[:, p : p + 1], (KS, 128))
        cos_p = jnp.broadcast_to(cos_col[:, p : p + 1], (KS, 128))
        for j in range(2):
            at = slice(j * 128, j * 128 + 128)
            split[...] = ibuf.at[j, p].reshape(2 * KS, 128)[...].astype(F32)
            ctf = (
                sin_p * u_row[p : p + 1, at]
                + cos_p * v_row[p : p + 1, at]
            )
            for part in range(2):
                product = ctf * split[pl.ds(part, KS, stride=2), :]
                cx[p, part, :, at] = product
                cq[p, part, :, at] = product.astype(BF16)

    def placed_term(o):
        for block in range(2):
            at = slice(block * 128, block * 128 + 128)
            t_re = None
            for p in range(P_DEV):
                table_h = hs[p * ORIENT + o]
                g = dot(ephase[block], table_h)
                g_re = g[0:128]
                g_im = g[128:]
                c_re = cx[p, 0, at]
                c_im = cx[p, 1, at]
                if t_re is None:
                    t_re = c_re * g_re - c_im * g_im
                    t_im = c_re * g_im + c_im * g_re
                else:
                    t_re += c_re * g_re - c_im * g_im
                    t_im += c_re * g_im + c_im * g_re
            term[at, 0:KS] = t_re.astype(BF16)
            term[at, KS:] = t_im.astype(BF16)
        return dot(place_t[o], term[...])

    def pair_copy(j):
        return pltpu.make_async_remote_copy(
            src_ref=sent.at[j],
            dst_ref=landed.at[j],
            send_sem=p_send.at[j],
            recv_sem=p_recv.at[j],
            device_id=partner,
            device_id_type=MESH,
        )

    def x_copy(j, k):
        return pltpu.make_async_remote_copy(
            src_ref=xsend.at[j, lax.rem(x + k, 4)],
            dst_ref=xrecv.at[j, x],
            send_sem=x_send.at[j],
            recv_sem=x_recv.at[j],
            device_id=x_peer(k),
            device_id_type=MESH,
        )

    def y_copy(j, k):
        return pltpu.make_async_remote_copy(
            src_ref=ysend.at[j, lax.rem(y + k, YS)],
            dst_ref=yrecv.at[j, y],
            send_sem=y_send.at[j],
            recv_sem=y_recv.at[j],
            device_id=y_peer(k),
            device_id_type=MESH,
        )

    def z_copy(j, k):
        return pltpu.make_async_remote_copy(
            src_ref=zsend.at[j],
            dst_ref=zrecv.at[j, z],
            send_sem=z_send.at[j],
            recv_sem=z_recv.at[j],
            device_id=z_peer(k),
            device_id_type=MESH,
        )

    def give(j, carry):
        sent[j] = placed_term(2 * (1 - c) + j).astype(BF16)
        return carry

    lax.fori_loop(0, 2, give, 0)

    pl.semaphore_wait(barrier, SLABS - 1 + ZS - 1 + 3 + 1)

    pair_copy(0).start()
    pair_copy(1).start()

    def slab_copy(k):
        return pltpu.make_async_remote_copy(
            src_ref=own,
            dst_ref=arrived.at[o_own, slab],
            send_sem=s_send.at[0],
            recv_sem=s_recv.at[0],
            device_id=slab_peer(k),
            device_id_type=MESH,
        )

    def send_slab(k, carry):
        slab_copy(k).start()
        return carry

    lax.fori_loop(1, SLABS, send_slab, 0)
    arrived[o_own, slab] = own[...]


    def keep(j, carry):
        mine = placed_term(2 * c + j)
        pair_copy(j).wait_recv()
        both = (mine + landed[j].astype(F32)).astype(BF16)
        xsend[j] = both.reshape(4, 64, 2 * KS)

        def send_x(k, inner):
            x_copy(j, k).start()
            return inner

        lax.fori_loop(1, 4, send_x, 0)
        xrecv[j, x] = xsend[j, x]
        return carry

    lax.fori_loop(0, 2, keep, 0)

    def wait_rows(n, sem):
        part = arrived.at[0, pl.ds(0, n)]
        pltpu.make_async_copy(part, part, sem).wait()

    def pass_rows(o, sem, first=0, n=SLABS, to=partner):
        part = arrived.at[o, pl.ds(first, n)]
        return pltpu.make_async_remote_copy(
            src_ref=part,
            dst_ref=part,
            send_sem=s_send.at[sem],
            recv_sem=s_recv.at[sem],
            device_id=to,
            device_id_type=MESH,
        )

    at_s = [owner[o : o + 1] * OWNED + ranks[o] for o in range(ORIENT)]
    at_s = jnp.concatenate(at_s + at_s, 0).astype(F32).T.astype(jnp.int32)
    for o in range(ORIENT):
        place_s[o] = (iota((KS, KS), 1) == at_s[:, o : o + 1]).astype(F32).astype(BF16)
    group = wide_lane // NT
    for o in range(ORIENT):
        cos_o = jnp.where(group == o, cos_x, 0.0).astype(BF16)
        sin_o = jnp.where(group == o, sin_x, 0.0).astype(BF16)
        at = (o // 2) * 2 * KS
        fx[o % 2, at : at + KS, 0:128] = cos_o
        fx[o % 2, at : at + KS, 128:] = -sin_o
        fx[o % 2, at + KS : at + 2 * KS, 0:128] = sin_o
        fx[o % 2, at + KS : at + 2 * KS, 128:] = cos_o
    table_y = jnp.concatenate([cos_y.T[0:NT], sin_y.T[0:NT]], 1) * (1.0 / KS)
    fy_hi = table_y.astype(BF16)
    fy[0:NT] = fy_hi
    fy[NT:] = (table_y - fy_hi.astype(F32)).astype(BF16)

    def correlate(parity, first):
        for j in range(2):
            o = 2 * j + parity
            su[j] = dot(place_s[o], arrived[o].reshape(KS, 2 * KS)).astype(BF16)
        for p in range(P_DEV):
            for block in range(2):
                at = slice(block * 128, block * 128 + 128)
                c_re = cq[p, 0, at]
                c_im = cq[p, 1, at]
                for j in range(2):
                    s_re = su[j, at, 0:KS]
                    s_im = su[j, at, KS:]
                    q[p, at, 2 * j * KS : (2 * j + 1) * KS] = s_re * c_re + s_im * c_im
                    q[p, at, (2 * j + 1) * KS : (2 * j + 2) * KS] = s_re * c_im - s_im * c_re
            part = dot(q[p], fx[parity])
            if first:
                zacc[p] = part
            else:
                zacc[p] += part

    line_row = jnp.concatenate([2 * own_line, 2 * own_line + 1], 0).astype(F32)
    line_row = jnp.broadcast_to(line_row, (128, 128)).T[0:8].astype(jnp.int32)
    line_ref[...] = line_row
    outs = [pltpu.make_async_copy(line_ref, line_hbm, out_sem.at[0])]
    outs[0].start()
    wait_rows(SLABS - 1, s_recv.at[0])
    to_up = pass_rows(o_own, 2, 0, 8, z_peer(1))
    to_down = pass_rows(o_own, 3, 8, 8, z_peer(ZS - 1))
    to_partner = pass_rows(o_own, 1)
    to_up.start()
    to_down.start()
    to_partner.start()

    def pass_on(j, carry):
        pltpu.make_async_copy(
            xrecv.at[j, pl.ds(0, 3)], xrecv.at[j, pl.ds(0, 3)], x_recv.at[j]
        ).wait()
        for part in range(2):
            at = slice(part * KS, part * KS + KS)
            total = xrecv[j, 0, :, at].astype(F32)
            for other in range(1, 4):
                total += xrecv[j, other, :, at].astype(F32)
            tile_y[:, part * 8 : part * 8 + 8] = total.reshape(YS, 8, KS)
        ysend[j] = tile_y[...].astype(BF16)

        def send_y(k, inner):
            y_copy(j, k).start()
            return inner

        lax.fori_loop(1, YS, send_y, 0)
        yrecv[j, y] = ysend[j, y]
        return carry

    lax.fori_loop(0, 2, pass_on, 0)
    wait_rows(SLABS, s_recv.at[1])
    correlate(z % 2, True)
    wait_rows(8, s_recv.at[2])
    wait_rows(8, s_recv.at[3])
    to_partner_too = pass_rows(2 * c + 1 - z % 2, 4)
    to_partner_too.start()

    def spread(j, carry):
        pltpu.make_async_copy(
            yrecv.at[j, pl.ds(0, YS - 1)], yrecv.at[j, pl.ds(0, YS - 1)], y_recv.at[j]
        ).wait()
        total = yrecv[j, 0].astype(F32)
        for other in range(1, YS):
            total += yrecv[j, other].astype(F32)
        zsend[j] = total.astype(BF16)

        def send_z(k, inner):
            z_copy(j, k).start()
            return inner

        lax.fori_loop(1, ZS, send_z, 0)
        zrecv[j, z] = zsend[j]
        return carry

    lax.fori_loop(0, 2, spread, 0)
    wait_rows(SLABS, s_recv.at[4])
    correlate(1 - z % 2, False)

    place = x_lo * 2 + c
    for j in range(2):
        pltpu.make_async_copy(
            zrecv.at[j, pl.ds(0, ZS - 1)], zrecv.at[j, pl.ds(0, ZS - 1)], z_recv.at[j]
        ).wait()
        total = zrecv[j, 0].astype(F32)
        for other in range(1, ZS):
            total += zrecv[j, other].astype(F32)
        fin[place, j] = (total * SCALE).astype(BF16)

    def group_copy(k):
        return pltpu.make_async_remote_copy(
            src_ref=fin.at[place],
            dst_ref=fin.at[place],
            send_sem=f_send.at[0],
            recv_sem=f_recv.at[0],
            device_id=group_peer(k),
            device_id_type=MESH,
        )

    for k in range(1, 4):
        group_copy(k).start()
    for p in range(P_DEV):
        full = jnp.concatenate([zacc[p, :, 0:128], zacc[p, :, 128:]], 0)
        full_hi = full.astype(BF16)
        full_lo = (full - full_hi.astype(F32)).astype(BF16)
        both = dot(fy[...], full_hi)
        scores_ref[p] = both[0:NT] + both[NT:] + dot(fy[0:NT], full_lo)
    outs.append(pltpu.make_async_copy(scores_ref, scores_hbm, out_sem.at[1]))
    outs[1].start()

    pltpu.make_async_copy(fin.at[pl.ds(0, 3)], fin.at[pl.ds(0, 3)], f_recv.at[0]).wait()
    outs.append(pltpu.make_async_copy(fin, rows_hbm, out_sem.at[2]))
    outs[2].start()

    wait_rows(SLABS - 1, s_send.at[0])
    for sent_rows in (to_partner, to_up, to_down, to_partner_too):
        sent_rows.wait_send()
    for j in range(2):
        pair_copy(j).wait_send()
    for j in range(2):
        pltpu.make_async_copy(
            xrecv.at[j, pl.ds(0, 3)], xrecv.at[j, pl.ds(0, 3)], x_send.at[j]
        ).wait()
    for j in range(2):
        pltpu.make_async_copy(
            yrecv.at[j, pl.ds(0, YS - 1)], yrecv.at[j, pl.ds(0, YS - 1)], y_send.at[j]
        ).wait()
        pltpu.make_async_copy(
            zrecv.at[j, pl.ds(0, ZS - 1)], zrecv.at[j, pl.ds(0, ZS - 1)], z_send.at[j]
        ).wait()
    pltpu.make_async_copy(fin.at[pl.ds(0, 3)], fin.at[pl.ds(0, 3)], f_send.at[0]).wait()
    for out in outs:
        out.wait()


def finish(
    fin_hbm, line_hbm, found_hbm, scores_hbm, update_hbm,
    fin_ref, line_ref, found_ref, scores_ref, insert, rows, buf, in_sem, out_sem,
):
    loads = [
        pltpu.make_async_copy(src, dst, in_sem.at[i])
        for i, (src, dst) in enumerate(
            ((line_hbm, line_ref), (fin_hbm, fin_ref), (found_hbm, found_ref))
        )
    ]
    for load in loads:
        load.start()
    loads[0].wait()
    insert[...] = (iota((2 * LINES, 128), 0) == line_ref[0:1]).astype(F32).astype(BF16)
    loads[1].wait()
    for o in range(ORIENT):
        for r in range(2):
            got = fin_ref[r * 2 + o // 2, o % 2].astype(F32)
            for part in range(2):
                first = part * 64 + o * OWNED + r * 8
                rows[first : first + 8] = got[part * 8 : part * 8 + 8]
    rows_bf16 = rows[...].astype(BF16)
    outs = []
    for piece in range(4):
        of = pl.ds(piece * 256, 256)
        at = slice(piece * 512, piece * 512 + 512)
        placed = dot(insert[at], rows_bf16).astype(BF16)
        for j in range(2):
            buf.at[j, of].reshape(512, 128)[...] = placed[:, j * 128 : j * 128 + 128]
            outs.append(
                pltpu.make_async_copy(
                    buf.at[j, of],
                    update_hbm.at[of, :, pl.ds(j * 128, 128)],
                    out_sem.at[piece * 2 + j],
                )
            )
            outs[-1].start()
    loads[2].wait()
    for o in range(ORIENT):
        scores_ref[:, o] = found_ref[:, :, o * NT : (o + 1) * NT]
    outs.append(pltpu.make_async_copy(scores_ref, scores_hbm, out_sem.at[8]))
    outs[-1].start()
    for out in outs:
        out.wait()


def body(volume, images, defocus, soft_weights, slice_lines, shift_y, shift_x):
    hbm = pl.BlockSpec(memory_space=pltpu.HBM)
    dma = pltpu.SemaphoreType.DMA
    found, rows, line = pl.pallas_call(
        kernel,
        out_shape=(
            jax.ShapeDtypeStruct((P_DEV, NT, ORIENT * NT), F32),
            jax.ShapeDtypeStruct((4, 2, 16, KS), BF16),
            jax.ShapeDtypeStruct((8, 128), jnp.int32),
        ),
        in_specs=[hbm] * 7,
        out_specs=(hbm, hbm, hbm),
        scratch_shapes=[
            pltpu.VMEM((P_DEV, NT, ORIENT * NT), F32),
            pltpu.VMEM((8, 128), jnp.int32),
            pltpu.VMEM((ORIENT, KS), jnp.int32),
            pltpu.VMEM((P_DEV * ORIENT * NT, NT), F32),
            pltpu.SMEM((P_DEV,), F32),
            pltpu.SMEM((NT,), jnp.int32),
            pltpu.SMEM((NT,), jnp.int32),
            pltpu.VMEM((2, LINES, 2, 128), BF16),
            pltpu.VMEM((2, P_DEV, KS, 2, 128), BF16),
            pltpu.VMEM((2 * KS, 128), F32),
            pltpu.VMEM((OWNED, 2 * KS), BF16),
            pltpu.VMEM((ORIENT, SLABS, OWNED, 2 * KS), BF16),
            pltpu.VMEM((2 * OWNED, 2 * LINES), BF16),
            pltpu.VMEM((ORIENT, KS, KS), BF16),
            pltpu.VMEM((ORIENT, KS, KS), BF16),
            pltpu.VMEM((2, 4 * KS, 256), BF16),
            pltpu.VMEM((2, KS, 2 * NT), BF16),
            pltpu.VMEM((2 * NT, 2 * KS), BF16),
            pltpu.VMEM((P_DEV * ORIENT, 2 * NT, KS), BF16),
            pltpu.VMEM((P_DEV, 2, KS, KS), F32),
            pltpu.VMEM((KS, 2 * KS), BF16),
            pltpu.VMEM((2, KS, 2 * KS), BF16),
            pltpu.VMEM((2, KS, 2 * KS), BF16),
            pltpu.VMEM((2, 4, 64, 2 * KS), BF16),
            pltpu.VMEM((2, 4, 64, 2 * KS), BF16),
            pltpu.VMEM((2, YS, 16, KS), BF16),
            pltpu.VMEM((2, YS, 16, KS), BF16),
            pltpu.VMEM((2, 16, KS), BF16),
            pltpu.VMEM((2, ZS, 16, KS), BF16),
            pltpu.VMEM((4, 2, 16, KS), BF16),
            pltpu.VMEM((YS, 16, KS), F32),
            pltpu.VMEM((P_DEV, KS, 256), F32),
            pltpu.VMEM((2, KS, 2 * KS), BF16),
            pltpu.VMEM((P_DEV, 2, KS, KS), BF16),
            pltpu.VMEM((P_DEV, KS, 4 * KS), BF16),
            dma((5,)),
            dma((4,)),
            dma((3,)),
            dma((5,)),
            dma((5,)),
            dma((2,)),
            dma((2,)),
            dma((2,)),
            dma((2,)),
            dma((2,)),
            dma((2,)),
            dma((2,)),
            dma((2,)),
            dma((1,)),
            dma((1,)),
        ],
        compiler_params=pltpu.CompilerParams(
            collective_id=0, has_side_effects=True, vmem_limit_bytes=60 * 1024 * 1024
        ),
        name="cryo",
    )(
        slice_lines,
        soft_weights.reshape(P_DEV * ORIENT * NT, NT),
        defocus,
        shift_y,
        shift_x,
        volume,
        images,
    )
    return pl.pallas_call(
        finish,
        out_shape=(
            jax.ShapeDtypeStruct((P_DEV, ORIENT, NT, NT), F32),
            jax.ShapeDtypeStruct((LINES, 2, KS), BF16),
        ),
        in_specs=[hbm] * 3,
        out_specs=(hbm, hbm),
        scratch_shapes=[
            pltpu.VMEM((4, 2, 16, KS), BF16),
            pltpu.VMEM((8, 128), jnp.int32),
            pltpu.VMEM((P_DEV, NT, ORIENT * NT), F32),
            pltpu.VMEM((P_DEV, ORIENT, NT, NT), F32),
            pltpu.VMEM((2 * LINES, 2 * ORIENT * OWNED), BF16),
            pltpu.VMEM((2 * ORIENT * OWNED, KS), F32),
            pltpu.VMEM((2, LINES, 2, 128), BF16),
            dma((3,)),
            dma((9,)),
        ],
        compiler_params=pltpu.CompilerParams(vmem_limit_bytes=60 * 1024 * 1024),
        name="finish",
    )(rows, line, found)


def solution(mesh):
    placed = (
        P("slab", None, None),
        P(("dom", "slab"), None, None, None),
        P(("dom", "slab")),
        P(("dom", "slab"), None, None, None),
        P(),
        P(),
        P(),
    )
    return jax.shard_map(
        body,
        mesh=mesh,
        in_specs=placed,
        out_specs=(P(("dom", "slab"), None, None, None), P("slab", None, None)),
        check_vma=False,
    )
```

```python
import math

import jax
import jax.numpy as jnp
from jax import lax
from jax.experimental import pallas as pl
from jax.experimental.pallas import tpu as pltpu
from jax.sharding import PartitionSpec as P

KS = 256
HALF = KS // 2
P_DEV = 4
LINES = 1024
ORIENT = 4
NT = 32
OWNED = 16
PARTICLES = 2048
SLABS = 16
ZS = 8
YS = 8
XLO = 2
SCALE = 1.0 / math.sqrt(NT * NT * PARTICLES)
F32 = jnp.float32
BF16 = jnp.bfloat16
MESH = pl.DeviceIdType.MESH


def dot(a, b):
    return jnp.dot(a, b, preferred_element_type=F32)


def poly_sin_cos(r):
    s = r * r
    sin = r * (1.0 + s * (-1 / 6 + s * (1 / 120 + s * (-1 / 5040 + s * (1 / 362880)))))
    cos = 1.0 + s * (-0.5 + s * (1 / 24 + s * (-1 / 720 + s * (1 / 40320))))
    return sin, cos


def rotate(quadrant, sin, cos):
    q = quadrant & 3
    odd = (q & 1) == 1
    s = jnp.where(odd, cos, sin)
    c = jnp.where(odd, sin, cos)
    s = jnp.where(q >= 2, -s, s)
    c = jnp.where((q == 1) | (q == 2), -c, c)
    return s, c


def turns_sin_cos(turns):
    t = turns & (KS - 1)
    q = (t + KS // 8) >> 6
    r = (t - (q << 6)).astype(F32) * (2.0 * math.pi / KS)
    return rotate(q, *poly_sin_cos(r))


def angle_sin_cos(x):
    n = jnp.floor(x * (2.0 / math.pi) + 0.5)
    r = x - n * 1.5703125
    r = r - n * 4.837512969970703e-4
    r = r - n * 7.549789948768648e-8
    return rotate(n.astype(jnp.int32), *poly_sin_cos(r))


def iota(shape, dim):
    return lax.broadcasted_iota(jnp.int32, shape, dim)


def kernel(
    lines_hbm, weights_hbm, defocus_hbm, sy_hbm, sx_hbm, volume_hbm, images_hbm,
    scores_hbm, rows_hbm, line_hbm,
    scores_ref, line_ref, lines_ref, weights_ref, defocus_ref, sy_ref, sx_ref,
    vbuf, ibuf, split, own, arrived, gather, place_s, place_t,
    fx, ephase, fy, hs, cx, term, sent, landed, xsend, xrecv, ysend, yrecv, zsend, zrecv,
    fin, tile_y, zacc, su, cq, q,
    small_sem, in_sem, out_sem, s_send, s_recv, p_send, p_recv, x_send, x_recv, z_send, z_recv,
    y_send, y_recv, f_send, f_recv,
):
    dom = lax.axis_index("dom")
    slab = lax.axis_index("slab")
    x_lo = dom // 16
    z = (dom // 2) % 8
    c = dom % 2
    zc = z * 2 + c
    partner = (dom + 1 - 2 * c, slab)
    y = slab // 2
    x_hi = slab % 2
    x = x_hi * 2 + x_lo

    small = [
        pltpu.make_async_copy(src, dst, small_sem.at[i])
        for i, (src, dst) in enumerate(
            (
                (lines_hbm, lines_ref),
                (sx_hbm, sx_ref),
                (sy_hbm, sy_ref),
                (defocus_hbm, defocus_ref),
                (weights_hbm, weights_ref),
            )
        )
    ]
    for load in small:
        load.start()
    loads = []
    for j in range(2):
        cols = pl.ds(j * 128, 128)
        loads.append(pltpu.make_async_copy(volume_hbm.at[:, :, cols], vbuf.at[j], in_sem.at[j]))
    for j in range(2):
        cols = pl.ds(j * 128, 128)
        loads.append(
            pltpu.make_async_copy(images_hbm.at[:, :, :, cols], ibuf.at[j], in_sem.at[2 + j])
        )
    for load in loads[2:] + loads[:2]:
        load.start()

    barrier = pltpu.get_barrier_semaphore()

    def slab_peer(k):
        to = lax.rem(slab + k, SLABS)
        flip = (to % 2 + x_hi) % 2
        return ((x_lo + flip) % 2) * 16 + zc, to

    def x_peer(k):
        to = lax.rem(x + k, 4)
        return (to % 2) * 16 + zc, y * 2 + to // 2

    def y_peer(k):
        return dom, lax.rem(y + k, YS) * 2 + x_hi

    def z_peer(k):
        return x_lo * 16 + lax.rem(z + k, ZS) * 2 + c, slab

    def group_peer(k):
        to = lax.rem(x_lo * 2 + c + k, 4)
        return (to // 2) * 16 + z * 2 + to % 2, slab

    def greet(peer):
        pl.semaphore_signal(barrier, inc=1, device_id=peer, device_id_type=MESH)

    def greet_slab(k, carry):
        greet(slab_peer(k))
        return carry

    def greet_z(k, carry):
        greet(z_peer(k))
        return carry

    lax.fori_loop(1, SLABS, greet_slab, 0)
    lax.fori_loop(1, ZS, greet_z, 0)
    for k in range(1, 4):
        greet(group_peer(k))
    greet((dom, y * 2 + 1 - x_hi))

    small[0].wait()
    lines = lines_ref[...]
    owner = lines >> 10
    local = (lines & (LINES - 1)).astype(F32)
    slab_rows = iota((SLABS, KS), 0)
    marks = jnp.concatenate(
        [(owner[o : o + 1] == slab_rows).astype(F32) for o in range(ORIENT)], 0
    )
    before = (iota((KS, KS), 0) < iota((KS, KS), 1)).astype(F32).astype(BF16)
    earlier = dot(marks.astype(BF16), before) * marks
    ranks = [
        jnp.sum(earlier[o * SLABS : (o + 1) * SLABS], axis=0, keepdims=True).astype(jnp.int32)
        for o in range(ORIENT)
    ]
    own_line = []
    for o in range(ORIENT):
        mine = (owner[o : o + 1] == slab) & (ranks[o] == slab_rows)
        own_line.append(
            jnp.sum(jnp.where(mine, local[o : o + 1], 0.0), axis=1, keepdims=True)
        )
    own_line = jnp.concatenate(own_line, 0).astype(jnp.int32)
    small[1].wait()
    small[2].wait()
    lane = iota((8, 128), 1) % NT
    row_x = jnp.zeros((8, 128), jnp.int32)
    row_y = jnp.zeros((8, 128), jnp.int32)
    for t in range(NT):
        row_x = jnp.where(lane == t, sx_ref[t], row_x)
        row_y = jnp.where(lane == t, sy_ref[t], row_y)
    freq = iota((KS, 128), 0) - HALF
    sin_x, cos_x = turns_sin_cos(freq * row_x[0:1])
    sin_y, cos_y = turns_sin_cos(freq * row_y[0:1])
    wide_lane = iota((KS, 128), 1)
    e_re = jnp.where(wide_lane < NT, cos_y, -sin_y)[:, : 2 * NT].astype(BF16)
    e_im = jnp.where(wide_lane < NT, sin_y, cos_y)[:, : 2 * NT].astype(BF16)
    for block in range(2):
        ephase[block, 0:128] = e_re[block * 128 : block * 128 + 128]
        ephase[block, 128:] = e_im[block * 128 : block * 128 + 128]
    t_cos = cos_x.T[0:NT]
    t_sin = sin_x.T[0:NT]
    table = jnp.concatenate([t_cos, t_sin], 1)
    table_hi = table.astype(BF16)
    table_lo = (table - table_hi.astype(F32)).astype(BF16)
    small[4].wait()
    weights = weights_ref[...]
    weights_hi = weights.astype(BF16)
    weights_lo = (weights - weights_hi.astype(F32)).astype(BF16)
    h = dot(weights_hi, table_hi) + dot(weights_lo, table_hi) + dot(weights_hi, table_lo)
    h = h.astype(BF16).reshape(P_DEV * ORIENT, NT, 2 * KS)
    hs[:, 0:NT] = h[:, :, 0:KS]
    hs[:, NT:] = h[:, :, KS:]
    for o in range(ORIENT):
        rank = ranks[o]
        row = owner[o : o + 1]
        at_t = (row & 1) * 128 + (rank >> 3) * 64 + (row >> 1) * 8 + (rank & 7)
        place_t[o] = (iota((KS, KS), 0) == at_t).astype(F32).astype(BF16)

    freq_row = (iota((8, KS), 1) - HALF).astype(F32)
    which = iota((8, KS), 0)
    focus = jnp.zeros((8, KS), F32)
    small[3].wait()
    for p in range(P_DEV):
        focus = jnp.where(which == p, defocus_ref[p], focus)
    sin_d, cos_d = angle_sin_cos(focus * (freq_row * freq_row * (1.0 / (HALF * HALF))))
    sin_col = sin_d.T
    cos_col = cos_d.T
    u_row = 0.1 * sin_d - 0.995 * cos_d
    v_row = -0.995 * sin_d - 0.1 * cos_d
    loads[2].wait()
    loads[3].wait()
    for p in range(P_DEV):
        sin_p = jnp.broadcast_to(sin_col[:, p : p + 1], (KS, 128))
        cos_p = jnp.broadcast_to(cos_col[:, p : p + 1], (KS, 128))
        for j in range(2):
            at = slice(j * 128, j * 128 + 128)
            split[...] = ibuf.at[j, p].reshape(2 * KS, 128)[...].astype(F32)
            ctf = (
                sin_p * u_row[p : p + 1, at]
                + cos_p * v_row[p : p + 1, at]
            )
            for part in range(2):
                product = ctf * split[pl.ds(part, KS, stride=2), :]
                cx[p, part, :, at] = product
                cq[p, part, :, at] = product.astype(BF16)

    def placed_term(o):
        for block in range(2):
            at = slice(block * 128, block * 128 + 128)
            t_re = None
            for p in range(P_DEV):
                table_h = hs[p * ORIENT + o]
                g = dot(ephase[block], table_h)
                g_re = g[0:128]
                g_im = g[128:]
                c_re = cx[p, 0, at]
                c_im = cx[p, 1, at]
                if t_re is None:
                    t_re = c_re * g_re - c_im * g_im
                    t_im = c_re * g_im + c_im * g_re
                else:
                    t_re += c_re * g_re - c_im * g_im
                    t_im += c_re * g_im + c_im * g_re
            term[at, 0:KS] = t_re.astype(BF16)
            term[at, KS:] = t_im.astype(BF16)
        return dot(place_t[o], term[...])

    def pair_copy(j):
        return pltpu.make_async_remote_copy(
            src_ref=sent.at[j],
            dst_ref=landed.at[j],
            send_sem=p_send.at[j],
            recv_sem=p_recv.at[j],
            device_id=partner,
            device_id_type=MESH,
        )

    def x_copy(j, k):
        return pltpu.make_async_remote_copy(
            src_ref=xsend.at[j, lax.rem(x + k, 4)],
            dst_ref=xrecv.at[j, x],
            send_sem=x_send.at[j],
            recv_sem=x_recv.at[j],
            device_id=x_peer(k),
            device_id_type=MESH,
        )

    def y_copy(j, k):
        return pltpu.make_async_remote_copy(
            src_ref=ysend.at[j, lax.rem(y + k, YS)],
            dst_ref=yrecv.at[j, y],
            send_sem=y_send.at[j],
            recv_sem=y_recv.at[j],
            device_id=y_peer(k),
            device_id_type=MESH,
        )

    def z_copy(j, k):
        return pltpu.make_async_remote_copy(
            src_ref=zsend.at[j],
            dst_ref=zrecv.at[j, z],
            send_sem=z_send.at[j],
            recv_sem=z_recv.at[j],
            device_id=z_peer(k),
            device_id_type=MESH,
        )

    def give(j, carry):
        sent[j] = placed_term(2 * (1 - c) + j).astype(BF16)
        return carry

    lax.fori_loop(0, 2, give, 0)

    pl.semaphore_wait(barrier, SLABS - 1 + ZS - 1 + 3 + 1)

    pair_copy(0).start()
    pair_copy(1).start()

    def keep(j, carry):
        mine = placed_term(2 * c + j)
        pair_copy(j).wait_recv()
        both = (mine + landed[j].astype(F32)).astype(BF16)
        xsend[j] = both.reshape(4, 64, 2 * KS)

        def send_x(k, inner):
            x_copy(j, k).start()
            return inner

        lax.fori_loop(1, 4, send_x, 0)
        xrecv[j, x] = xsend[j, x]
        return carry

    lax.fori_loop(0, 2, keep, 0)

    o_own = 2 * c + z % 2
    first_line = own_line[0:OWNED]
    for o in range(1, ORIENT):
        first_line = jnp.where(o_own == o, own_line[o * OWNED : (o + 1) * OWNED], first_line)
    column = iota((OWNED, 2 * LINES), 1)
    gather[0:OWNED] = (column == 2 * first_line).astype(F32).astype(BF16)
    gather[OWNED:] = (column == 2 * first_line + 1).astype(F32).astype(BF16)

    for j in range(2):
        loads[j].wait()
        picked = dot(gather[...], vbuf.at[j].reshape(2 * LINES, 128)[...]).astype(BF16)
        for part in range(2):
            at = slice(part * KS + j * 128, part * KS + j * 128 + 128)
            own[:, at] = picked[part * OWNED : part * OWNED + OWNED]

    def slab_copy(k):
        return pltpu.make_async_remote_copy(
            src_ref=own,
            dst_ref=arrived.at[o_own, slab],
            send_sem=s_send.at[0],
            recv_sem=s_recv.at[0],
            device_id=slab_peer(k),
            device_id_type=MESH,
        )

    def send_slab(k, carry):
        slab_copy(k).start()
        return carry

    lax.fori_loop(1, SLABS, send_slab, 0)
    arrived[o_own, slab] = own[...]

    def wait_rows(n, sem):
        part = arrived.at[0, pl.ds(0, n)]
        pltpu.make_async_copy(part, part, sem).wait()

    def pass_rows(o, sem, first=0, n=SLABS, to=partner):
        part = arrived.at[o, pl.ds(first, n)]
        return pltpu.make_async_remote_copy(
            src_ref=part,
            dst_ref=part,
            send_sem=s_send.at[sem],
            recv_sem=s_recv.at[sem],
            device_id=to,
            device_id_type=MESH,
        )

    at_s = [owner[o : o + 1] * OWNED + ranks[o] for o in range(ORIENT)]
    at_s = jnp.concatenate(at_s + at_s, 0).astype(F32).T.astype(jnp.int32)
    for o in range(ORIENT):
        place_s[o] = (iota((KS, KS), 1) == at_s[:, o : o + 1]).astype(F32).astype(BF16)
    group = wide_lane // NT
    for o in range(ORIENT):
        cos_o = jnp.where(group == o, cos_x, 0.0).astype(BF16)
        sin_o = jnp.where(group == o, sin_x, 0.0).astype(BF16)
        at = (o // 2) * 2 * KS
        fx[o % 2, at : at + KS, 0:128] = cos_o
        fx[o % 2, at : at + KS, 128:] = -sin_o
        fx[o % 2, at + KS : at + 2 * KS, 0:128] = sin_o
        fx[o % 2, at + KS : at + 2 * KS, 128:] = cos_o
    table_y = jnp.concatenate([cos_y.T[0:NT], sin_y.T[0:NT]], 1) * (1.0 / KS)
    fy_hi = table_y.astype(BF16)
    fy[0:NT] = fy_hi
    fy[NT:] = (table_y - fy_hi.astype(F32)).astype(BF16)

    def correlate(parity, first):
        for j in range(2):
            o = 2 * j + parity
            su[j] = dot(place_s[o], arrived[o].reshape(KS, 2 * KS)).astype(BF16)
        for p in range(P_DEV):
            for block in range(2):
                at = slice(block * 128, block * 128 + 128)
                c_re = cq[p, 0, at]
                c_im = cq[p, 1, at]
                for j in range(2):
                    s_re = su[j, at, 0:KS]
                    s_im = su[j, at, KS:]
                    q[p, at, 2 * j * KS : (2 * j + 1) * KS] = s_re * c_re + s_im * c_im
                    q[p, at, (2 * j + 1) * KS : (2 * j + 2) * KS] = s_re * c_im - s_im * c_re
            part = dot(q[p], fx[parity])
            if first:
                zacc[p] = part
            else:
                zacc[p] += part

    line_row = jnp.concatenate([2 * own_line, 2 * own_line + 1], 0).astype(F32)
    line_row = jnp.broadcast_to(line_row, (128, 128)).T[0:8].astype(jnp.int32)
    line_ref[...] = line_row
    outs = [pltpu.make_async_copy(line_ref, line_hbm, out_sem.at[0])]
    outs[0].start()
    wait_rows(SLABS - 1, s_recv.at[0])
    to_up = pass_rows(o_own, 2, 0, 8, z_peer(1))
    to_down = pass_rows(o_own, 3, 8, 8, z_peer(ZS - 1))
    to_partner = pass_rows(o_own, 1)
    to_up.start()
    to_down.start()
    to_partner.start()

    def pass_on(j, carry):
        pltpu.make_async_copy(
            xrecv.at[j, pl.ds(0, 3)], xrecv.at[j, pl.ds(0, 3)], x_recv.at[j]
        ).wait()
        for part in range(2):
            at = slice(part * KS, part * KS + KS)
            total = xrecv[j, 0, :, at].astype(F32)
            for other in range(1, 4):
                total += xrecv[j, other, :, at].astype(F32)
            tile_y[:, part * 8 : part * 8 + 8] = total.reshape(YS, 8, KS)
        ysend[j] = tile_y[...].astype(BF16)

        def send_y(k, inner):
            y_copy(j, k).start()
            return inner

        lax.fori_loop(1, YS, send_y, 0)
        yrecv[j, y] = ysend[j, y]
        return carry

    lax.fori_loop(0, 2, pass_on, 0)
    wait_rows(SLABS, s_recv.at[1])
    correlate(z % 2, True)
    wait_rows(8, s_recv.at[2])
    wait_rows(8, s_recv.at[3])
    to_partner_too = pass_rows(2 * c + 1 - z % 2, 4)
    to_partner_too.start()

    def spread(j, carry):
        pltpu.make_async_copy(
            yrecv.at[j, pl.ds(0, YS - 1)], yrecv.at[j, pl.ds(0, YS - 1)], y_recv.at[j]
        ).wait()
        total = yrecv[j, 0].astype(F32)
        for other in range(1, YS):
            total += yrecv[j, other].astype(F32)
        zsend[j] = total.astype(BF16)

        def send_z(k, inner):
            z_copy(j, k).start()
            return inner

        lax.fori_loop(1, ZS, send_z, 0)
        zrecv[j, z] = zsend[j]
        return carry

    lax.fori_loop(0, 2, spread, 0)
    wait_rows(SLABS, s_recv.at[4])
    correlate(1 - z % 2, False)

    place = x_lo * 2 + c
    for j in range(2):
        pltpu.make_async_copy(
            zrecv.at[j, pl.ds(0, ZS - 1)], zrecv.at[j, pl.ds(0, ZS - 1)], z_recv.at[j]
        ).wait()
        total = zrecv[j, 0].astype(F32)
        for other in range(1, ZS):
            total += zrecv[j, other].astype(F32)
        fin[place, j] = (total * SCALE).astype(BF16)

    def group_copy(k):
        return pltpu.make_async_remote_copy(
            src_ref=fin.at[place],
            dst_ref=fin.at[place],
            send_sem=f_send.at[0],
            recv_sem=f_recv.at[0],
            device_id=group_peer(k),
            device_id_type=MESH,
        )

    for k in range(1, 4):
        group_copy(k).start()
    for p in range(P_DEV):
        full = jnp.concatenate([zacc[p, :, 0:128], zacc[p, :, 128:]], 0)
        full_hi = full.astype(BF16)
        full_lo = (full - full_hi.astype(F32)).astype(BF16)
        both = dot(fy[...], full_hi)
        scores_ref[p] = both[0:NT] + both[NT:] + dot(fy[0:NT], full_lo)
    outs.append(pltpu.make_async_copy(scores_ref, scores_hbm, out_sem.at[1]))
    outs[1].start()

    pltpu.make_async_copy(fin.at[pl.ds(0, 3)], fin.at[pl.ds(0, 3)], f_recv.at[0]).wait()
    outs.append(pltpu.make_async_copy(fin, rows_hbm, out_sem.at[2]))
    outs[2].start()

    wait_rows(SLABS - 1, s_send.at[0])
    for sent_rows in (to_partner, to_up, to_down, to_partner_too):
        sent_rows.wait_send()
    for j in range(2):
        pair_copy(j).wait_send()
    for j in range(2):
        pltpu.make_async_copy(
            xrecv.at[j, pl.ds(0, 3)], xrecv.at[j, pl.ds(0, 3)], x_send.at[j]
        ).wait()
    for j in range(2):
        pltpu.make_async_copy(
            yrecv.at[j, pl.ds(0, YS - 1)], yrecv.at[j, pl.ds(0, YS - 1)], y_send.at[j]
        ).wait()
        pltpu.make_async_copy(
            zrecv.at[j, pl.ds(0, ZS - 1)], zrecv.at[j, pl.ds(0, ZS - 1)], z_send.at[j]
        ).wait()
    pltpu.make_async_copy(fin.at[pl.ds(0, 3)], fin.at[pl.ds(0, 3)], f_send.at[0]).wait()
    for out in outs:
        out.wait()


def finish(
    fin_hbm, line_hbm, found_hbm, scores_hbm, update_hbm,
    fin_ref, line_ref, found_ref, scores_ref, insert, rows, buf, in_sem, out_sem,
):
    loads = [
        pltpu.make_async_copy(src, dst, in_sem.at[i])
        for i, (src, dst) in enumerate(
            ((line_hbm, line_ref), (fin_hbm, fin_ref), (found_hbm, found_ref))
        )
    ]
    for load in loads:
        load.start()
    loads[0].wait()
    insert[...] = (iota((2 * LINES, 128), 0) == line_ref[0:1]).astype(F32).astype(BF16)
    loads[1].wait()
    for o in range(ORIENT):
        for r in range(2):
            got = fin_ref[r * 2 + o // 2, o % 2].astype(F32)
            for part in range(2):
                first = part * 64 + o * OWNED + r * 8
                rows[first : first + 8] = got[part * 8 : part * 8 + 8]
    rows_bf16 = rows[...].astype(BF16)
    outs = []
    for piece in range(4):
        of = pl.ds(piece * 256, 256)
        at = slice(piece * 512, piece * 512 + 512)
        placed = dot(insert[at], rows_bf16).astype(BF16)
        for j in range(2):
            buf.at[j, of].reshape(512, 128)[...] = placed[:, j * 128 : j * 128 + 128]
            outs.append(
                pltpu.make_async_copy(
                    buf.at[j, of],
                    update_hbm.at[of, :, pl.ds(j * 128, 128)],
                    out_sem.at[piece * 2 + j],
                )
            )
            outs[-1].start()
    loads[2].wait()
    for o in range(ORIENT):
        scores_ref[:, o] = found_ref[:, :, o * NT : (o + 1) * NT]
    outs.append(pltpu.make_async_copy(scores_ref, scores_hbm, out_sem.at[8]))
    outs[-1].start()
    for out in outs:
        out.wait()


def body(volume, images, defocus, soft_weights, slice_lines, shift_y, shift_x):
    hbm = pl.BlockSpec(memory_space=pltpu.HBM)
    dma = pltpu.SemaphoreType.DMA
    found, rows, line = pl.pallas_call(
        kernel,
        out_shape=(
            jax.ShapeDtypeStruct((P_DEV, NT, ORIENT * NT), F32),
            jax.ShapeDtypeStruct((4, 2, 16, KS), BF16),
            jax.ShapeDtypeStruct((8, 128), jnp.int32),
        ),
        in_specs=[hbm] * 7,
        out_specs=(hbm, hbm, hbm),
        scratch_shapes=[
            pltpu.VMEM((P_DEV, NT, ORIENT * NT), F32),
            pltpu.VMEM((8, 128), jnp.int32),
            pltpu.VMEM((ORIENT, KS), jnp.int32),
            pltpu.VMEM((P_DEV * ORIENT * NT, NT), F32),
            pltpu.SMEM((P_DEV,), F32),
            pltpu.SMEM((NT,), jnp.int32),
            pltpu.SMEM((NT,), jnp.int32),
            pltpu.VMEM((2, LINES, 2, 128), BF16),
            pltpu.VMEM((2, P_DEV, KS, 2, 128), BF16),
            pltpu.VMEM((2 * KS, 128), F32),
            pltpu.VMEM((OWNED, 2 * KS), BF16),
            pltpu.VMEM((ORIENT, SLABS, OWNED, 2 * KS), BF16),
            pltpu.VMEM((2 * OWNED, 2 * LINES), BF16),
            pltpu.VMEM((ORIENT, KS, KS), BF16),
            pltpu.VMEM((ORIENT, KS, KS), BF16),
            pltpu.VMEM((2, 4 * KS, 256), BF16),
            pltpu.VMEM((2, KS, 2 * NT), BF16),
            pltpu.VMEM((2 * NT, 2 * KS), BF16),
            pltpu.VMEM((P_DEV * ORIENT, 2 * NT, KS), BF16),
            pltpu.VMEM((P_DEV, 2, KS, KS), F32),
            pltpu.VMEM((KS, 2 * KS), BF16),
            pltpu.VMEM((2, KS, 2 * KS), BF16),
            pltpu.VMEM((2, KS, 2 * KS), BF16),
            pltpu.VMEM((2, 4, 64, 2 * KS), BF16),
            pltpu.VMEM((2, 4, 64, 2 * KS), BF16),
            pltpu.VMEM((2, YS, 16, KS), BF16),
            pltpu.VMEM((2, YS, 16, KS), BF16),
            pltpu.VMEM((2, 16, KS), BF16),
            pltpu.VMEM((2, ZS, 16, KS), BF16),
            pltpu.VMEM((4, 2, 16, KS), BF16),
            pltpu.VMEM((YS, 16, KS), F32),
            pltpu.VMEM((P_DEV, KS, 256), F32),
            pltpu.VMEM((2, KS, 2 * KS), BF16),
            pltpu.VMEM((P_DEV, 2, KS, KS), BF16),
            pltpu.VMEM((P_DEV, KS, 4 * KS), BF16),
            dma((5,)),
            dma((4,)),
            dma((3,)),
            dma((5,)),
            dma((5,)),
            dma((2,)),
            dma((2,)),
            dma((2,)),
            dma((2,)),
            dma((2,)),
            dma((2,)),
            dma((2,)),
            dma((2,)),
            dma((1,)),
            dma((1,)),
        ],
        compiler_params=pltpu.CompilerParams(
            collective_id=0, has_side_effects=True, vmem_limit_bytes=60 * 1024 * 1024
        ),
        name="cryo",
    )(
        slice_lines,
        soft_weights.reshape(P_DEV * ORIENT * NT, NT),
        defocus,
        shift_y,
        shift_x,
        volume,
        images,
    )
    return pl.pallas_call(
        finish,
        out_shape=(
            jax.ShapeDtypeStruct((P_DEV, ORIENT, NT, NT), F32),
            jax.ShapeDtypeStruct((LINES, 2, KS), BF16),
        ),
        in_specs=[hbm] * 3,
        out_specs=(hbm, hbm),
        scratch_shapes=[
            pltpu.VMEM((4, 2, 16, KS), BF16),
            pltpu.VMEM((8, 128), jnp.int32),
            pltpu.VMEM((P_DEV, NT, ORIENT * NT), F32),
            pltpu.VMEM((P_DEV, ORIENT, NT, NT), F32),
            pltpu.VMEM((2 * LINES, 2 * ORIENT * OWNED), BF16),
            pltpu.VMEM((2 * ORIENT * OWNED, KS), F32),
            pltpu.VMEM((2, LINES, 2, 128), BF16),
            dma((3,)),
            dma((9,)),
        ],
        compiler_params=pltpu.CompilerParams(vmem_limit_bytes=60 * 1024 * 1024),
        name="finish",
    )(rows, line, found)


def solution(mesh):
    placed = (
        P("slab", None, None),
        P(("dom", "slab"), None, None, None),
        P(("dom", "slab")),
        P(("dom", "slab"), None, None, None),
        P(),
        P(),
        P(),
    )
    return jax.shard_map(
        body,
        mesh=mesh,
        in_specs=placed,
        out_specs=(P(("dom", "slab"), None, None, None), P("slab", None, None)),
        check_vma=False,
    )
```
